32 devices in a mesh: blk: 16 (over z, y, core), pb: 2 (over x).
Axes of the slice: x: 2, y: 2, z: 4, core: 2. Of those that a mesh axis runs over, the one named last changes fastest.
Arguments:
- tokens: bfloat16 [8192, 768], P(('blk', 'pb')), may hold values from -6 to 6
- memory: bfloat16 [2048, 768], P(('blk', 'pb')), may hold values from -6 to 6
- self_query: bfloat16 [768, 768], P(('blk', 'pb')), may hold values from -0.3125 to 0.3125
- self_key: bfloat16 [768, 768], P(('blk', 'pb')), may hold values from -0.3125 to 0.3125
- self_value: bfloat16 [768, 768], P(('blk', 'pb')), may hold values from -0.21875 to 0.21875
- self_output: bfloat16 [768, 768], P(('blk', 'pb')), may hold values from -0.625 to 0.625
- cross_query: bfloat16 [768, 768], P(('blk', 'pb')), may hold values from -0.3125 to 0.3125
- cross_key: bfloat16 [768, 768], P(('blk', 'pb')), may hold values from -0.3125 to 0.3125
- cross_value: bfloat16 [768, 768], P(('blk', 'pb')), may hold values from -0.21875 to 0.21875
- cross_output: bfloat16 [768, 768], P(('blk', 'pb')), may hold values from -0.875 to 0.875
- feed_in: bfloat16 [768, 3072], P(('blk', 'pb')), may hold values from -0.21875 to 0.21875
- feed_out: bfloat16 [3072, 768], P(('blk', 'pb')), may hold values from -0.109375 to 0.109375
- gain_self: bfloat16 [768], P(('blk', 'pb')), may hold values from 0.099609375 to 1.8984375
- gain_cross: bfloat16 [768], P(('blk', 'pb')), may hold values from 0.099609375 to 1.8984375
- gain_feed: bfloat16 [768], P(('blk', 'pb')), may hold values from 0.099609375 to 1.8984375
- doc_lengths: int32 [5], replicated, may hold values from 1 to 1024, as said below
- seg_doc: int32 [16], replicated, may hold values from 0 to 4, as said below
- cotangent: bfloat16 [8192, 768], P(('blk', 'pb')), may hold values from -6 to 6
Outputs:
- layer_output: bfloat16 [8192, 768], P(('blk', 'pb'))
- gradient_tokens: float32 [8192, 768], P(('blk', 'pb'))
- gradient_memory: float32 [2048, 768], P(('blk', 'pb'))
- gradient_self_query: float32 [768, 768], P(('blk', 'pb'))
- gradient_self_key: float32 [768, 768], P(('blk', 'pb'))
- gradient_self_value: float32 [768, 768], P(('blk', 'pb'))
- gradient_self_output: float32 [768, 768], P(('blk', 'pb'))
- gradient_cross_query: float32 [768, 768], P(('blk', 'pb'))
- gradient_cross_key: float32 [768, 768], P(('blk', 'pb'))
- gradient_cross_value: float32 [768, 768], P(('blk', 'pb'))
- gradient_cross_output: float32 [768, 768], P(('blk', 'pb'))
- gradient_feed_in: float32 [768, 3072], P(('blk', 'pb'))
- gradient_feed_out: float32 [3072, 768], P(('blk', 'pb'))
- gradient_gain_self: float32 [768], P(('blk', 'pb'))
- gradient_gain_cross: float32 [768], P(('blk', 'pb'))
- gradient_gain_feed: float32 [768], P(('blk', 'pb'))
The draws below stay inside these ranges and needn't reach their ends.
Inputs may be any that keep to these rules, and one draw needn't show every extreme that they name: `doc_lengths`: the 5 lengths sum to 2048; exactly one of them equals 1024. `seg_doc`: every document is read by at least one segment.
All inputs are finite; a program needn't handle non-finite values.
Results may differ from the reference program's by a relative error of at most 0.03.
The reference program's roundings to bfloat16 on the way count: a program that leaves them out, or rounds other values in their place, can miss the bound.
Values may be sent and summed in bfloat16 or wider, within the bound.
No kernel may reach another device: no remote copies, remote signals or barrier semaphores. Data moves between devices by JAX's collectives and lax.ppermute only.
A program may use at most 192 MiB of HBM per device.

```python
from functools import partial
import jax
import jax.numpy as jnp
from jax import lax

D = 768
HEADS = 12
HEAD = 64
FF = 3072
NDOC = 5
SEG = 512
NSEG = 16
TOKENS = 8192
MEM = 2048


def draw_doc_lengths(key, part):
    key = jax.random.fold_in(key, 11)
    pick_key, weight_key = jax.random.split(key)
    long_place = jax.random.randint(pick_key, (), 0, NDOC)
    places = jnp.arange(NDOC, dtype=jnp.int32)
    weights = jax.random.randint(weight_key, (NDOC,), 2, 5)
    weights = jnp.where(places == long_place, 0, weights)
    half_size = MEM // 2
    remaining = MEM - half_size
    shares = remaining * weights // jnp.sum(weights)
    leftover = remaining - jnp.sum(shares)
    first_other = jnp.where(long_place == 0, 1, 0)
    shares = shares + jnp.where(places == first_other, leftover, 0)
    return jnp.where(places == long_place, half_size, shares).astype(jnp.int32)


def draw_seg_doc(key, part):
    key = jax.random.fold_in(key, 23)
    first_key, second_key = jax.random.split(key)
    chosen = jax.random.randint(first_key, (NSEG,), 0, NDOC)
    order = jax.random.permutation(second_key, NSEG)
    forced = jnp.zeros((NSEG,), jnp.int32).at[order[:NDOC]].set(jnp.arange(NDOC, dtype=jnp.int32))
    marked = jnp.zeros((NSEG,), jnp.int32).at[order[:NDOC]].set(1)
    return jnp.where(marked == 1, forced, chosen).astype(jnp.int32)


def block_scale(own_key, shape, cuts, least, top_value):
    loudness, own = 1.0, jax.random.fold_in(own_key, 6)
    for axis_at, blocks in cuts:
        draws = jnp.exp(jax.random.uniform(jax.random.fold_in(own, axis_at), (blocks,), jnp.float32, least / len(cuts), top_value / len(cuts)))
        loudness = loudness * jnp.repeat(draws, shape[axis_at] // blocks).reshape([-1 if axis == axis_at else 1 for axis in range(len(shape))])
    return loudness


def normal_values(key, shape, scale, most, cuts=(), kind=jnp.bfloat16):
    values = scale * jax.random.normal(key, shape, jnp.float32)
    if cuts:
        values = values * block_scale(key, shape, cuts, -0.22, 0.18)
    return jnp.clip(values, -most, most).astype(kind)


def setup_inputs(seed: int = 0) -> dict:
    seeds = jax.random.split(jax.random.key(seed), 19)
    return {
        "tokens": normal_values(seeds[0], (TOKENS, D), 1.0, 6.0, ((0, 32),)),
        "memory": normal_values(seeds[1], (MEM, D), 1.0, 6.0, ((0, 32),)),
        "self_query": normal_values(seeds[2], (D, D), (D // 2) ** -0.5, 0.3125, ((0, 32),)),
        "self_key": normal_values(seeds[3], (D, D), (D // 2) ** -0.5, 0.3125, ((0, 32),)),
        "self_value": normal_values(seeds[4], (D, D), D ** -0.5, 0.21875, ((0, 32),)),
        "self_output": normal_values(seeds[5], (D, D), (D // 8) ** -0.5, 0.625, ((0, 32),)),
        "cross_query": normal_values(seeds[6], (D, D), (D // 2) ** -0.5, 0.3125, ((0, 32),)),
        "cross_key": normal_values(seeds[7], (D, D), (D // 2) ** -0.5, 0.3125, ((0, 32),)),
        "cross_value": normal_values(seeds[8], (D, D), D ** -0.5, 0.21875, ((0, 32),)),
        "cross_output": normal_values(seeds[9], (D, D), (D // 16) ** -0.5, 0.875, ((0, 32),)),
        "feed_in": normal_values(seeds[10], (D, FF), D ** -0.5, 0.21875, ((0, 32),)),
        "feed_out": normal_values(seeds[11], (FF, D), FF ** -0.5, 0.109375, ((0, 32),)),
        "gain_self": jnp.clip(1.0 + 0.18 * jax.random.normal(seeds[12], (D,), jnp.float32), 0.099609375, 1.8984375).astype(jnp.bfloat16),
        "gain_cross": jnp.clip(1.0 + 0.18 * jax.random.normal(seeds[13], (D,), jnp.float32), 0.099609375, 1.8984375).astype(jnp.bfloat16),
        "gain_feed": jnp.clip(1.0 + 0.18 * jax.random.normal(seeds[14], (D,), jnp.float32), 0.099609375, 1.8984375).astype(jnp.bfloat16),
        "doc_lengths": draw_doc_lengths(jax.random.fold_in(seeds[18], 71), 0),
        "seg_doc": draw_seg_doc(jax.random.fold_in(seeds[18], 71), 0),
        "cotangent": normal_values(seeds[17], (TOKENS, D), 1.0, 6.0, ((0, 32),)),
    }


@jax.custom_vjp
def low(v):
    return lax.optimization_barrier(v.astype(jnp.bfloat16)).astype(jnp.float32)

@jax.custom_vjp
def low_back(v):
    return v

def low_keep(v):
    return (low(v), None)

def low_pass(kept, grad):
    return (grad,)

def back_keep(v):
    return (v, None)

def back_low(kept, grad):
    return (low(grad),)
low.defvjp(low_keep, low_pass)
low_back.defvjp(back_keep, back_low)
highest = lax.Precision.HIGHEST
big_negative = -1e+30
epsilon = 1e-05

def dense(left, right):
    return jnp.dot(left, right, precision=highest, preferred_element_type=jnp.float32)

def project(values, weight):
    return low_back(low(dense(values, weight)))

def layer_norm(values, gain):
    centered = values - lax.optimization_barrier(jnp.mean(values, axis=-1, keepdims=True))
    variance = lax.optimization_barrier(jnp.mean(centered * centered, axis=-1, keepdims=True))
    return centered * lax.rsqrt(variance + epsilon) * gain

def by_segment(values):
    return values.reshape(NSEG, SEG, HEADS, HEAD)

def attend(queries, keys, values, allowed):
    scores = low_back(jnp.einsum('qhd,khd->hqk', queries, keys, precision=highest) * HEAD ** (-0.5))
    scores = jnp.where(allowed[None], scores, big_negative)
    probs = jax.nn.softmax(scores, axis=-1)
    return jnp.einsum('hqk,khd->qhd', low(probs), values, precision=highest)

def causal_segment(blocks):
    queries, keys, values = blocks
    rows = lax.broadcasted_iota(jnp.int32, (SEG, SEG), 0)
    columns = lax.broadcasted_iota(jnp.int32, (SEG, SEG), 1)
    return attend(queries, keys, values, columns <= rows)

def cross_segment(keys, values, key_doc, blocks):
    queries, document = blocks
    allowed = jnp.broadcast_to((key_doc == document)[None, :], (SEG, MEM))
    return attend(queries, keys, values, allowed)

def forward(key_doc, seg_doc, tokens, memory, self_query, self_key, self_value, self_output, cross_query, cross_key, cross_value, cross_output, feed_in, feed_out, gain_self, gain_cross, gain_feed):
    queries = by_segment(project(tokens, self_query))
    keys = by_segment(project(tokens, self_key))
    values = by_segment(project(tokens, self_value))
    attended = lax.map(jax.checkpoint(causal_segment), (queries, keys, values))
    self_out = low_back(low(attended.reshape(TOKENS, D)))
    hidden_self = layer_norm(tokens + low_back(dense(self_out, self_output)), gain_self)
    cross_queries = by_segment(project(low(hidden_self), cross_query))
    memory_keys = project(memory, cross_key).reshape(MEM, HEADS, HEAD)
    memory_values = project(memory, cross_value).reshape(MEM, HEADS, HEAD)
    crossed = lax.map(jax.checkpoint(partial(cross_segment, memory_keys, memory_values, key_doc)), (cross_queries, seg_doc))
    cross_out = low_back(low(crossed.reshape(TOKENS, D)))
    hidden_cross = layer_norm(hidden_self + low_back(dense(cross_out, cross_output)), gain_cross)
    inner = low_back(dense(low(hidden_cross), feed_in))
    activated = low(jax.nn.gelu(inner, approximate=False))
    return layer_norm(hidden_cross + low_back(dense(activated, feed_out)), gain_feed)

def reference(tokens, memory, self_query, self_key, self_value, self_output, cross_query, cross_key, cross_value, cross_output, feed_in, feed_out, gain_self, gain_cross, gain_feed, doc_lengths, seg_doc, cotangent):
    ends = jnp.cumsum(doc_lengths).astype(jnp.int32)
    rows = jnp.arange(MEM, dtype=jnp.int32)
    key_doc = lax.optimization_barrier(jnp.sum((rows[:, None] >= ends[None, :]).astype(jnp.int32), axis=1)).astype(jnp.int32)
    floats = (tokens.astype(jnp.float32), memory.astype(jnp.float32), self_query.astype(jnp.float32), self_key.astype(jnp.float32), self_value.astype(jnp.float32), self_output.astype(jnp.float32), cross_query.astype(jnp.float32), cross_key.astype(jnp.float32), cross_value.astype(jnp.float32), cross_output.astype(jnp.float32), feed_in.astype(jnp.float32), feed_out.astype(jnp.float32), gain_self.astype(jnp.float32), gain_cross.astype(jnp.float32), gain_feed.astype(jnp.float32))
    result, pullback = jax.vjp(partial(forward, key_doc, seg_doc), *floats)
    gradients = pullback(cotangent.astype(jnp.float32))
    return (result.astype(jnp.bfloat16), gradients[0], gradients[1], gradients[2], gradients[3], gradients[4], gradients[5], gradients[6], gradients[7], gradients[8], gradients[9], gradients[10], gradients[11], gradients[12], gradients[13], gradients[14])
```

```python
import math

import jax
import jax.numpy as jnp
from jax import lax
from jax.experimental import pallas as pl
from jax.experimental.pallas import tpu as pltpu
from jax.sharding import Mesh
from jax.sharding import PartitionSpec as P

D = 768
HEADS = 12
HEAD = 64
PAIR = 2 * HEAD
PAIRS = HEADS // 2
SCALE = HEAD ** (-0.5)

big_negative = -1e30
epsilon = 1e-05
bf16 = jnp.bfloat16
f32 = jnp.float32
ALL = ("z", "y", "c", "x")
VMEM = pl.BlockSpec(memory_space=pltpu.VMEM)
ROOM = 56 * 2**20
SMEM = pl.BlockSpec(memory_space=pltpu.SMEM)


def matmul(left, right):
    return jnp.dot(left, right, preferred_element_type=f32)


def contract_rows(left, right):
    return lax.dot_general(left, right, (((0,), (0,)), ((), ())), preferred_element_type=f32)


def times_transpose(left, right):
    return lax.dot_general(left, right, (((1,), (1,)), ((), ())), preferred_element_type=f32)


def layer_norm(values, gain):
    centered = values - jnp.mean(values, axis=-1, keepdims=True)
    variance = jnp.mean(centered * centered, axis=-1, keepdims=True)
    return centered * lax.rsqrt(variance + epsilon) * gain


def exact_gelu(values):
    return jax.nn.gelu(values, approximate=False)


def table_entry(table, index):
    places = jnp.arange(table.shape[0], dtype=jnp.int32)
    return jnp.sum(jnp.where(places == index, table, 0))


def swapped(value, axis, by=1):
    size = lax.axis_size(axis)
    return lax.ppermute(value, axis, [(i, i ^ by) for i in range(size)])


def position():
    return jnp.stack([lax.axis_index(a).astype(jnp.int32) for a in ALL])


def in_order(pieces, where):
    count = len(pieces)

    def kernel(at, *refs):
        for r in range(count):
            refs[count][jnp.bitwise_xor(at[0], r)] = refs[r][...]

    return pl.pallas_call(
        kernel,
        out_shape=jax.ShapeDtypeStruct((count,) + pieces[0].shape, pieces[0].dtype),
        in_specs=[SMEM] + [VMEM] * count,
        out_specs=VMEM,
        compiler_params=pltpu.CompilerParams(vmem_limit_bytes=ROOM),
        name="in_order",
    )(where, *pieces)


def assembled(planes, cuts, where):
    keys = sorted(planes)
    count, groups, *tail = planes[keys[0]].shape
    tail = tuple(tail)
    n_in = len(keys)

    def kernel(at, *refs):
        for i, (dy, dc, dx) in enumerate(keys):
            y, c, x = (jnp.bitwise_xor(at[1 + j], d) for j, d in enumerate((dy, dc, dx)))
            for o, (first, size) in enumerate(cuts):
                refs[n_in + o][0, y, c, x] = refs[i][0, first : first + size]

    return pl.pallas_call(
        kernel,
        grid=(count,),
        out_shape=[
            jax.ShapeDtypeStruct((count, 2, 2, 2, size) + tail, planes[keys[0]].dtype)
            for _, size in cuts
        ],
        in_specs=[SMEM]
        + [pl.BlockSpec((1, groups) + tail, lambda z: (z, 0, 0, 0)) for _ in range(n_in)],
        out_specs=[
            pl.BlockSpec((1, 2, 2, 2, size) + tail, lambda z: (z, 0, 0, 0, 0, 0, 0))
            for _, size in cuts
        ],
        compiler_params=pltpu.CompilerParams(vmem_limit_bytes=ROOM),
        name="assembled",
    )(where, *(planes[k] for k in keys))


def taken_apart(wholes, where):
    n_in = len(wholes)
    sizes = [w.shape[4] for w in wholes]
    count, tail, dtype = wholes[0].shape[0], wholes[0].shape[5:], wholes[0].dtype

    def kernel(at, *refs):
        for dc in (1, 0):
            for dy in range(2):
                for dx in range(2):
                    y, c, x = (jnp.bitwise_xor(at[1 + j], d) for j, d in enumerate((dy, dc, dx)))
                    first = 0
                    for i in range(n_in):
                        refs[n_in + dc][dy, dx, 0, first : first + sizes[i]] = refs[i][0, y, c, x]
                        first += sizes[i]

    shape = jax.ShapeDtypeStruct((2, 2, count, sum(sizes)) + tail, dtype)
    return pl.pallas_call(
        kernel,
        grid=(count,),
        out_shape=[shape, shape],
        in_specs=[SMEM]
        + [
            pl.BlockSpec((1, 2, 2, 2, size) + tail, lambda z: (z, 0, 0, 0, 0, 0, 0))
            for size in sizes
        ],
        out_specs=[pl.BlockSpec((2, 2, 1, sum(sizes)) + tail, lambda z: (0, 0, z, 0, 0, 0))] * 2,
        compiler_params=pltpu.CompilerParams(vmem_limit_bytes=ROOM),
        name="taken_apart",
    )(where, *wholes)


def gathered(shard, cuts, where, relay):
    pieces = {0: shard}
    by = lax.axis_size("z") // 2
    while by:
        keys = sorted(pieces)
        if len(keys) == 1:
            received = swapped(shard, "z", by)[None]
        else:
            received = swapped(jnp.stack([pieces[k] for k in keys]), "z", by)
        for i, k in enumerate(keys):
            pieces[k ^ by] = received[i]
        by //= 2
    own = in_order([pieces[r] for r in range(len(pieces))], where)
    over_x = swapped(own, "x")
    over_y = swapped(own, "y")
    corner = swapped(over_x, "y") if relay == "y" else swapped(over_y, "x")
    planes = {(0, 0, 0): own, (0, 0, 1): over_x, (1, 0, 0): over_y, (1, 0, 1): corner}
    for dy, _, dx in list(planes):
        planes[dy, 1, dx] = swapped(planes[dy, 0, dx], "c")
    return assembled(planes, cuts, where)


def scattered_sum(wholes, where, relay):
    mine, other = taken_apart(wholes, where)
    received = swapped(other, "c")

    def both(dy, dx):
        return mine[dy, dx].astype(f32) + received[dy, dx].astype(f32)

    corner = swapped(both(1, 1).astype(bf16), relay).astype(f32)
    for_x, for_y = both(0, 1), both(1, 0)
    if relay == "y":
        for_x = for_x + corner
    else:
        for_y = for_y + corner
    total = (
        both(0, 0)
        + swapped(for_x.astype(bf16), "x").astype(f32)
        + swapped(for_y.astype(bf16), "y").astype(f32)
    )
    by = 1
    while by < lax.axis_size("z"):
        halves = total.reshape((total.shape[0] // 2, 2) + total.shape[1:])
        bit = (where[0] // by) % 2
        keep = lax.dynamic_index_in_dim(halves, bit, 1, keepdims=False)
        give = lax.dynamic_index_in_dim(halves, 1 - bit, 1, keepdims=False)
        total = keep + swapped(give.astype(bf16), "z", by).astype(f32)
        by *= 2
    return total[0]


def lane_halves(block):
    lanes = lax.broadcasted_iota(jnp.int32, block.shape, 1)
    zero = jnp.zeros_like(block)
    return jnp.where(lanes < HEAD, block, zero), jnp.where(lanes < HEAD, zero, block)


def allowed_at(shape, first, bounds, causal):
    keys = first + lax.broadcasted_iota(jnp.int32, shape, 0)
    allowed = (keys >= bounds[0]) & (keys < bounds[1])
    if causal:
        queries = lax.broadcasted_iota(jnp.int32, shape, 1)
        allowed = allowed & (keys - shape[1] <= queries)
    return allowed


def attend_kernel(causal, block, bounds, q_ref, k_ref, v_ref, out_ref, low_ref, lse_ref):
    rows, width = q_ref.shape[0], k_ref.shape[0]
    halves = lane_halves(q_ref[...] * SCALE)

    def step(i, state):
        first = pl.multiple_of(i * block, block)
        keys, values = k_ref[pl.ds(first, block)], v_ref[pl.ds(first, block)]
        allowed = allowed_at((block, rows), first, bounds, causal)
        new = []
        for half in range(2):
            peak, total, summed = state[half]
            scores = jnp.where(allowed, times_transpose(keys, halves[half]), big_negative)
            top = jnp.maximum(peak, jnp.max(scores, axis=0, keepdims=True))
            weights = jnp.exp(scores - top)
            factor = jnp.exp(peak - top)
            new.append(
                (
                    top,
                    total * factor + jnp.sum(weights, axis=0, keepdims=True),
                    summed * factor + contract_rows(values, weights.astype(bf16)),
                )
            )
        return tuple(new)

    start = (
        jnp.full((1, rows), big_negative, f32),
        jnp.zeros((1, rows), f32),
        jnp.zeros((PAIR, rows), f32),
    )
    state = (start, start)
    if width == block:
        state = step(0, state)
    else:
        state = lax.fori_loop(0, width // block, step, state)
    outs = [s[2] / s[1] for s in state]
    out = jnp.concatenate([outs[0][:HEAD], outs[1][HEAD:]], axis=0).T
    out_ref[...] = out
    low_ref[...] = out.astype(bf16)
    for half in range(2):
        lse_ref[0, half : half + 1, :] = state[half][0] + jnp.log(state[half][1])


def attend(queries, keys, values, bounds, causal):
    rows, width = queries.shape[0], keys.shape[0]
    block = min(width, 1024)
    spec = lambda n: pl.BlockSpec((n, PAIR), lambda h: (0, h))
    return pl.pallas_call(
        lambda *refs: attend_kernel(causal, block, *refs),
        grid=(PAIRS,),
        in_specs=[SMEM, spec(rows), spec(width), spec(width)],
        out_specs=[spec(rows), spec(rows), pl.BlockSpec((1, 2, rows), lambda h: (h, 0, 0))],
        out_shape=[
            jax.ShapeDtypeStruct((rows, D), f32),
            jax.ShapeDtypeStruct((rows, D), bf16),
            jax.ShapeDtypeStruct((PAIRS, 2, rows), f32),
        ],
        compiler_params=pltpu.CompilerParams(vmem_limit_bytes=48 * 2**20),
        name="attend_self" if causal else "attend_cross",
    )(bounds, queries, keys, values)


def attend_back_kernel(
    causal, block, bounds, q_ref, k_ref, v_ref, o_ref, g_ref, lse_ref, dq_ref, dk_ref, dv_ref
):
    rows, width = q_ref.shape[0], k_ref.shape[0]
    query_halves = lane_halves(q_ref[...] * SCALE)
    grad_halves = lane_halves(g_ref[...])
    products = (g_ref[...].astype(f32) * o_ref[...]).T
    deltas = [
        jnp.sum(products[:HEAD], axis=0, keepdims=True),
        jnp.sum(products[HEAD:], axis=0, keepdims=True),
    ]

    def step(i, state):
        first = pl.multiple_of(i * block, block)
        keys, values = k_ref[pl.ds(first, block)], v_ref[pl.ds(first, block)]
        allowed = allowed_at((block, rows), first, bounds, causal)
        new, key_grad, value_grad = [], None, None
        for half in range(2):
            scores = jnp.where(allowed, times_transpose(keys, query_halves[half]), big_negative)
            probs = jnp.exp(scores - lse_ref[0, half : half + 1, :])
            value_part = matmul(probs.astype(bf16), grad_halves[half])
            slopes = times_transpose(values, grad_halves[half])
            score_grad = (probs * (slopes - deltas[half])).astype(bf16)
            key_part = matmul(score_grad, query_halves[half])
            new.append(state[half] + contract_rows(keys, score_grad))
            key_grad = key_part if key_grad is None else key_grad + key_part
            value_grad = value_part if value_grad is None else value_grad + value_part
        dk_ref[pl.ds(first, block)] = key_grad.astype(bf16)
        dv_ref[pl.ds(first, block)] = value_grad.astype(bf16)
        return tuple(new)

    zero = jnp.zeros((PAIR, rows), f32)
    state = (zero, zero)
    if width == block:
        state = step(0, state)
    else:
        state = lax.fori_loop(0, width // block, step, state)
    dq_ref[...] = (
        (jnp.concatenate([state[0][:HEAD], state[1][HEAD:]], axis=0) * SCALE).T.astype(bf16)
    )


def attend_back(queries, keys, values, out, grad, lse, bounds, causal):
    rows, width = queries.shape[0], keys.shape[0]
    block = min(width, 1024)
    spec = lambda n: pl.BlockSpec((n, PAIR), lambda h: (0, h))
    return pl.pallas_call(
        lambda *refs: attend_back_kernel(causal, block, *refs),
        grid=(PAIRS,),
        in_specs=[SMEM, spec(rows), spec(width), spec(width), spec(rows), spec(rows)]
        + [pl.BlockSpec((1, 2, rows), lambda h: (h, 0, 0))],
        out_specs=[spec(rows), spec(width), spec(width)],
        out_shape=[
            jax.ShapeDtypeStruct((rows, D), bf16),
            jax.ShapeDtypeStruct((width, D), bf16),
            jax.ShapeDtypeStruct((width, D), bf16),
        ],
        compiler_params=pltpu.CompilerParams(vmem_limit_bytes=48 * 2**20),
        name="attend_back_self" if causal else "attend_back_cross",
    )(bounds, queries, keys, values, out, grad, lse)


def padded(shard, rows):
    return jnp.pad(shard, ((0, rows - shard.shape[0]), (0, 0)))


def grouped(shard, group):
    return shard.reshape(shard.shape[0] // group, group, shard.shape[1])


def spread(whole, group):
    z = lax.axis_size("z")
    return whole.reshape(z, 2, 2, 2, whole.shape[0] // (8 * z * group), group, whole.shape[1])


def per_device(
    tokens,
    memory,
    self_query,
    self_key,
    self_value,
    self_output,
    cross_query,
    cross_key,
    cross_value,
    cross_output,
    feed_in,
    feed_out,
    gain_self,
    gain_cross,
    gain_feed,
    doc_lengths,
    seg_doc,
    cotangent,
):
    where = position()
    token_rows = tokens.shape[0]
    count = lax.axis_size("z") * 8
    slots = self_query.shape[0]
    memory_rows = memory.shape[0]
    group = math.gcd(8, slots) if slots % 4 == 0 else slots
    memory_groups = pl.cdiv(memory_rows, group)
    gain_groups = pl.cdiv(3, group)
    gain_rows = gain_groups * group
    slot_groups = slots // group

    earlier = lax.ppermute(tokens, "x", [(0, 1)])

    gains = jnp.pad(jnp.stack([gain_self, gain_cross, gain_feed]), ((0, gain_rows - 3), (0, D - slots)))
    four = [(i * slot_groups, slot_groups) for i in range(4)]
    self_shard = jnp.concatenate(
        [grouped(w, group) for w in (self_query, self_key, self_value, self_output, gains)]
    )
    wholes = gathered(self_shard, four + [(4 * slot_groups, gain_groups)], where, "y")
    self_query, self_key, self_value, self_output = (w.reshape(D, D) for w in wholes[:4])
    gains = wholes[4].reshape(count, gain_rows, D)[:, :3, :slots]
    gain_self, gain_cross, gain_feed = (
        gains[:, i].reshape(D).astype(f32) for i in range(3)
    )
    cross_shard = jnp.concatenate(
        [grouped(w, group) for w in (cross_query, cross_key, cross_value, cross_output)]
        + [grouped(padded(memory, memory_groups * group), group)]
    )
    wholes = gathered(cross_shard, four + [(4 * slot_groups, memory_groups)], where, "x")
    cross_query, cross_key, cross_value, cross_output = (w.reshape(D, D) for w in wholes[:4])
    memory_all = wholes[4].reshape(count, memory_groups * group, D)[:, :memory_rows]
    memory_all = memory_all.reshape(count * memory_rows, D)
    feed_in = gathered(grouped(feed_in, group), [(0, slot_groups)], where, "y")[0].reshape(
        D, feed_in.shape[1]
    )
    feed_out = gathered(grouped(feed_out, group), [(0, feed_out.shape[0] // group)], where, "x")[
        0
    ].reshape(count * feed_out.shape[0], D)

    both_tokens = jnp.concatenate([earlier, tokens], axis=0)
    queries = matmul(tokens, self_query).astype(bf16)
    keys = matmul(both_tokens, self_key).astype(bf16)
    values = matmul(both_tokens, self_value).astype(bf16)
    self_bounds = jnp.stack(
        [jnp.where(where[3] == 0, token_rows, 0), jnp.int32(2 * token_rows)]
    ).astype(jnp.int32)
    self_full, self_out, self_lse = attend(queries, keys, values, self_bounds, True)
    mid_self = tokens.astype(f32) + matmul(self_out, self_output)
    hidden_self, back_self = jax.vjp(layer_norm, mid_self, gain_self)
    hidden_self_low = hidden_self.astype(bf16)

    window = count * memory_rows // 2
    ends = jnp.cumsum(doc_lengths)
    document = table_entry(seg_doc, (where[0] * 2 + where[1]) * 2 + where[2])
    doc_end = table_entry(ends, document)
    doc_start = doc_end - table_entry(doc_lengths, document)
    window_start = jnp.minimum(doc_start, window)
    cross_bounds = jnp.stack([doc_start - window_start, doc_end - window_start]).astype(jnp.int32)
    memory_here = lax.dynamic_slice(memory_all, (window_start, 0), (window, D))
    cross_queries = matmul(hidden_self_low, cross_query).astype(bf16)
    memory_keys = matmul(memory_here, cross_key).astype(bf16)
    memory_values = matmul(memory_here, cross_value).astype(bf16)
    cross_full, cross_out, cross_lse = attend(
        cross_queries, memory_keys, memory_values, cross_bounds, False
    )
    mid_cross = hidden_self + matmul(cross_out, cross_output)
    hidden_cross, back_cross = jax.vjp(layer_norm, mid_cross, gain_cross)
    hidden_cross_low = hidden_cross.astype(bf16)

    inner = matmul(hidden_cross_low, feed_in)
    activated_full, back_gelu = jax.vjp(exact_gelu, inner)
    activated = activated_full.astype(bf16)
    mid_feed = hidden_cross + matmul(activated, feed_out)
    layer_out, back_feed = jax.vjp(layer_norm, mid_feed, gain_feed)
    gradient_feed_mid, gain_feed_sum = back_feed(cotangent.astype(f32))
    feed_rounded = gradient_feed_mid.astype(bf16)
    sum_feed_out = contract_rows(activated, feed_rounded).astype(bf16)
    total_feed_out = scattered_sum([spread(sum_feed_out, group)], where, "y")
    gradient_inner = back_gelu(times_transpose(feed_rounded, feed_out))[0].astype(bf16)
    sum_feed_in = contract_rows(hidden_cross_low, gradient_inner).astype(bf16)
    total_feed_in = scattered_sum([spread(sum_feed_in, group)], where, "x")
    gradient_hidden_cross = gradient_feed_mid + times_transpose(gradient_inner, feed_in)
    gradient_cross_mid, gain_cross_sum = back_cross(gradient_hidden_cross)
    cross_rounded = gradient_cross_mid.astype(bf16)

    sum_cross_output = contract_rows(cross_out, cross_rounded).astype(bf16)
    outgoing = times_transpose(cross_rounded, cross_output).astype(bf16)
    cross_query_grad, memory_key_grad, memory_value_grad = attend_back(
        cross_queries,
        memory_keys,
        memory_values,
        cross_full,
        outgoing,
        cross_lse,
        cross_bounds,
        False,
    )
    sum_cross_key = contract_rows(memory_here, memory_key_grad).astype(bf16)
    sum_cross_value = contract_rows(memory_here, memory_value_grad).astype(bf16)
    sum_cross_query = contract_rows(hidden_self_low, cross_query_grad).astype(bf16)
    sum_memory = lax.dynamic_update_slice(
        jnp.zeros((2 * window, D), bf16),
        (
            times_transpose(memory_key_grad, cross_key)
            + times_transpose(memory_value_grad, cross_value)
        ).astype(bf16),
        (window_start, 0),
    ).reshape(count, memory_rows, D)
    if memory_groups * group > memory_rows:
        sum_memory = jnp.pad(sum_memory, ((0, 0), (0, memory_groups * group - memory_rows), (0, 0)))
    sum_memory = sum_memory.reshape(count * memory_groups * group, D)
    total_cross = scattered_sum(
        [
            spread(s, group)
            for s in (
                sum_cross_query,
                sum_cross_key,
                sum_cross_value,
                sum_cross_output,
                sum_memory,
            )
        ],
        where,
        "y",
    )
    gradient_hidden_self = gradient_cross_mid + times_transpose(cross_query_grad, cross_query)
    gradient_self_mid, gain_self_sum = back_self(gradient_hidden_self)
    self_rounded = gradient_self_mid.astype(bf16)

    sum_self_output = contract_rows(self_out, self_rounded).astype(bf16)
    self_outgoing = times_transpose(self_rounded, self_output).astype(bf16)
    query_grad, key_grad, value_grad = attend_back(
        queries, keys, values, self_full, self_outgoing, self_lse, self_bounds, True
    )
    both_grad = times_transpose(key_grad, self_key) + times_transpose(value_grad, self_value)
    sent_back = lax.ppermute(both_grad[:token_rows].astype(bf16), "x", [(1, 0)])
    sum_self_query = contract_rows(tokens, query_grad).astype(bf16)
    sum_self_key = contract_rows(both_tokens, key_grad).astype(bf16)
    sum_self_value = contract_rows(both_tokens, value_grad).astype(bf16)
    gain_sums = jnp.stack([gain_self_sum, gain_cross_sum, gain_feed_sum]).astype(bf16)
    gain_sums = jnp.pad(
        jnp.transpose(gain_sums.reshape(3, count, slots), (1, 0, 2)),
        ((0, 0), (0, gain_rows - 3), (0, D - slots)),
    ).reshape(count * gain_rows, D)
    total_self = scattered_sum(
        [
            spread(s, group)
            for s in (sum_self_query, sum_self_key, sum_self_value, sum_self_output, gain_sums)
        ],
        where,
        "x",
    )
    gradient_tokens = (
        gradient_self_mid
        + times_transpose(query_grad, self_query)
        + both_grad[token_rows:]
        + sent_back.astype(f32)
    )

    def rows_of(total, first, groups):
        return total[first : first + groups].reshape(groups * group, total.shape[2])

    self_parts = [rows_of(total_self, first, size) for first, size in four]
    cross_parts = [rows_of(total_cross, first, size) for first, size in four]
    gain_parts = rows_of(total_self, 4 * slot_groups, gain_groups)
    return (
        layer_out.astype(bf16),
        gradient_tokens,
        rows_of(total_cross, 4 * slot_groups, memory_groups)[:memory_rows],
        *self_parts,
        *cross_parts,
        rows_of(total_feed_in, 0, total_feed_in.shape[0]),
        rows_of(total_feed_out, 0, total_feed_out.shape[0]),
        gain_parts[0, :slots],
        gain_parts[1, :slots],
        gain_parts[2, :slots],
    )


def solution(mesh):
    fine = Mesh(mesh.devices.reshape(-1, 2, 2, 2), ALL)
    rows = P(ALL, None)
    return jax.shard_map(
        per_device,
        mesh=fine,
        in_specs=(rows,) * 12 + (P(ALL),) * 3 + (P(), P(), rows),
        out_specs=(rows,) * 13 + (P(ALL),) * 3,
        check_vma=False,
    )
```

```python
import math

import jax
import jax.numpy as jnp
from jax import lax
from jax.experimental import pallas as pl
from jax.experimental.pallas import tpu as pltpu
from jax.sharding import Mesh
from jax.sharding import PartitionSpec as P

D = 768
HEADS = 12
HEAD = 64
PAIR = 2 * HEAD
PAIRS = HEADS // 2
SCALE = HEAD ** (-0.5)

big_negative = -1e30
epsilon = 1e-05
bf16 = jnp.bfloat16
f32 = jnp.float32
ALL = ("z", "y", "c", "x")
NOTHING = pl.CostEstimate(flops=1, bytes_accessed=1, transcendentals=0)
VMEM = pl.BlockSpec(memory_space=pltpu.VMEM)
ANY = pl.BlockSpec(memory_space=pl.ANY)


def room_for(*arrays):
    held = 0
    for a in arrays:
        rows, width = a.shape[-2], a.shape[-1]
        held += math.prod(a.shape[:-2]) * pl.cdiv(rows, 16 if rows % 8 else 8) * (
            16 if rows % 8 else 8
        ) * pl.cdiv(width, 128) * 128 * a.dtype.itemsize
    return held + 2 * 2**20
SMEM = pl.BlockSpec(memory_space=pltpu.SMEM)


def matmul(left, right):
    return jnp.dot(left, right, preferred_element_type=f32)


def contract_rows(left, right):
    return lax.dot_general(left, right, (((0,), (0,)), ((), ())), preferred_element_type=f32)


def times_transpose(left, right):
    return lax.dot_general(left, right, (((1,), (1,)), ((), ())), preferred_element_type=f32)


def layer_norm(values, gain):
    centered = values - jnp.mean(values, axis=-1, keepdims=True)
    variance = jnp.mean(centered * centered, axis=-1, keepdims=True)
    return centered * lax.rsqrt(variance + epsilon) * gain


def exact_gelu(values):
    return jax.nn.gelu(values, approximate=False)


def table_entry(table, index):
    places = jnp.arange(table.shape[0], dtype=jnp.int32)
    return jnp.sum(jnp.where(places == index, table, 0))


def swapped(value, axis, by=1):
    size = lax.axis_size(axis)
    return lax.ppermute(value, axis, [(i, i ^ by) for i in range(size)])


def position():
    return jnp.stack([lax.axis_index(a).astype(jnp.int32) for a in ALL])


def packed(shards, group):
    blocks, first = [], 0
    for i, shard in enumerate(shards):
        size = shard.shape[0] // group
        for column in range(0, shard.shape[1], D):
            blocks.append((i, column, first, size))
            first += size
    n_in = len(shards)

    def kernel(*refs):
        out, sems = refs[-2:]
        copies = [
            pltpu.make_async_copy(
                refs[i].at[:, :, pl.ds(column, D)], out.at[pl.ds(at, size)], sems.at[n]
            )
            for n, (i, column, at, size) in enumerate(blocks)
        ]
        for copy in copies:
            copy.start()
        for copy in copies:
            copy.wait()

    return pl.pallas_call(
        kernel,
        out_shape=jax.ShapeDtypeStruct((first, group, D), shards[0].dtype),
        in_specs=[pl.BlockSpec(memory_space=pltpu.HBM)] * n_in,
        out_specs=VMEM,
        scratch_shapes=[pltpu.SemaphoreType.DMA((len(blocks),))],
        compiler_params=pltpu.CompilerParams(vmem_limit_bytes=60 * 2**20),
        cost_estimate=NOTHING,
        name="packed",
    )(*(s.reshape(s.shape[0] // group, group, s.shape[1]) for s in shards))


def in_order(pieces, places, where, cut=None):
    n_in = len(pieces)
    count, groups = len(places), pieces[0].shape[1]
    spans = [(0, groups)] if cut is None else [(0, cut), (cut, groups - cut)]

    def kernel(at, *refs):
        first = 0
        for i in range(n_in):
            for j in range(pieces[i].shape[0]):
                z = jnp.bitwise_xor(at[0], places[first])
                for o, (start, size) in enumerate(spans):
                    refs[n_in + o][z] = refs[i][j, start : start + size]
                first += 1

    outs = pl.pallas_call(
        kernel,
        out_shape=[
            jax.ShapeDtypeStruct((count, size) + pieces[0].shape[2:], pieces[0].dtype)
            for _, size in spans
        ],
        in_specs=[SMEM] + [VMEM] * n_in,
        out_specs=[VMEM] * len(spans),
        compiler_params=pltpu.CompilerParams(vmem_limit_bytes=room_for(*pieces)),
        cost_estimate=NOTHING,
        name="in_order",
    )(where, *pieces)
    return outs[0] if cut is None else outs


def half_of(own, over_x, over_y, corners, where):
    count, groups, *tail = own.shape
    tail = tuple(tail)
    half = count // 2

    def kernel(at, own_ref, x_ref, y_ref, first_ref, second_ref, out_ref):
        y, x = at[1], at[3]
        out_ref[:, y, x] = own_ref[...]
        out_ref[:, y, 1 - x] = x_ref[...]
        out_ref[:, 1 - y, x] = y_ref[...]
        out_ref[:half, 1 - y, 1 - x] = first_ref[...]
        out_ref[half:, 1 - y, 1 - x] = second_ref[...]

    return pl.pallas_call(
        kernel,
        out_shape=jax.ShapeDtypeStruct((count, 2, 2, groups) + tail, own.dtype),
        in_specs=[SMEM] + [VMEM] * 5,
        out_specs=VMEM,
        compiler_params=pltpu.CompilerParams(vmem_limit_bytes=room_for(*[own] * 4)),
        cost_estimate=NOTHING,
        name="half_of",
    )(where, own, over_x, over_y, *corners)


def assembled(own, other, cuts, where):
    count, _, _, groups, group, width = own.shape
    step = count if count <= 8 else 1

    def kernel(at, *refs):
        for dc in range(2):
            c = jnp.bitwise_xor(at[2], dc)
            for o, (first, size, blocks) in enumerate(cuts):
                for b in range(blocks):
                    here = first + b * size
                    columns = slice(b * width, (b + 1) * width)
                    for z in range(step):
                        for y in range(2):
                            block = refs[dc][z, y, :, here : here + size]
                            refs[2 + o][z, y, c, :, :, :, columns] = block

    outs = [
        jax.ShapeDtypeStruct((count, 2, 2, 2, size, group, blocks * width), own.dtype)
        for _, size, blocks in cuts
    ]
    if step == count:
        specs = dict(in_specs=[SMEM, VMEM, VMEM], out_specs=[VMEM] * len(outs))
    else:
        specs = dict(
            grid=(count,),
            in_specs=[SMEM]
            + [pl.BlockSpec((1, 2, 2, groups, group, width), lambda z: (z, 0, 0, 0, 0, 0))] * 2,
            out_specs=[
                pl.BlockSpec((1,) + out.shape[1:], lambda z: (z, 0, 0, 0, 0, 0, 0)) for out in outs
            ],
        )
    return pl.pallas_call(
        kernel,
        out_shape=outs,
        compiler_params=pltpu.CompilerParams(
            vmem_limit_bytes=room_for(*outs) if step == count else 32 * 2**20
        ),
        cost_estimate=NOTHING,
        name="assembled",
        **specs,
    )(where, own, other)


def selection(where, core, slots, order):
    depth = 4 * len(order) * slots
    row = lax.broadcasted_iota(jnp.int32, (depth, 2 * depth), 0)
    column = lax.broadcasted_iota(jnp.int32, (depth, 2 * depth), 1)
    s, row = row % slots, row // slots
    z, row = jnp.zeros_like(row), row
    if len(order) > 1:
        step = row % len(order)
        bits, reversed_step = len(order).bit_length() - 1, jnp.zeros_like(row)
        for i in range(bits):
            reversed_step = reversed_step + ((step >> i) & 1) * (len(order) >> (i + 1))
        z = jnp.bitwise_xor(where[0], reversed_step)
        row = row // len(order)
    y, x = jnp.bitwise_xor(where[1], row // 2), jnp.bitwise_xor(where[3], row % 2)
    c = jnp.bitwise_xor(where[2], core)
    return (column == (((z * 2 + y) * 2 + c) * 2 + x) * slots + s).astype(bf16)


def mine_shapes(rows, width):
    return [jax.ShapeDtypeStruct((rows, width), f32)] + [
        jax.ShapeDtypeStruct((n, width), bf16) for n in (rows, rows, rows // 2, rows - rows // 2)
    ]


def taken_in(mine, received):
    _, rows, width = mine.shape
    half = rows // 2

    def kernel(mine_ref, got_ref, own, for_x, for_y, first, second):
        def total(side, at):
            return mine_ref[side, at].astype(f32) + got_ref[side, at].astype(f32)

        for i, ref in enumerate((own, for_x, for_y)):
            ref[...] = total(i, pl.ds(0, rows)).astype(ref.dtype)
        first[...] = total(3, pl.ds(0, half)).astype(bf16)
        second[...] = total(3, pl.ds(half, rows - half)).astype(bf16)

    out_shape = mine_shapes(rows, width)
    return pl.pallas_call(
        kernel,
        out_shape=out_shape,
        in_specs=[VMEM] * 2,
        out_specs=[VMEM] * 5,
        compiler_params=pltpu.CompilerParams(vmem_limit_bytes=room_for(*out_shape)),
        cost_estimate=NOTHING,
        name="taken_in",
    )(mine, received)


def sums_in_parts(where, arrays, products, memory_rows):
    order = z_places()
    slots = D // (8 * len(order))
    width = D * sum(arrays[right].shape[1] // D for _, right, _ in products if right is not None)
    width += sum(arrays[left].shape[0] for left, right, _ in products if right is None)
    given = []
    for core in range(2):
        pick = selection(where, core, slots, order)
        columns = []
        for left, right, first in products:
            turned = times_transpose(pick, arrays[left]).astype(bf16)
            if right is not None:
                turned = matmul(turned[:, first:], arrays[right]).astype(bf16)
            columns.append(turned)
        rows = jnp.concatenate(columns, axis=1).reshape(4, -1, width)
        if memory_rows:
            devices = []
            for side in range(4):
                y, x = jnp.bitwise_xor(where[1], side // 2), jnp.bitwise_xor(where[3], side % 2)
                c = jnp.bitwise_xor(where[2], core)
                devices += [((jnp.bitwise_xor(where[0], r) * 2 + y) * 2 + c) * 2 + x for r in order]
            key_grad, value_grad, key_weight, value_weight = arrays[-4:]
            grad = times_transpose(key_grad, key_weight) + times_transpose(value_grad, value_weight)
            whole = lax.dynamic_update_slice(
                jnp.zeros((8 * len(order) * memory_rows, D), bf16), grad.astype(bf16), (where[4], 0)
            )
            slabs = whole.reshape(8 * len(order), memory_rows, D)[jnp.stack(devices)]
            fold = width // D
            slabs = slabs.reshape(4, len(order), fold, memory_rows // fold, D)
            slabs = jnp.transpose(slabs, (0, 1, 3, 2, 4)).reshape(4, -1, width)
            rows = jnp.concatenate([rows, slabs], axis=1)
        given.append(rows)
    return given


def sums_out(where, arrays, products, memory_rows=0):
    order = z_places()
    slots = D // (8 * len(order))
    if slots % 8:
        return sums_in_parts(where, arrays, products, memory_rows)
    n_in = len(arrays)
    depth = slots * len(order)
    blocks, column = [], 0
    for left, right, first in products:
        wide = arrays[left].shape[0] if right is None else arrays[right].shape[1]
        for at in range(0, wide, D):
            size = min(D, wide - at)
            blocks.append((left, right, first, at, size, column))
            column += size
    width = column
    fold = width // D
    part = memory_rows // fold
    rows = depth + len(order) * part
    window = arrays[-4].shape[0] if memory_rows else 8

    def kernel(at, *refs):
        ins, outs, block_ref, grad_ref = refs[:n_in], refs[n_in : n_in + 2], refs[-2], refs[-1]

        def places(core):
            c = jnp.bitwise_xor(at[2], core)
            for side in range(4):
                y, x = jnp.bitwise_xor(at[1], side // 2), jnp.bitwise_xor(at[3], side % 2)
                for i, r in enumerate(order):
                    yield side, i, ((jnp.bitwise_xor(at[0], r) * 2 + y) * 2 + c) * 2 + x

        if memory_rows:
            key_grad, value_grad, key_weight, value_weight = ins[-4:]
            grad_ref[...] = times_transpose(key_grad[...], key_weight[...]) + times_transpose(
                value_grad[...], value_weight[...]
            )
            for core in (1, 0):
                for side, i, device in places(core):
                    start = device * memory_rows - at[4]
                    inside = (start >= 0) & (start + memory_rows <= window)
                    start = pl.multiple_of(jnp.where(inside, start, 0), memory_rows)
                    slab = grad_ref[pl.ds(start, memory_rows), :]
                    slab = jnp.where(inside, slab, jnp.zeros_like(slab)).astype(bf16)
                    for j in range(fold):
                        here = pl.ds(depth + i * part, part)
                        outs[core][side, here, j * D : (j + 1) * D] = slab[
                            j * part : (j + 1) * part
                        ]
        for n, (left, right, first, from_, size, to) in enumerate(blocks):
            if right is None:
                block = ins[left][...].astype(f32).T
            else:
                block = contract_rows(ins[left][first:, :], ins[right][:, from_ : from_ + size])
            slot = n % 2
            block_ref[slot, :, :, :size] = block.reshape(8 * len(order), slots, size)
            for core in (1, 0):
                for side, i, device in places(core):
                    slab = block_ref[slot, device, :, :size].astype(bf16)
                    outs[core][side, i * slots : (i + 1) * slots, to : to + size] = slab

    shape = jax.ShapeDtypeStruct((4, rows, width), bf16)
    return pl.pallas_call(
        kernel,
        out_shape=[shape, shape],
        in_specs=[SMEM] + [VMEM] * n_in,
        out_specs=[VMEM] * 2,
        scratch_shapes=[
            pltpu.VMEM((2, 8 * len(order), slots, D), f32),
            pltpu.VMEM((window, D), f32),
        ],
        compiler_params=pltpu.CompilerParams(
            vmem_limit_bytes=room_for(shape, shape) + 2 * D * D * 4 + window * D * 4 + 3 * 2**20
        ),
        cost_estimate=NOTHING,
        name="sums_out",
    )(where, *arrays)


def hidden_sums_out(where, activated, grad):
    hidden = activated.shape[1]
    order = z_places()
    span = hidden // len(order)
    slots = span // 8
    if span % 128 or slots % 8:
        given = []
        for core in range(2):
            pick = selection(where, core, slots, order)
            turned = times_transpose(pick, activated).astype(bf16)
            given.append(matmul(turned, grad).astype(bf16).reshape(4, -1, D))
        return given

    def kernel(at, act_ref, grad_ref, mine, other, block_ref):
        for i, r in enumerate(order):
            first = pl.multiple_of(jnp.bitwise_xor(at[0], r) * span, 128)
            block = contract_rows(act_ref[:, pl.ds(first, span)], grad_ref[...])
            block_ref[i % 2] = block.reshape(8, slots, D)
            for core, ref in ((1, other), (0, mine)):
                c = jnp.bitwise_xor(at[2], core)
                for side in range(4):
                    y, x = jnp.bitwise_xor(at[1], side // 2), jnp.bitwise_xor(at[3], side % 2)
                    slab = block_ref[i % 2, (y * 2 + c) * 2 + x].astype(bf16)
                    ref[side, i * slots : (i + 1) * slots, :] = slab

    shape = jax.ShapeDtypeStruct((4, len(order) * slots, D), bf16)
    return pl.pallas_call(
        kernel,
        out_shape=[shape, shape],
        in_specs=[SMEM] + [VMEM] * 2,
        out_specs=[VMEM] * 2,
        scratch_shapes=[pltpu.VMEM((2, 8, slots, D), f32)],
        compiler_params=pltpu.CompilerParams(
            vmem_limit_bytes=room_for(shape, shape) + 8 * 2**20
        ),
        cost_estimate=NOTHING,
        name="hidden_sums_out",
    )(where, activated, grad)


def hold(*values):
    return lax.optimization_barrier(values)


def z_first(shard):
    return swapped(shard[None], "z", lax.axis_size("z") // 2)


def z_rest(shard, received):
    by = lax.axis_size("z") // 2
    pieces, places = [shard[None], received], [0, by]
    while by > 1:
        by //= 2
        received = swapped(jnp.concatenate(pieces), "z", by)
        pieces, places = pieces + [received], places + [p ^ by for p in places]
    return pieces


def z_places():
    by, places = lax.axis_size("z") // 2, [0]
    while by:
        places = places + [p ^ by for p in places]
        by //= 2
    return places


def corners_in(over_x, over_y):
    half = over_x.shape[0] // 2
    return swapped(over_x[:half], "y"), swapped(over_y[half:], "x")


def corners_out(mine):
    return swapped(mine[3], "y"), swapped(mine[4], "x")


def sides_out(mine, corners):
    _, for_x, for_y = mine[:3]
    half = corners[0].shape[0]

    def kernel(x_ref, y_ref, first_ref, second_ref, x_out, y_out):
        x_out[:half] = (x_ref[:half].astype(f32) + first_ref[...].astype(f32)).astype(bf16)
        x_out[half:] = x_ref[half:]
        y_out[:half] = y_ref[:half]
        y_out[half:] = (y_ref[half:].astype(f32) + second_ref[...].astype(f32)).astype(bf16)

    shape = jax.ShapeDtypeStruct(for_x.shape, bf16)
    x_out, y_out = pl.pallas_call(
        kernel,
        out_shape=[shape, shape],
        in_specs=[VMEM] * 4,
        out_specs=[VMEM] * 2,
        compiler_params=pltpu.CompilerParams(vmem_limit_bytes=room_for(shape, shape)),
        cost_estimate=NOTHING,
        name="sides_out",
    )(for_x, for_y, *corners)
    return swapped(x_out, "x"), swapped(y_out, "y")


def halved(terms, parts):
    rows, width = terms[0].shape
    n_in = len(terms)

    def kernel(*refs):
        start, out = 0, 0
        for part in parts:
            half = part // 2
            for first, ref in ((start, refs[n_in]), (start + half, refs[n_in + 1])):
                total = sum(r[pl.ds(first, half), :].astype(f32) for r in refs[:n_in])
                ref[pl.ds(out, half), :] = total.astype(ref.dtype)
            start, out = start + part, out + half

    return pl.pallas_call(
        kernel,
        out_shape=[
            jax.ShapeDtypeStruct((rows // 2, width), f32),
            jax.ShapeDtypeStruct((rows // 2, width), bf16),
        ],
        in_specs=[VMEM] * n_in,
        out_specs=[VMEM] * 2,
        compiler_params=pltpu.CompilerParams(vmem_limit_bytes=room_for(terms[0])),
        cost_estimate=NOTHING,
        name="halved",
    )(*terms)


def z_most(terms, parts):
    by = 1
    keep, give = halved(terms, parts)
    received, parts = swapped(give, "z", by), [p // 2 for p in parts]
    while 2 * by < lax.axis_size("z") // 2:
        by *= 2
        keep, give = halved([keep, received], parts)
        received, parts = swapped(give, "z", by), [p // 2 for p in parts]
    return keep, received


def z_last(keep, received, parts):
    by = lax.axis_size("z") // 2
    keep, give = halved([keep, received], [p // by for p in parts])
    return keep, swapped(give, "z", by)


def plus(keep, received):
    return keep + received.astype(f32)


def lane_halves(block):
    lanes = lax.broadcasted_iota(jnp.int32, block.shape, 1)
    zero = jnp.zeros_like(block)
    return jnp.where(lanes < HEAD, block, zero), jnp.where(lanes < HEAD, zero, block)


def allowed_at(shape, first, bounds, causal):
    keys = first + lax.broadcasted_iota(jnp.int32, shape, 0)
    allowed = (keys >= bounds[0]) & (keys < bounds[1])
    if causal:
        queries = lax.broadcasted_iota(jnp.int32, shape, 1)
        allowed = allowed & (keys - shape[1] <= queries)
    return allowed


def key_block(width):
    return next(width // n for n in range(1, width) if width % (16 * n) == 0 and width // n <= 1536)


def attend_kernel(causal, block, bounds, q_ref, k_ref, v_ref, out_ref, low_ref, lse_ref):
    rows, width = q_ref.shape[0], k_ref.shape[0]

    def pair(h, carried):
        lanes = pl.ds(pl.multiple_of(h * PAIR, PAIR), PAIR)
        halves = lane_halves(q_ref[:, lanes] * SCALE)

        def step(i, state):
            first = pl.multiple_of(i * block, block)
            keys, values = k_ref[pl.ds(first, block), lanes], v_ref[pl.ds(first, block), lanes]
            allowed = allowed_at((block, rows), first, bounds, causal)
            new = []
            for half in range(2):
                peak, total, summed = state[half]
                scores = jnp.where(allowed, times_transpose(keys, halves[half]), big_negative)
                top = jnp.maximum(peak, jnp.max(scores, axis=0, keepdims=True))
                weights = jnp.exp(scores - top)
                factor = jnp.exp(peak - top)
                new.append(
                    (
                        top,
                        total * factor + jnp.sum(weights, axis=0, keepdims=True),
                        summed * factor + contract_rows(values, weights.astype(bf16)),
                    )
                )
            return tuple(new)

        start = (
            jnp.full((1, rows), big_negative, f32),
            jnp.zeros((1, rows), f32),
            jnp.zeros((PAIR, rows), f32),
        )
        state = (start, start)
        if width == block:
            state = step(0, state)
        else:
            state = lax.fori_loop(0, width // block, step, state)
        outs = [s[2] / s[1] for s in state]
        out = jnp.concatenate([outs[0][:HEAD], outs[1][HEAD:]], axis=0).T
        out_ref[:, lanes] = out
        low_ref[:, lanes] = out.astype(bf16)
        for half in range(2):
            lse_ref[h, half : half + 1, :] = state[half][0] + jnp.log(state[half][1])
        return carried

    lax.fori_loop(0, PAIRS, pair, 0)


def attend(queries, keys, values, bounds, causal):
    rows, width = queries.shape[0], keys.shape[0]
    block = key_block(width)
    out_shape = [
        jax.ShapeDtypeStruct((rows, D), f32),
        jax.ShapeDtypeStruct((rows, D), bf16),
        jax.ShapeDtypeStruct((PAIRS, 2, rows), f32),
    ]
    return pl.pallas_call(
        lambda *refs: attend_kernel(causal, block, *refs),
        in_specs=[SMEM] + [VMEM] * 3,
        out_specs=[VMEM] * 3,
        out_shape=out_shape,
        compiler_params=pltpu.CompilerParams(
            vmem_limit_bytes=6 * 2**20 if width <= 2048 else 40 * 2**20
        ),
        cost_estimate=NOTHING,
        name="attend_self" if causal else "attend_cross",
    )(bounds, queries, keys, values)


def attend_back_kernel(
    causal, block, bounds, q_ref, k_ref, v_ref, o_ref, g_ref, lse_ref, dq_ref, dk_ref, dv_ref
):
    rows, width = q_ref.shape[0], k_ref.shape[0]

    def pair(h, carried):
        lanes = pl.ds(pl.multiple_of(h * PAIR, PAIR), PAIR)
        query_halves = lane_halves(q_ref[:, lanes] * SCALE)
        grads = g_ref[:, lanes]
        grad_halves = lane_halves(grads)
        products = (grads.astype(f32) * o_ref[:, lanes]).T
        deltas = [
            jnp.sum(products[:HEAD], axis=0, keepdims=True),
            jnp.sum(products[HEAD:], axis=0, keepdims=True),
        ]

        def step(i, state):
            first = pl.multiple_of(i * block, block)
            keys, values = k_ref[pl.ds(first, block), lanes], v_ref[pl.ds(first, block), lanes]
            allowed = allowed_at((block, rows), first, bounds, causal)
            new, key_grad, value_grad = [], None, None
            for half in range(2):
                scores = jnp.where(allowed, times_transpose(keys, query_halves[half]), big_negative)
                probs = jnp.exp(scores - lse_ref[h, half : half + 1, :])
                value_part = matmul(probs.astype(bf16), grad_halves[half])
                slopes = times_transpose(values, grad_halves[half])
                score_grad = (probs * (slopes - deltas[half])).astype(bf16)
                key_part = matmul(score_grad, query_halves[half])
                new.append(state[half] + contract_rows(keys, score_grad))
                key_grad = key_part if key_grad is None else key_grad + key_part
                value_grad = value_part if value_grad is None else value_grad + value_part
            dk_ref[pl.ds(first, block), lanes] = key_grad.astype(bf16)
            dv_ref[pl.ds(first, block), lanes] = value_grad.astype(bf16)
            return tuple(new)

        zero = jnp.zeros((PAIR, rows), f32)
        state = (zero, zero)
        if width == block:
            state = step(0, state)
        else:
            state = lax.fori_loop(0, width // block, step, state)
        dq_ref[:, lanes] = (
            (jnp.concatenate([state[0][:HEAD], state[1][HEAD:]], axis=0) * SCALE)
            .T.astype(bf16)
        )
        return carried

    lax.fori_loop(0, PAIRS, pair, 0)


def attend_back(queries, keys, values, out, grad, lse, bounds, causal):
    rows, width = queries.shape[0], keys.shape[0]
    block = key_block(width)
    out_shape = [
        jax.ShapeDtypeStruct((rows, D), bf16),
        jax.ShapeDtypeStruct((width, D), bf16),
        jax.ShapeDtypeStruct((width, D), bf16),
    ]
    return pl.pallas_call(
        lambda *refs: attend_back_kernel(causal, block, *refs),
        in_specs=[SMEM] + [VMEM] * 6,
        out_specs=[VMEM] * 3,
        out_shape=out_shape,
        compiler_params=pltpu.CompilerParams(
            vmem_limit_bytes=11 * 2**20 if width <= 2048 else 60 * 2**20
        ),
        cost_estimate=NOTHING,
        name="attend_back_self" if causal else "attend_back_cross",
    )(bounds, queries, keys, values, out, grad, lse)


def activate(values, weight):
    rows, hidden = values.shape[0], weight.shape[1]
    step = min(hidden, D)

    def kernel(values_ref, weight_ref, out_ref, slope_ref):
        for at in range(0, hidden, step):
            inner = matmul(values_ref[...], weight_ref[:, at : at + step])
            below = 0.5 * (1.0 + lax.erf(inner * (0.5**0.5)))
            out_ref[:, at : at + step] = (inner * below).astype(bf16)
            bell = jnp.exp(-0.5 * inner * inner) * (1.0 / math.sqrt(2.0 * math.pi))
            slope_ref[:, at : at + step] = below + inner * bell

    return pl.pallas_call(
        kernel,
        out_shape=[
            jax.ShapeDtypeStruct((rows, hidden), bf16),
            jax.ShapeDtypeStruct((rows, hidden), f32),
        ],
        in_specs=[VMEM] * 2,
        out_specs=[VMEM] * 2,
        compiler_params=pltpu.CompilerParams(vmem_limit_bytes=8 * 2**20),
        cost_estimate=NOTHING,
        name="activate",
    )(values, weight)


def padded(shard, rows):
    return jnp.pad(shard, ((0, rows - shard.shape[0]), (0, 0)))


def grouped(shard, group):
    return shard.reshape(shard.shape[0] // group, group, shard.shape[1])


def per_device(
    tokens,
    memory,
    self_query,
    self_key,
    self_value,
    self_output,
    cross_query,
    cross_key,
    cross_value,
    cross_output,
    feed_in,
    feed_out,
    gain_self,
    gain_cross,
    gain_feed,
    doc_lengths,
    seg_doc,
    cotangent,
):
    where = position()
    token_rows = tokens.shape[0]
    count = lax.axis_size("z") * 8
    slots = self_query.shape[0]
    memory_rows = memory.shape[0]
    group = math.gcd(8, slots) if slots % 4 == 0 else slots
    memory_groups = pl.cdiv(memory_rows, group)
    gain_groups = pl.cdiv(3, group)
    gain_rows = gain_groups * group
    slot_groups = slots // group

    gains = jnp.pad(jnp.stack([gain_self, gain_cross, gain_feed]), ((0, gain_rows - 3), (0, D - slots)))
    hidden = feed_in.shape[1]
    places = z_places()
    cuts1 = [(i * slot_groups, slot_groups, 1) for i in range(4)]
    cuts1.append((4 * slot_groups, gain_groups, 1))
    cuts2 = [(i * slot_groups, slot_groups, 1) for i in range(3)]
    cuts2.append((3 * slot_groups, memory_groups, 1))
    cuts3 = [(0, slot_groups, 1), (slot_groups, slot_groups, hidden // D)]
    cuts4 = [(0, feed_out.shape[0] // group, 1)]
    s1 = packed([self_query, self_key, self_value, self_output, gains], group)
    s2 = packed(
        [cross_query, cross_key, cross_value, padded(memory, memory_groups * group)], group
    )
    s3 = packed([cross_output, feed_in], group)
    s4 = grouped(feed_out, group)

    a1 = z_first(s1)
    earlier = lax.ppermute(tokens, "x", [(0, 1)])
    a1, s2, s3, s4 = hold(a1, s2, s3, s4)
    b1 = z_rest(s1, a1)
    a2 = z_first(s2)
    own1 = in_order(b1, places, where)
    own1, a2, earlier, s3, s4, doc_lengths, seg_doc = hold(
        own1, a2, earlier, s3, s4, doc_lengths, seg_doc
    )
    x1, y1 = swapped(own1, "x"), swapped(own1, "y")
    b2 = z_rest(s2, a2)
    a3 = z_first(s3)
    window = count * memory_rows // 2 + memory_rows
    ends = jnp.cumsum(doc_lengths)
    document = table_entry(seg_doc, (where[0] * 2 + where[1]) * 2 + where[2])
    doc_end = table_entry(ends, document)
    doc_start = doc_end - table_entry(doc_lengths, document)
    window_start = jnp.minimum(
        doc_start // memory_rows * memory_rows, count * memory_rows - window
    ).astype(jnp.int32)
    cross_bounds = jnp.stack([doc_start - window_start, doc_end - window_start]).astype(jnp.int32)
    where_window = jnp.concatenate([where, window_start[None]])
    self_bounds = jnp.stack(
        [jnp.where(where[3] == 0, token_rows, 0), jnp.int32(2 * token_rows)]
    ).astype(jnp.int32)
    both_tokens = jnp.concatenate([earlier, tokens], axis=0)
    own2 = in_order(b2, places, where)
    own2, x1, y1, own1, both_tokens, where_window, cross_bounds, self_bounds, s4 = hold(
        own2, x1, y1, own1, both_tokens, where_window, cross_bounds, self_bounds, s4
    )

    d1 = corners_in(x1, y1)
    x2, y2 = swapped(own2, "x"), swapped(own2, "y")
    b3 = z_rest(s3, a3)
    own3 = in_order(b3, places, where)
    a4 = z_first(s4)
    d1, x2, y2, own2, own3, a4 = hold(d1, x2, y2, own2, own3, a4)

    d2 = corners_in(x2, y2)
    x3, y3 = swapped(own3, "x"), swapped(own3, "y")
    half1 = half_of(own1, x1, y1, d1, where)
    c1 = swapped(half1, "c")
    wholes = assembled(half1, c1, cuts1, where)
    self_query, self_key, self_value, self_output = (w.reshape(D, D) for w in wholes[:4])
    a4, s4, self_query = hold(a4, s4, self_query)
    b4 = z_rest(s4, a4)
    own4 = in_order(b4, places, where)
    gains = wholes[4].reshape(count, gain_rows, D)[:, :3, :slots]
    gain_self, gain_cross, gain_feed = (
        gains[:, i].reshape(D).astype(f32) for i in range(3)
    )
    queries = matmul(tokens, self_query).astype(bf16)
    keys = matmul(both_tokens, self_key).astype(bf16)
    values = matmul(both_tokens, self_value).astype(bf16)
    self_full, self_out, self_lse = attend(queries, keys, values, self_bounds, True)
    mid_self = tokens.astype(f32) + matmul(self_out, self_output)
    hidden_self, back_self = jax.vjp(layer_norm, mid_self, gain_self)
    hidden_self_low = hidden_self.astype(bf16)
    d2, x3, y3, own3, own4, hidden_self, hidden_self_low = hold(
        d2, x3, y3, own3, own4, hidden_self, hidden_self_low
    )

    d3 = corners_in(x3, y3)
    x4, y4 = swapped(own4, "x"), swapped(own4, "y")
    half2 = half_of(own2, x2, y2, d2, where)
    c2 = swapped(half2, "c")
    wholes = assembled(half2, c2, cuts2, where)
    cross_query, cross_key, cross_value = (w.reshape(D, D) for w in wholes[:3])
    memory_all = wholes[3].reshape(count, memory_groups * group, D)[:, :memory_rows]
    memory_all = memory_all.reshape(count * memory_rows, D)
    memory_here = lax.dynamic_slice(memory_all, (where_window[4], 0), (window, D))
    cross_queries = matmul(hidden_self_low, cross_query).astype(bf16)
    memory_keys = matmul(memory_here, cross_key).astype(bf16)
    memory_values = matmul(memory_here, cross_value).astype(bf16)
    cross_full, cross_out, cross_lse = attend(
        cross_queries, memory_keys, memory_values, cross_bounds, False
    )
    d3, x4, y4, own4, cross_out = hold(d3, x4, y4, own4, cross_out)

    d4 = corners_in(x4, y4)
    half3 = half_of(own3, x3, y3, d3, where)
    c3 = swapped(half3, "c")
    wholes = assembled(half3, c3, cuts3, where)
    cross_output, feed_in = (w.reshape(D, w.shape[-1]) for w in wholes)
    mid_cross = hidden_self + matmul(cross_out, cross_output)
    hidden_cross, back_cross = jax.vjp(layer_norm, mid_cross, gain_cross)
    hidden_cross_low = hidden_cross.astype(bf16)
    activated, slope = activate(hidden_cross_low, feed_in)
    d4, activated, own4 = hold(d4, activated, own4)
    half4 = half_of(own4, x4, y4, d4, where)
    c4 = swapped(half4, "c")
    wholes = assembled(half4, c4, cuts4, where)
    feed_out = wholes[0].reshape(hidden, D)
    mid_feed = hidden_cross + matmul(activated, feed_out)
    layer_out, back_feed = jax.vjp(layer_norm, mid_feed, gain_feed)
    gradient_feed_mid, gain_feed_sum = back_feed(cotangent.astype(f32))
    feed_rounded = gradient_feed_mid.astype(bf16)
    m4, o4 = hidden_sums_out(where, activated, feed_rounded)
    m4, o4, feed_rounded = hold(m4, o4, feed_rounded)
    r4 = swapped(o4, "c")
    gradient_inner = (times_transpose(feed_rounded, feed_out) * slope).astype(bf16)
    m3, o3 = sums_out(where, [hidden_cross_low, gradient_inner], [(0, 1, 0)])
    r4, m3, o3, gradient_inner = hold(r4, m3, o3, gradient_inner)
    m4 = taken_in(m4, r4)
    d4 = corners_out(m4)
    r3 = swapped(o3, "c")
    gradient_hidden_cross = gradient_feed_mid + times_transpose(gradient_inner, feed_in)
    gradient_cross_mid, gain_cross_sum = back_cross(gradient_hidden_cross)
    cross_rounded = gradient_cross_mid.astype(bf16)

    outgoing = times_transpose(cross_rounded, cross_output).astype(bf16)
    r3, d4, outgoing, cross_rounded = hold(r3, d4, outgoing, cross_rounded)
    x4, y4 = sides_out(m4, d4)
    m3 = taken_in(m3, r3)
    d3 = corners_out(m3)
    cross_query_grad, memory_key_grad, memory_value_grad = attend_back(
        cross_queries,
        memory_keys,
        memory_values,
        cross_full,
        outgoing,
        cross_lse,
        cross_bounds,
        False,
    )
    x4, y4, d3, cross_query_grad, memory_key_grad, memory_value_grad, cross_rounded = hold(
        x4, y4, d3, cross_query_grad, memory_key_grad, memory_value_grad, cross_rounded
    )
    x3, y3 = sides_out(m3, d3)
    parts4, parts2, parts1 = [hidden // 8], [D // 8, count * memory_rows // 32], [D // 8]
    k4 = z_most([m4[0], x4, y4], parts4)
    m2, o2 = sums_out(
        where_window,
        [
            hidden_self_low,
            cross_query_grad,
            memory_here,
            cross_out,
            cross_rounded,
            memory_key_grad,
            memory_value_grad,
            cross_key,
            cross_value,
        ],
        [(0, 1, 0), (2, 5, 0), (2, 6, 0), (3, 4, 0)],
        memory_rows,
    )
    x3, y3, k4, m2, o2, cross_query_grad = hold(x3, y3, k4, m2, o2, cross_query_grad)
    r2 = swapped(o2, "c")
    k3 = z_most([m3[0], x3, y3], parts1)
    k4 = z_last(*k4, parts4)
    gradient_hidden_self = gradient_cross_mid + times_transpose(cross_query_grad, cross_query)
    gradient_self_mid, gain_self_sum = back_self(gradient_hidden_self)
    self_rounded = gradient_self_mid.astype(bf16)
    self_outgoing = times_transpose(self_rounded, self_output).astype(bf16)

    query_grad, key_grad, value_grad = attend_back(
        queries, keys, values, self_full, self_outgoing, self_lse, self_bounds, True
    )
    r2, k3, k4, query_grad, key_grad, value_grad, self_rounded = hold(
        r2, k3, k4, query_grad, key_grad, value_grad, self_rounded
    )
    m2 = taken_in(m2, r2)
    d2 = corners_out(m2)
    k3 = z_last(*k3, parts1)
    gain_sums = jnp.pad(
        jnp.stack([gain_self_sum, gain_cross_sum, gain_feed_sum]).astype(bf16),
        ((0, 128 - 3), (0, 0)),
    )
    m1, o1 = sums_out(
        where,
        [
            both_tokens,
            query_grad,
            key_grad,
            value_grad,
            self_out,
            self_rounded,
            gain_sums,
        ],
        [(0, 1, token_rows), (0, 2, 0), (0, 3, 0), (4, 5, 0), (6, None, 0)],
    )
    m1, o1, query_grad, key_grad, value_grad = hold(m1, o1, query_grad, key_grad, value_grad)
    r1 = swapped(o1, "c")
    both_grad = times_transpose(key_grad, self_key) + times_transpose(value_grad, self_value)
    d2, k3, r1, both_grad = hold(d2, k3, r1, both_grad)
    x2, y2 = sides_out(m2, d2)
    sent_back = lax.ppermute(both_grad[:token_rows].astype(bf16), "x", [(1, 0)])
    m1 = taken_in(m1, r1)
    d1 = corners_out(m1)
    partial_tokens = (
        gradient_self_mid + times_transpose(query_grad, self_query) + both_grad[token_rows:]
    )
    x2, y2, d1, partial_tokens = hold(x2, y2, d1, partial_tokens)
    x1, y1 = sides_out(m1, d1)
    k2 = z_most([m2[0], x2, y2], parts2)
    total_feed_out = plus(*k4)
    total_feed_in = plus(*k3)
    k2 = z_last(*k2, parts2)
    k2, x1, y1, total_feed_in, total_feed_out = hold(k2, x1, y1, total_feed_in, total_feed_out)
    k1 = z_most([m1[0], x1, y1], parts1)
    k1 = z_last(*k1, parts1)
    total_cross = plus(*k2)
    gradient_tokens = plus(partial_tokens, sent_back)
    total_self = plus(*k1)

    self_parts = [total_self[:, i * D : (i + 1) * D] for i in range(4)]
    cross_parts = [total_cross[:slots, i * D : (i + 1) * D] for i in range(4)]
    return (
        layer_out.astype(bf16),
        gradient_tokens,
        jnp.concatenate([total_cross[slots:, i * D : (i + 1) * D] for i in range(4)]),
        *self_parts,
        *cross_parts,
        total_feed_in,
        total_feed_out,
        total_self[:, 4 * D],
        total_self[:, 4 * D + 1],
        total_self[:, 4 * D + 2],
    )


def solution(mesh):
    fine = Mesh(mesh.devices.reshape(-1, 2, 2, 2), ALL)
    rows = P(ALL, None)
    return jax.shard_map(
        per_device,
        mesh=fine,
        in_specs=(rows,) * 12 + (P(ALL),) * 3 + (P(), P(), rows),
        out_specs=(rows,) * 13 + (P(ALL),) * 3,
        check_vma=False,
    )
```

```python
import math

import jax
import jax.numpy as jnp
from jax import lax
from jax.experimental import pallas as pl
from jax.experimental.pallas import tpu as pltpu
from jax.sharding import Mesh
from jax.sharding import PartitionSpec as P

D = 768
HEADS = 12
HEAD = 64
PAIR = 2 * HEAD
PAIRS = HEADS // 2
SCALE = HEAD ** (-0.5)

big_negative = -1e30
epsilon = 1e-05
bf16 = jnp.bfloat16
f32 = jnp.float32
ALL = ("z", "y", "c", "x")
NOTHING = pl.CostEstimate(flops=1, bytes_accessed=1, transcendentals=0)
VMEM = pl.BlockSpec(memory_space=pltpu.VMEM)
ANY = pl.BlockSpec(memory_space=pl.ANY)


def room_for(*arrays):
    held = 0
    for a in arrays:
        rows, width = a.shape[-2], a.shape[-1]
        held += math.prod(a.shape[:-2]) * pl.cdiv(rows, 16 if rows % 8 else 8) * (
            16 if rows % 8 else 8
        ) * pl.cdiv(width, 128) * 128 * a.dtype.itemsize
    return held + 2 * 2**20
SMEM = pl.BlockSpec(memory_space=pltpu.SMEM)


def matmul(left, right):
    return jnp.dot(left, right, preferred_element_type=f32)


def contract_rows(left, right):
    return lax.dot_general(left, right, (((0,), (0,)), ((), ())), preferred_element_type=f32)


def times_transpose(left, right):
    return lax.dot_general(left, right, (((1,), (1,)), ((), ())), preferred_element_type=f32)


def layer_norm(values, gain):
    centered = values - jnp.mean(values, axis=-1, keepdims=True)
    variance = jnp.mean(centered * centered, axis=-1, keepdims=True)
    return centered * lax.rsqrt(variance + epsilon) * gain


def exact_gelu(values):
    return jax.nn.gelu(values, approximate=False)


def table_entry(table, index):
    places = jnp.arange(table.shape[0], dtype=jnp.int32)
    return jnp.sum(jnp.where(places == index, table, 0))


def swapped(value, axis, by=1):
    size = lax.axis_size(axis)
    return lax.ppermute(value, axis, [(i, i ^ by) for i in range(size)])


def position():
    return jnp.stack([lax.axis_index(a).astype(jnp.int32) for a in ALL])


def packed(shards, group):
    blocks, first = [], 0
    for i, shard in enumerate(shards):
        size = shard.shape[0] // group
        for column in range(0, shard.shape[1], D):
            blocks.append((i, column, first, size))
            first += size
    n_in = len(shards)

    def kernel(*refs):
        out, sems = refs[-2:]
        copies = [
            pltpu.make_async_copy(
                refs[i].at[:, :, pl.ds(column, D)], out.at[pl.ds(at, size)], sems.at[n]
            )
            for n, (i, column, at, size) in enumerate(blocks)
        ]
        for copy in copies:
            copy.start()
        for copy in copies:
            copy.wait()

    return pl.pallas_call(
        kernel,
        out_shape=jax.ShapeDtypeStruct((first, group, D), shards[0].dtype),
        in_specs=[pl.BlockSpec(memory_space=pltpu.HBM)] * n_in,
        out_specs=VMEM,
        scratch_shapes=[pltpu.SemaphoreType.DMA((len(blocks),))],
        compiler_params=pltpu.CompilerParams(vmem_limit_bytes=60 * 2**20),
        cost_estimate=NOTHING,
        name="packed",
    )(*(s.reshape(s.shape[0] // group, group, s.shape[1]) for s in shards))


def in_order(pieces, places, where, cut=None):
    n_in = len(pieces)
    count, groups = len(places), pieces[0].shape[1]
    spans = [(0, groups)] if cut is None else [(0, cut), (cut, groups - cut)]

    def kernel(at, *refs):
        first = 0
        for i in range(n_in):
            for j in range(pieces[i].shape[0]):
                z = jnp.bitwise_xor(at[0], places[first])
                for o, (start, size) in enumerate(spans):
                    refs[n_in + o][z] = refs[i][j, start : start + size]
                first += 1

    outs = pl.pallas_call(
        kernel,
        out_shape=[
            jax.ShapeDtypeStruct((count, size) + pieces[0].shape[2:], pieces[0].dtype)
            for _, size in spans
        ],
        in_specs=[SMEM] + [VMEM] * n_in,
        out_specs=[VMEM] * len(spans),
        compiler_params=pltpu.CompilerParams(vmem_limit_bytes=room_for(*pieces)),
        cost_estimate=NOTHING,
        name="in_order",
    )(where, *pieces)
    return outs[0] if cut is None else outs


def half_of(own, over_x, over_y, corners, where):
    count, groups, *tail = own.shape
    tail = tuple(tail)
    half = count // 2

    def kernel(at, own_ref, x_ref, y_ref, first_ref, second_ref, out_ref):
        y, x = at[1], at[3]
        out_ref[:, y, x] = own_ref[...]
        out_ref[:, y, 1 - x] = x_ref[...]
        out_ref[:, 1 - y, x] = y_ref[...]
        out_ref[:half, 1 - y, 1 - x] = first_ref[...]
        out_ref[half:, 1 - y, 1 - x] = second_ref[...]

    return pl.pallas_call(
        kernel,
        out_shape=jax.ShapeDtypeStruct((count, 2, 2, groups) + tail, own.dtype),
        in_specs=[SMEM] + [VMEM] * 5,
        out_specs=VMEM,
        compiler_params=pltpu.CompilerParams(vmem_limit_bytes=room_for(*[own] * 4)),
        cost_estimate=NOTHING,
        name="half_of",
    )(where, own, over_x, over_y, *corners)


def assembled(own, other, cuts, where):
    count, _, _, groups, group, width = own.shape
    step = count if count <= 8 else 1

    def kernel(at, *refs):
        for dc in range(2):
            c = jnp.bitwise_xor(at[2], dc)
            for o, (first, size, blocks) in enumerate(cuts):
                for b in range(blocks):
                    here = first + b * size
                    columns = slice(b * width, (b + 1) * width)
                    for z in range(step):
                        for y in range(2):
                            block = refs[dc][z, y, :, here : here + size]
                            refs[2 + o][z, y, c, :, :, :, columns] = block

    outs = [
        jax.ShapeDtypeStruct((count, 2, 2, 2, size, group, blocks * width), own.dtype)
        for _, size, blocks in cuts
    ]
    if step == count:
        specs = dict(in_specs=[SMEM, VMEM, VMEM], out_specs=[VMEM] * len(outs))
    else:
        specs = dict(
            grid=(count,),
            in_specs=[SMEM]
            + [pl.BlockSpec((1, 2, 2, groups, group, width), lambda z: (z, 0, 0, 0, 0, 0))] * 2,
            out_specs=[
                pl.BlockSpec((1,) + out.shape[1:], lambda z: (z, 0, 0, 0, 0, 0, 0)) for out in outs
            ],
        )
    return pl.pallas_call(
        kernel,
        out_shape=outs,
        compiler_params=pltpu.CompilerParams(
            vmem_limit_bytes=room_for(*outs) if step == count else 32 * 2**20
        ),
        cost_estimate=NOTHING,
        name="assembled",
        **specs,
    )(where, own, other)


def window_of(own, other, first_group, rows, window, where):
    count, _, _, groups, group, width = own.shape
    groups = groups - first_group
    if count > 8 or group % 8:
        whole = assembled(own, other, [(first_group, groups, 1)], where)[0]
        whole = whole.reshape(8 * count, groups * group, width)[:, :rows]
        return lax.dynamic_slice(
            whole.reshape(8 * count * rows, width), (where[4], 0), (window, width)
        )
    held = window // rows

    def kernel(at, own_ref, other_ref, out_ref):
        first = at[4] // rows
        for i in range(held):
            device = first + i
            core = jnp.bitwise_xor(device // 2 % 2, at[2])
            z, y, x = device // 8, device // 4 % 2, device % 2
            for c, ref in ((0, own_ref), (1, other_ref)):

                @pl.when(core == c)
                def _(ref=ref):
                    out_ref[i] = ref[z, y, x, first_group:]

    out = jax.ShapeDtypeStruct((held, groups, group, width), own.dtype)
    out = pl.pallas_call(
        kernel,
        out_shape=out,
        in_specs=[SMEM, VMEM, VMEM],
        out_specs=VMEM,
        compiler_params=pltpu.CompilerParams(vmem_limit_bytes=room_for(own, out)),
        cost_estimate=NOTHING,
        name="window_of",
    )(where, own, other)
    return out.reshape(window, width)


def bounds_of(doc_lengths, seg_doc, where, rows, memory_rows, window, token_rows):
    def kernel(lengths, seg, at, place, cross, own):
        document = seg[(at[0] * 2 + at[1]) * 2 + at[2]]
        start, size = jnp.int32(0), jnp.int32(0)
        for d in range(doc_lengths.shape[0]):
            start = start + jnp.where(document > d, lengths[d], 0)
            size = size + jnp.where(document == d, lengths[d], 0)
        first = jnp.minimum(start // rows * rows, memory_rows - window)
        for i in range(4):
            place[i] = at[i]
        place[4] = first
        cross[0], cross[1] = start - first, start - first + size
        own[0] = jnp.where(at[3] == 0, token_rows, 0)
        own[1] = jnp.int32(2 * token_rows)

    return pl.pallas_call(
        kernel,
        out_shape=[jax.ShapeDtypeStruct((n,), jnp.int32) for n in (5, 2, 2)],
        in_specs=[SMEM] * 3,
        out_specs=[SMEM] * 3,
        cost_estimate=NOTHING,
        name="bounds_of",
    )(doc_lengths, seg_doc, where)


def selection(where, core, slots, order):
    depth = 4 * len(order) * slots
    row = lax.broadcasted_iota(jnp.int32, (depth, 2 * depth), 0)
    column = lax.broadcasted_iota(jnp.int32, (depth, 2 * depth), 1)
    s, row = row % slots, row // slots
    z, row = jnp.zeros_like(row), row
    if len(order) > 1:
        step = row % len(order)
        bits, reversed_step = len(order).bit_length() - 1, jnp.zeros_like(row)
        for i in range(bits):
            reversed_step = reversed_step + ((step >> i) & 1) * (len(order) >> (i + 1))
        z = jnp.bitwise_xor(where[0], reversed_step)
        row = row // len(order)
    y, x = jnp.bitwise_xor(where[1], row // 2), jnp.bitwise_xor(where[3], row % 2)
    c = jnp.bitwise_xor(where[2], core)
    return (column == (((z * 2 + y) * 2 + c) * 2 + x) * slots + s).astype(bf16)


def mine_shapes(rows, width):
    return [jax.ShapeDtypeStruct((rows, width), f32)] + [
        jax.ShapeDtypeStruct((n, width), bf16) for n in (rows, rows, rows // 2, rows - rows // 2)
    ]


def taken_in(mine, received):
    _, rows, width = mine.shape
    half = rows // 2

    def kernel(mine_ref, got_ref, own, for_x, for_y, first, second):
        def total(side, at):
            return mine_ref[side, at].astype(f32) + got_ref[side, at].astype(f32)

        for i, ref in enumerate((own, for_x, for_y)):
            ref[...] = total(i, pl.ds(0, rows)).astype(ref.dtype)
        first[...] = total(3, pl.ds(0, half)).astype(bf16)
        second[...] = total(3, pl.ds(half, rows - half)).astype(bf16)

    out_shape = mine_shapes(rows, width)
    return pl.pallas_call(
        kernel,
        out_shape=out_shape,
        in_specs=[VMEM] * 2,
        out_specs=[VMEM] * 5,
        compiler_params=pltpu.CompilerParams(vmem_limit_bytes=room_for(*out_shape)),
        cost_estimate=NOTHING,
        name="taken_in",
    )(mine, received)


def sums_in_parts(where, arrays, products, memory_rows):
    order = z_places()
    slots = D // (8 * len(order))
    width = D * sum(arrays[right].shape[1] // D for _, right, _ in products if right is not None)
    width += sum(arrays[left].shape[0] for left, right, _ in products if right is None)
    given, memory = [], []
    for core in range(2):
        pick = selection(where, core, slots, order)
        columns = []
        for left, right, first in products:
            turned = times_transpose(pick, arrays[left]).astype(bf16)
            if right is not None:
                turned = matmul(turned[:, first:], arrays[right]).astype(bf16)
            columns.append(turned)
        given.append(jnp.concatenate(columns, axis=1).reshape(4, -1, width))
    if not memory_rows:
        return given
    key_grad, value_grad, key_weight, value_weight = arrays[-4:]
    grad = times_transpose(key_grad, key_weight) + times_transpose(value_grad, value_weight)
    whole = lax.dynamic_update_slice(
        jnp.zeros((8 * len(order) * memory_rows, D), bf16), grad.astype(bf16), (where[4], 0)
    ).reshape(8 * len(order), memory_rows, D)
    for core in range(2):
        c = jnp.bitwise_xor(where[2], core)
        devices = []
        for r in order:
            for side in range(4):
                y, x = jnp.bitwise_xor(where[1], side // 2), jnp.bitwise_xor(where[3], side % 2)
                devices.append(((jnp.bitwise_xor(where[0], r) * 2 + y) * 2 + c) * 2 + x)
        slabs = whole[jnp.stack(devices)].reshape(len(devices), 2, memory_rows // 2, D)
        memory.append(jnp.transpose(slabs, (1, 0, 2, 3)).reshape(-1, D))
    return given + memory


def sums_out(where, arrays, products, memory_rows=0):
    order = z_places()
    slots = D // (8 * len(order))
    if slots % 8:
        return sums_in_parts(where, arrays, products, memory_rows)
    n_in = len(arrays)
    depth = slots * len(order)
    blocks, column = [], 0
    for left, right, first in products:
        wide = arrays[left].shape[0] if right is None else arrays[right].shape[1]
        for at in range(0, wide, D):
            size = min(D, wide - at)
            blocks.append((left, right, first, at, size, column))
            column += size
    width = column
    window = arrays[-4].shape[0] if memory_rows else 8
    half = memory_rows // 2

    def kernel(at, *refs):
        ins, outs, block_ref, grad_ref = refs[:n_in], refs[n_in:-2], refs[-2], refs[-1]

        def places(core):
            c = jnp.bitwise_xor(at[2], core)
            for side in range(4):
                y, x = jnp.bitwise_xor(at[1], side // 2), jnp.bitwise_xor(at[3], side % 2)
                for i, r in enumerate(order):
                    yield side, i, ((jnp.bitwise_xor(at[0], r) * 2 + y) * 2 + c) * 2 + x

        if memory_rows:
            key_grad, value_grad, key_weight, value_weight = ins[-4:]
            grad_ref[...] = times_transpose(key_grad[...], key_weight[...]) + times_transpose(
                value_grad[...], value_weight[...]
            )
            for core in (1, 0):
                for side, i, device in places(core):
                    start = device * memory_rows - at[4]
                    inside = (start >= 0) & (start + memory_rows <= window)
                    start = pl.multiple_of(jnp.where(inside, start, 0), memory_rows)
                    slab = grad_ref[pl.ds(start, memory_rows), :]
                    slab = jnp.where(inside, slab, jnp.zeros_like(slab)).astype(bf16)
                    for n in range(2):
                        first = ((n * len(order) + i) * 4 + side) * half
                        outs[2 + core][first : first + half, :] = slab[n * half : (n + 1) * half]
        for n, (left, right, first, from_, size, to) in enumerate(blocks):
            if right is None:
                block = ins[left][...].astype(f32).T
            else:
                block = contract_rows(ins[left][first:, :], ins[right][:, from_ : from_ + size])
            slot = n % 2
            block_ref[slot, :, :, :size] = block.reshape(8 * len(order), slots, size)
            for core in (1, 0):
                for side, i, device in places(core):
                    slab = block_ref[slot, device, :, :size].astype(bf16)
                    outs[core][side, i * slots : (i + 1) * slots, to : to + size] = slab

    out_shape = [jax.ShapeDtypeStruct((4, depth, width), bf16)] * 2
    if memory_rows:
        out_shape += [jax.ShapeDtypeStruct((len(order) * 4 * memory_rows, D), bf16)] * 2
    return pl.pallas_call(
        kernel,
        out_shape=out_shape,
        in_specs=[SMEM] + [VMEM] * n_in,
        out_specs=[VMEM] * len(out_shape),
        scratch_shapes=[
            pltpu.VMEM((2, 8 * len(order), slots, D), f32),
            pltpu.VMEM((window, D), f32),
        ],
        compiler_params=pltpu.CompilerParams(
            vmem_limit_bytes=room_for(*out_shape) + 2 * D * D * 4 + window * D * 4 + 3 * 2**20
        ),
        cost_estimate=NOTHING,
        name="sums_out",
    )(where, *arrays)


def hidden_sums_out(where, activated, grad):
    hidden = activated.shape[1]
    order = z_places()
    span = hidden // len(order)
    slots, fold = span // 8, hidden // D
    part = slots // fold
    if span % 128 or part % 8:
        given = []
        for core in range(2):
            pick = selection(where, core, slots, order)
            turned = times_transpose(pick, activated).astype(bf16)
            rows = matmul(turned, grad).astype(bf16).reshape(4, len(order), fold, part, D)
            given.append(jnp.transpose(rows, (0, 1, 3, 2, 4)).reshape(4, -1, hidden))
        return given

    def kernel(at, act_ref, grad_ref, mine, other, block_ref):
        for i, r in enumerate(order):
            first = pl.multiple_of(jnp.bitwise_xor(at[0], r) * span, 128)
            block = contract_rows(act_ref[:, pl.ds(first, span)], grad_ref[...])
            block_ref[i % 2] = block.reshape(8, slots, D)
            for core, ref in ((1, other), (0, mine)):
                c = jnp.bitwise_xor(at[2], core)
                for side in range(4):
                    y, x = jnp.bitwise_xor(at[1], side // 2), jnp.bitwise_xor(at[3], side % 2)
                    slab = block_ref[i % 2, (y * 2 + c) * 2 + x].astype(bf16)
                    for j in range(fold):
                        ref[side, i * part : (i + 1) * part, j * D : (j + 1) * D] = slab[
                            j * part : (j + 1) * part
                        ]

    shape = jax.ShapeDtypeStruct((4, len(order) * part, hidden), bf16)
    return pl.pallas_call(
        kernel,
        out_shape=[shape, shape],
        in_specs=[SMEM] + [VMEM] * 2,
        out_specs=[VMEM] * 2,
        scratch_shapes=[pltpu.VMEM((2, 8, slots, D), f32)],
        compiler_params=pltpu.CompilerParams(
            vmem_limit_bytes=room_for(shape, shape) + 8 * 2**20
        ),
        cost_estimate=NOTHING,
        name="hidden_sums_out",
    )(where, activated, grad)


def hold(*values):
    return lax.optimization_barrier(values)


def z_first(shard):
    return swapped(shard[None], "z", lax.axis_size("z") // 2)


def z_rest(shard, received):
    by = lax.axis_size("z") // 2
    pieces, places = [shard[None], received], [0, by]
    while by > 1:
        by //= 2
        received = swapped(jnp.concatenate(pieces), "z", by)
        pieces, places = pieces + [received], places + [p ^ by for p in places]
    return pieces


def z_places():
    by, places = lax.axis_size("z") // 2, [0]
    while by:
        places = places + [p ^ by for p in places]
        by //= 2
    return places


def corners_in(over_x, over_y):
    half = over_x.shape[0] // 2
    return swapped(over_x[:half], "y"), swapped(over_y[half:], "x")


def corners_out(mine):
    return swapped(mine[3], "y"), swapped(mine[4], "x")


def sides_out(mine, corners, following=None):
    _, for_x, for_y = mine[:3]
    rows, width = for_x.shape
    half = rows // 2
    (over_y, y_first), (over_x, x_first) = corners
    more = [] if following is None else [following[3], following[4]]
    tail = half if more else 0

    def kernel(x_ref, y_ref, over_y_ref, over_x_ref, *refs):
        x_out, y_out = refs[-2:]
        came = over_y_ref[y_first : y_first + half].astype(f32)
        x_out[:half] = (x_ref[:half].astype(f32) + came).astype(bf16)
        x_out[half:rows] = x_ref[half:]
        came = over_x_ref[x_first : x_first + half].astype(f32)
        y_out[:half] = y_ref[:half]
        y_out[half:rows] = (y_ref[half:].astype(f32) + came).astype(bf16)
        if tail:
            y_out[rows:] = refs[0][...]
            x_out[rows:] = refs[1][...]

    shape = jax.ShapeDtypeStruct((rows + tail, width), bf16)
    x_out, y_out = pl.pallas_call(
        kernel,
        out_shape=[shape, shape],
        in_specs=[VMEM] * (4 + len(more)),
        out_specs=[VMEM] * 2,
        compiler_params=pltpu.CompilerParams(vmem_limit_bytes=room_for(shape, shape)),
        cost_estimate=NOTHING,
        name="sides_out",
    )(for_x, for_y, over_y, over_x, *more)
    return swapped(x_out, "x"), swapped(y_out, "y")


def apart(corners):
    return [(c, 0) for c in corners]


def halved(terms, parts, begin=0):
    rows, width = sum(parts), terms[0].shape[1]
    n_in = len(terms)

    def kernel(*refs):
        start, out = begin, 0
        for part in parts:
            half = part // 2
            for first, ref in ((start, refs[n_in]), (start + half, refs[n_in + 1])):
                total = sum(r[pl.ds(first, half), :].astype(f32) for r in refs[:n_in])
                ref[pl.ds(out, half), :] = total.astype(ref.dtype)
            start, out = start + part, out + half

    return pl.pallas_call(
        kernel,
        out_shape=[
            jax.ShapeDtypeStruct((rows // 2, width), f32),
            jax.ShapeDtypeStruct((rows // 2, width), bf16),
        ],
        in_specs=[VMEM] * n_in,
        out_specs=[VMEM] * 2,
        compiler_params=pltpu.CompilerParams(vmem_limit_bytes=room_for(terms[0])),
        cost_estimate=NOTHING,
        name="halved",
    )(*terms)


def halved_pair(first, second):
    rows, width = first[0].shape
    half = rows // 2
    counts = (len(first), len(second))

    def kernel(*refs):
        keep, give = refs[-2:]
        start = 0
        for n, count in enumerate(counts):
            terms = refs[start : start + count]
            start += count
            for at, ref in ((0, keep), (half, give)):
                total = sum(r[pl.ds(at, half), :].astype(f32) for r in terms)
                ref[pl.ds(n * half, half), :] = total.astype(ref.dtype)

    shapes = [jax.ShapeDtypeStruct((rows, width), kind) for kind in (f32, bf16)]
    return pl.pallas_call(
        kernel,
        out_shape=shapes,
        in_specs=[VMEM] * sum(counts),
        out_specs=[VMEM] * 2,
        compiler_params=pltpu.CompilerParams(vmem_limit_bytes=room_for(*shapes)),
        cost_estimate=NOTHING,
        name="halved_pair",
    )(*first, *second)


def z_most(terms, parts, begin=0, pair=None):
    by = 1
    keep, give = halved(terms, parts, begin) if pair is None else halved_pair(terms, pair)
    received, parts = swapped(give, "z", by), [p // 2 for p in parts]
    while 2 * by < lax.axis_size("z") // 2:
        by *= 2
        keep, give = halved([keep, received], parts)
        received, parts = swapped(give, "z", by), [p // 2 for p in parts]
    return keep, received


def z_last(keep, received, parts):
    by = lax.axis_size("z") // 2
    keep, give = halved([keep, received], [p // by for p in parts])
    return keep, swapped(give, "z", by)


def memory_taken(keep, received, rows):
    def kernel(keep_ref, got_ref, *outs):
        half = rows // 2
        for n in range(2):
            for side in range(4):
                here = pl.ds((n * 4 + side) * half, half)
                total = keep_ref[here, :] + got_ref[here, :].astype(f32)
                ref = outs[side] if side < 3 else outs[3 + n]
                to = pl.ds(n * half if side < 3 else 0, half)
                ref[to, :] = total.astype(ref.dtype)

    out_shape = mine_shapes(rows, D)
    return pl.pallas_call(
        kernel,
        out_shape=out_shape,
        in_specs=[VMEM] * 2,
        out_specs=[VMEM] * 5,
        compiler_params=pltpu.CompilerParams(vmem_limit_bytes=room_for(*out_shape, keep)),
        cost_estimate=NOTHING,
        name="memory_taken",
    )(keep, received)


def plus(keep, received):
    return keep + received.astype(f32)


def lane_halves(block):
    lanes = lax.broadcasted_iota(jnp.int32, block.shape, 1)
    zero = jnp.zeros_like(block)
    return jnp.where(lanes < HEAD, block, zero), jnp.where(lanes < HEAD, zero, block)


def fill_bias(bias_ref, first, bounds, causal):
    shape = bias_ref.shape
    rows = shape[1] // 2
    keys = first + lax.broadcasted_iota(jnp.int32, shape, 0)
    allowed = (keys >= bounds[0]) & (keys < bounds[1])
    if causal:
        queries = lax.broadcasted_iota(jnp.int32, shape, 1)
        queries = jnp.where(queries < rows, queries, queries - rows)
        allowed = allowed & (keys - rows <= queries)
    bias_ref[...] = jnp.where(allowed, 0.0, big_negative)


def both_halves(block):
    return jnp.concatenate(lane_halves(block), axis=0)


def key_block(width):
    return next(width // n for n in range(1, width) if width % (16 * n) == 0 and width // n <= 1536)


def attend_kernel(causal, block, bounds, q_ref, k_ref, v_ref, out_ref, low_ref, lse_ref, bias_ref):
    rows, width = q_ref.shape[0], k_ref.shape[0]
    if width == block:
        fill_bias(bias_ref, 0, bounds, causal)

    def pair(h, carried):
        lanes = pl.ds(pl.multiple_of(h * PAIR, PAIR), PAIR)
        both = both_halves(q_ref[:, lanes] * SCALE)

        def step(i, state):
            first = pl.multiple_of(i * block, block)
            if width > block:
                fill_bias(bias_ref, first, bounds, causal)
            keys, values = k_ref[pl.ds(first, block), lanes], v_ref[pl.ds(first, block), lanes]
            scores = times_transpose(keys, both) + bias_ref[...]
            top = jnp.max(scores, axis=0, keepdims=True)
            if state is not None:
                top = jnp.maximum(state[0], top)
            weights = jnp.exp(scores - top)
            total = jnp.sum(weights, axis=0, keepdims=True)
            summed = contract_rows(values, weights.astype(bf16))
            if state is not None:
                factor = jnp.exp(state[0] - top)
                total, summed = total + state[1] * factor, summed + state[2] * factor
            return top, total, summed

        state = step(0, None)
        if width > block:
            state = lax.fori_loop(1, width // block, step, state)
        top, total, summed = state
        out = summed / total
        out = jnp.concatenate([out[:HEAD, :rows], out[HEAD:, rows:]], axis=0).T
        out_ref[:, lanes] = out
        low_ref[:, lanes] = out.astype(bf16)
        lse_ref[h] = top + jnp.log(total)
        return carried

    lax.fori_loop(0, PAIRS, pair, 0, unroll=2)


def attend(queries, keys, values, bounds, causal):
    rows, width = queries.shape[0], keys.shape[0]
    block = key_block(width)
    out_shape = [
        jax.ShapeDtypeStruct((rows, D), f32),
        jax.ShapeDtypeStruct((rows, D), bf16),
        jax.ShapeDtypeStruct((PAIRS, 1, 2 * rows), f32),
    ]
    return pl.pallas_call(
        lambda *refs: attend_kernel(causal, block, *refs),
        scratch_shapes=[pltpu.VMEM((block, 2 * rows), f32)],
        in_specs=[SMEM] + [VMEM] * 3,
        out_specs=[VMEM] * 3,
        out_shape=out_shape,
        compiler_params=pltpu.CompilerParams(
            vmem_limit_bytes=16 * 2**20 if width <= 2048 else 48 * 2**20
        ),
        cost_estimate=NOTHING,
        name="attend_self" if causal else "attend_cross",
    )(bounds, queries, keys, values)


def attend_back_kernel(
    causal,
    block,
    bounds,
    q_ref,
    k_ref,
    v_ref,
    o_ref,
    g_ref,
    lse_ref,
    dq_ref,
    dk_ref,
    dv_ref,
    bias_ref,
):
    rows, width = q_ref.shape[0], k_ref.shape[0]
    if width == block:
        fill_bias(bias_ref, 0, bounds, causal)

    def pair(h, carried):
        lanes = pl.ds(pl.multiple_of(h * PAIR, PAIR), PAIR)
        queries = both_halves(q_ref[:, lanes] * SCALE)
        grads = both_halves(g_ref[:, lanes])
        products = (g_ref[:, lanes].astype(f32) * o_ref[:, lanes]).T
        delta = jnp.concatenate(
            [
                jnp.sum(products[:HEAD], axis=0, keepdims=True),
                jnp.sum(products[HEAD:], axis=0, keepdims=True),
            ],
            axis=1,
        )

        def step(i, query_grad):
            first = pl.multiple_of(i * block, block)
            if width > block:
                fill_bias(bias_ref, first, bounds, causal)
            here = pl.ds(first, block)
            keys, values = k_ref[here, lanes], v_ref[here, lanes]
            scores = times_transpose(keys, queries) + bias_ref[...]
            probs = jnp.exp(scores - lse_ref[h])
            dv_ref[here, lanes] = matmul(probs.astype(bf16), grads).astype(bf16)
            slopes = times_transpose(values, grads)
            score_grad = (probs * (slopes - delta)).astype(bf16)
            dk_ref[here, lanes] = matmul(score_grad, queries).astype(bf16)
            part = contract_rows(keys, score_grad)
            return part if query_grad is None else query_grad + part

        grad = step(0, None)
        if width > block:
            grad = lax.fori_loop(1, width // block, step, grad)
        grad = jnp.concatenate([grad[:HEAD, :rows], grad[HEAD:, rows:]], axis=0)
        dq_ref[:, lanes] = (grad * SCALE).T.astype(bf16)
        return carried

    lax.fori_loop(0, PAIRS, pair, 0, unroll=2)


def attend_back(queries, keys, values, out, grad, lse, bounds, causal):
    rows, width = queries.shape[0], keys.shape[0]
    block = key_block(width)
    out_shape = [
        jax.ShapeDtypeStruct((rows, D), bf16),
        jax.ShapeDtypeStruct((width, D), bf16),
        jax.ShapeDtypeStruct((width, D), bf16),
    ]
    return pl.pallas_call(
        lambda *refs: attend_back_kernel(causal, block, *refs),
        scratch_shapes=[pltpu.VMEM((block, 2 * rows), f32)],
        in_specs=[SMEM] + [VMEM] * 6,
        out_specs=[VMEM] * 3,
        out_shape=out_shape,
        compiler_params=pltpu.CompilerParams(
            vmem_limit_bytes=26 * 2**20 if width <= 2048 else 62 * 2**20
        ),
        cost_estimate=NOTHING,
        name="attend_back_self" if causal else "attend_back_cross",
    )(bounds, queries, keys, values, out, grad, lse)


def activate(values, weight):
    rows, hidden = values.shape[0], weight.shape[1]
    step = min(hidden, D)

    def kernel(values_ref, weight_ref, out_ref, slope_ref):
        for at in range(0, hidden, step):
            inner = matmul(values_ref[...], weight_ref[:, at : at + step])
            below = 0.5 * (1.0 + lax.erf(inner * (0.5**0.5)))
            out_ref[:, at : at + step] = (inner * below).astype(bf16)
            bell = jnp.exp(-0.5 * inner * inner) * (1.0 / math.sqrt(2.0 * math.pi))
            slope_ref[:, at : at + step] = below + inner * bell

    return pl.pallas_call(
        kernel,
        out_shape=[
            jax.ShapeDtypeStruct((rows, hidden), bf16),
            jax.ShapeDtypeStruct((rows, hidden), f32),
        ],
        in_specs=[VMEM] * 2,
        out_specs=[VMEM] * 2,
        compiler_params=pltpu.CompilerParams(vmem_limit_bytes=8 * 2**20),
        cost_estimate=NOTHING,
        name="activate",
    )(values, weight)


def whole_kernel(kernel, name, out_shape, *arrays, spare=2):
    return pl.pallas_call(
        kernel,
        out_shape=out_shape,
        in_specs=[VMEM] * len(arrays),
        out_specs=[VMEM] * len(out_shape),
        compiler_params=pltpu.CompilerParams(
            vmem_limit_bytes=min(room_for(*out_shape) + spare * 2**20, 62 * 2**20)
        ),
        cost_estimate=NOTHING,
        name=name,
    )(*arrays)


def like(rows, columns, dtype):
    return jax.ShapeDtypeStruct((rows, columns), dtype)


def row_mean(values):
    return jnp.sum(values, axis=-1, keepdims=True) * (1.0 / values.shape[-1])


def normed(values):
    centered = values - row_mean(values)
    inverse = lax.rsqrt(row_mean(centered * centered) + epsilon)
    return centered * inverse, inverse


def norm_back(grad, unit, inverse, gain):
    scaled = grad * gain
    inner = scaled - row_mean(scaled) - unit * row_mean(scaled * unit)
    return inner * inverse, jnp.sum(grad * unit, axis=0, keepdims=True)


def add_and_norm(base, out, weight, gain):
    rows = base.shape[0]

    def kernel(b_ref, o_ref, w_ref, g_ref, hidden_ref, low_ref, unit_ref, inverse_ref):
        mid = b_ref[...].astype(f32) + matmul(o_ref[...], w_ref[...])
        unit, inverse = normed(mid)
        hidden = unit * g_ref[...]
        hidden_ref[...], low_ref[...] = hidden, hidden.astype(bf16)
        unit_ref[...], inverse_ref[...] = unit, inverse

    out_shape = [like(rows, D, f32), like(rows, D, bf16), like(rows, D, f32), like(rows, 1, f32)]
    return whole_kernel(kernel, "add_and_norm", out_shape, base, out, weight, gain)


def self_turn(above, grad, weight, unit, inverse, gain, out_weight, gain_cross, gain_feed):
    rows = above.shape[0]

    def kernel(a_ref, d_ref, w_ref, u_ref, i_ref, g_ref, o_ref, c_ref, f_ref, *outs):
        grad_ref, low_ref, gains_ref, out_ref = outs
        total = a_ref[...] + times_transpose(d_ref[...], w_ref[...])
        grad, gain_grad = norm_back(total, u_ref[...], i_ref[...], g_ref[...])
        low = grad.astype(bf16)
        grad_ref[...], low_ref[...] = grad, low
        rest = jnp.zeros((125, D), f32)
        gains = jnp.concatenate([gain_grad, c_ref[...], f_ref[...], rest], axis=0)
        gains_ref[...] = gains.astype(bf16)
        out_ref[...] = times_transpose(low, o_ref[...]).astype(bf16)

    out_shape = [like(rows, D, f32), like(rows, D, bf16), like(128, D, bf16), like(rows, D, bf16)]
    return whole_kernel(
        kernel,
        "self_turn",
        out_shape,
        above,
        grad,
        weight,
        unit,
        inverse,
        gain,
        out_weight,
        gain_cross,
        gain_feed,
    )


def padded(shard, rows):
    return jnp.pad(shard, ((0, rows - shard.shape[0]), (0, 0)))


def grouped(shard, group):
    return shard.reshape(shard.shape[0] // group, group, shard.shape[1])


def per_device(
    tokens,
    memory,
    self_query,
    self_key,
    self_value,
    self_output,
    cross_query,
    cross_key,
    cross_value,
    cross_output,
    feed_in,
    feed_out,
    gain_self,
    gain_cross,
    gain_feed,
    doc_lengths,
    seg_doc,
    cotangent,
):
    where = position()
    token_rows = tokens.shape[0]
    count = lax.axis_size("z") * 8
    slots = self_query.shape[0]
    memory_rows = memory.shape[0]
    group = math.gcd(8, slots) if slots % 4 == 0 else slots
    memory_groups = pl.cdiv(memory_rows, group)
    gain_groups = pl.cdiv(3, group)
    gain_rows = gain_groups * group
    slot_groups = slots // group

    gains = jnp.pad(jnp.stack([gain_self, gain_cross, gain_feed]), ((0, gain_rows - 3), (0, D - slots)))
    hidden = feed_in.shape[1]
    places = z_places()
    cuts1 = [(i * slot_groups, slot_groups, 1) for i in range(4)]
    cuts1.append((4 * slot_groups, gain_groups, 1))
    cuts2 = [(i * slot_groups, slot_groups, 1) for i in range(3)]
    cuts3 = [(0, slot_groups, 1), (slot_groups, slot_groups, hidden // D)]
    cuts4 = [(0, feed_out.shape[0] // group, 1)]
    s1 = packed([self_query, self_key, self_value, self_output, gains], group)
    s2 = packed(
        [cross_query, cross_key, cross_value, padded(memory, memory_groups * group)], group
    )
    s3 = packed([cross_output, feed_in], group)
    s4 = grouped(feed_out, group)

    window = count * memory_rows // 2 + memory_rows
    where_window, cross_bounds, self_bounds = bounds_of(
        doc_lengths, seg_doc, where, memory_rows, count * memory_rows, window, token_rows
    )
    a1 = z_first(s1)
    earlier = lax.ppermute(tokens, "x", [(0, 1)])
    a1, s2, s3, s4 = hold(a1, s2, s3, s4)
    b1 = z_rest(s1, a1)
    a2 = z_first(s2)
    own1 = in_order(b1, places, where)
    own1, a2, earlier, s3, s4 = hold(own1, a2, earlier, s3, s4)
    x1, y1 = swapped(own1, "x"), swapped(own1, "y")
    b2 = z_rest(s2, a2)
    a3 = z_first(s3)
    both_tokens = jnp.concatenate([earlier, tokens], axis=0)
    own2 = in_order(b2, places, where)
    own2, x1, y1, own1, both_tokens, s4 = hold(own2, x1, y1, own1, both_tokens, s4)

    d1 = corners_in(x1, y1)
    x2, y2 = swapped(own2, "x"), swapped(own2, "y")
    b3 = z_rest(s3, a3)
    own3 = in_order(b3, places, where)
    a4 = z_first(s4)
    d1, x2, y2, own2, own3, a4, where_window, cross_bounds, self_bounds = hold(
        d1, x2, y2, own2, own3, a4, where_window, cross_bounds, self_bounds
    )

    d2 = corners_in(x2, y2)
    x3, y3 = swapped(own3, "x"), swapped(own3, "y")
    half1 = half_of(own1, x1, y1, d1, where)
    c1 = swapped(half1, "c")
    wholes = assembled(half1, c1, cuts1, where)
    self_query, self_key, self_value, self_output = (w.reshape(D, D) for w in wholes[:4])
    b4 = z_rest(s4, a4)
    gains = wholes[4].reshape(count, gain_rows, D)[:, :3, :slots]
    gain_self, gain_cross, gain_feed = (
        gains[:, i].reshape(D).astype(f32) for i in range(3)
    )
    queries = matmul(tokens, self_query).astype(bf16)
    keys = matmul(both_tokens, self_key).astype(bf16)
    values = matmul(both_tokens, self_value).astype(bf16)
    self_full, self_out, self_lse = attend(queries, keys, values, self_bounds, True)
    b4, self_out = hold(b4, self_out)
    own4 = in_order(b4, places, where)
    hidden_self, hidden_self_low, unit_self, inverse_self = add_and_norm(
        tokens, self_out, self_output, gain_self.reshape(1, D)
    )
    d2, x3, y3, own3, own4, hidden_self, hidden_self_low = hold(
        d2, x3, y3, own3, own4, hidden_self, hidden_self_low
    )

    d3 = corners_in(x3, y3)
    x4, y4 = swapped(own4, "x"), swapped(own4, "y")
    half2 = half_of(own2, x2, y2, d2, where)
    c2 = swapped(half2, "c")
    wholes = assembled(half2, c2, cuts2, where)
    cross_query, cross_key, cross_value = (w.reshape(D, D) for w in wholes)
    memory_here = window_of(half2, c2, 3 * slot_groups, memory_rows, window, where_window)
    cross_queries = matmul(hidden_self_low, cross_query).astype(bf16)
    memory_keys = matmul(memory_here, cross_key).astype(bf16)
    memory_values = matmul(memory_here, cross_value).astype(bf16)
    cross_full, cross_out, cross_lse = attend(
        cross_queries, memory_keys, memory_values, cross_bounds, False
    )
    d3, x4, y4, own4, cross_out = hold(d3, x4, y4, own4, cross_out)

    d4 = corners_in(x4, y4)
    half3 = half_of(own3, x3, y3, d3, where)
    c3 = swapped(half3, "c")
    wholes = assembled(half3, c3, cuts3, where)
    cross_output, feed_in = (w.reshape(D, w.shape[-1]) for w in wholes)
    mid_cross = hidden_self + matmul(cross_out, cross_output)
    hidden_cross, back_cross = jax.vjp(layer_norm, mid_cross, gain_cross)
    hidden_cross_low = hidden_cross.astype(bf16)
    activated, slope = activate(hidden_cross_low, feed_in)
    d4, activated, own4 = hold(d4, activated, own4)
    half4 = half_of(own4, x4, y4, d4, where)
    c4 = swapped(half4, "c")
    wholes = assembled(half4, c4, cuts4, where)
    feed_out = wholes[0].reshape(hidden, D)
    mid_feed = hidden_cross + matmul(activated, feed_out)
    layer_out, back_feed = jax.vjp(layer_norm, mid_feed, gain_feed)
    gradient_feed_mid, gain_feed_sum = back_feed(cotangent.astype(f32))
    feed_rounded = gradient_feed_mid.astype(bf16)
    m4, o4 = hidden_sums_out(where, activated, feed_rounded)
    m4, o4, feed_rounded = hold(m4, o4, feed_rounded)
    r4 = swapped(o4, "c")
    gradient_inner = (times_transpose(feed_rounded, feed_out) * slope).astype(bf16)
    m3, o3 = sums_out(where, [hidden_cross_low, gradient_inner], [(0, 1, 0)])
    r4, m3, o3, gradient_inner = hold(r4, m3, o3, gradient_inner)
    m4 = taken_in(m4, r4)
    d4 = corners_out(m4)
    r3 = swapped(o3, "c")
    gradient_hidden_cross = gradient_feed_mid + times_transpose(gradient_inner, feed_in)
    gradient_cross_mid, gain_cross_sum = back_cross(gradient_hidden_cross)
    cross_rounded = gradient_cross_mid.astype(bf16)

    outgoing = times_transpose(cross_rounded, cross_output).astype(bf16)
    r3, d4, outgoing, cross_rounded = hold(r3, d4, outgoing, cross_rounded)
    m3 = taken_in(m3, r3)
    x4, y4 = sides_out(m4, apart(d4), m3)
    cross_query_grad, memory_key_grad, memory_value_grad = attend_back(
        cross_queries,
        memory_keys,
        memory_values,
        cross_full,
        outgoing,
        cross_lse,
        cross_bounds,
        False,
    )
    gradient_self_mid, self_rounded, gain_sums, self_outgoing = self_turn(
        gradient_cross_mid,
        cross_query_grad,
        cross_query,
        unit_self,
        inverse_self,
        gain_self.reshape(1, D),
        self_output,
        gain_cross_sum.reshape(1, D),
        gain_feed_sum.reshape(1, D),
    )

    query_grad, key_grad, value_grad = attend_back(
        queries, keys, values, self_full, self_outgoing, self_lse, self_bounds, True
    )
    m1, o1 = sums_out(
        where,
        [
            both_tokens,
            query_grad,
            key_grad,
            value_grad,
            self_out,
            self_rounded,
            gain_sums,
        ],
        [(0, 1, token_rows), (0, 2, 0), (0, 3, 0), (4, 5, 0), (6, None, 0)],
    )
    x4, y4, m1, o1, cross_query_grad, query_grad, key_grad, value_grad = hold(
        x4, y4, m1, o1, cross_query_grad, query_grad, key_grad, value_grad
    )
    x3, y3 = sides_out(m3, [(y4, D // 8), (x4, D // 8)])
    parts1, parts5 = [D // 8], [count * memory_rows // 4] * 2
    k4 = z_most([m4[0], x4, y4], parts1)
    r1 = swapped(o1, "c")
    m2, o2, m5, o5 = sums_out(
        where_window,
        [
            hidden_self_low,
            cross_query_grad,
            memory_here,
            cross_out,
            cross_rounded,
            gain_sums,
            memory_key_grad,
            memory_value_grad,
            cross_key,
            cross_value,
        ],
        [(0, 1, 0), (2, 6, 0), (2, 7, 0), (3, 4, 0), (5, None, 0)],
        memory_rows,
    )
    x3, y3, k4, m1, r1, m2, o2, m5, o5, query_grad, key_grad, value_grad = hold(
        x3, y3, k4, m1, r1, m2, o2, m5, o5, query_grad, key_grad, value_grad
    )
    m1 = taken_in(m1, r1)
    d1 = corners_out(m1)
    r2, r5 = swapped(o2, "c"), swapped(o5, "c")
    k3 = z_most([m3[0], x3, y3], parts1)
    both_grad = times_transpose(key_grad, self_key) + times_transpose(value_grad, self_value)
    to_earlier = both_grad[:token_rows].astype(bf16)
    partial_tokens = (
        gradient_self_mid + times_transpose(query_grad, self_query) + both_grad[token_rows:]
    )
    d1, m1, r2, r5, k3, k4, m2, m5, partial_tokens, to_earlier = hold(
        d1, m1, r2, r5, k3, k4, m2, m5, partial_tokens, to_earlier
    )
    m2 = taken_in(m2, r2)
    x1, y1 = sides_out(m1, apart(d1), m2)
    k5 = z_most([m5, r5], parts5)
    keep, give = halved_pair(list(k4), list(k3))
    k3 = keep, swapped(give, "z", lax.axis_size("z") // 2)
    x1, y1, k3, k5 = hold(x1, y1, k3, k5)
    x2, y2 = sides_out(m2, [(y1, D // 8), (x1, D // 8)])
    k1 = z_most([m1[0], x1, y1], parts1)
    k5 = z_last(*k5, parts5)
    total_feed = plus(*k3)
    x2, y2, k1, k5, to_earlier, total_feed = hold(x2, y2, k1, k5, to_earlier, total_feed)
    k2 = z_most([m2[0], x2, y2], parts1)
    k1 = z_last(*k1, parts1)
    sent_back = lax.ppermute(to_earlier, "x", [(1, 0)])
    m5 = memory_taken(*k5, memory_rows)
    d5 = corners_out(m5)
    k2, d5, k1 = hold(k2, d5, k1)
    k2 = z_last(*k2, parts1)
    x5, y5 = sides_out(m5, apart(d5))
    total_self = plus(*k1)
    gradient_memory = plus(plus(m5[0], x5), y5)
    gradient_tokens = plus(partial_tokens, sent_back)
    total_cross = plus(*k2)

    self_parts = [total_self[:, i * D : (i + 1) * D] for i in range(4)]
    cross_parts = [total_cross[:, i * D : (i + 1) * D] for i in range(4)]
    return (
        layer_out.astype(bf16),
        gradient_tokens,
        gradient_memory,
        *self_parts,
        *cross_parts,
        total_feed[slots:],
        jnp.concatenate([total_feed[:slots, i * D : (i + 1) * D] for i in range(hidden // D)]),
        total_self[:, 4 * D],
        total_self[:, 4 * D + 1],
        total_self[:, 4 * D + 2],
    )


def solution(mesh):
    fine = Mesh(mesh.devices.reshape(-1, 2, 2, 2), ALL)
    rows = P(ALL, None)
    return jax.shard_map(
        per_device,
        mesh=fine,
        in_specs=(rows,) * 12 + (P(ALL),) * 3 + (P(), P(), rows),
        out_specs=(rows,) * 13 + (P(ALL),) * 3,
        check_vma=False,
    )
```

```python
import math

import jax
import jax.numpy as jnp
from jax import lax
from jax.experimental import pallas as pl
from jax.experimental.pallas import tpu as pltpu
from jax.sharding import Mesh
from jax.sharding import PartitionSpec as P

D = 768
HEADS = 12
HEAD = 64
PAIR = 2 * HEAD
PAIRS = HEADS // 2
SCALE = HEAD ** (-0.5)

big_negative = -1e30
epsilon = 1e-05
bf16 = jnp.bfloat16
f32 = jnp.float32
ALL = ("z", "y", "c", "x")
NOTHING = pl.CostEstimate(flops=1, bytes_accessed=1, transcendentals=0)
VMEM = pl.BlockSpec(memory_space=pltpu.VMEM)
ANY = pl.BlockSpec(memory_space=pl.ANY)


def room_for(*arrays):
    held = 0
    for a in arrays:
        rows, width = a.shape[-2], a.shape[-1]
        held += math.prod(a.shape[:-2]) * pl.cdiv(rows, 16 if rows % 8 else 8) * (
            16 if rows % 8 else 8
        ) * pl.cdiv(width, 128) * 128 * a.dtype.itemsize
    return held + 2 * 2**20
SMEM = pl.BlockSpec(memory_space=pltpu.SMEM)


def matmul(left, right):
    return jnp.dot(left, right, preferred_element_type=f32)


def contract_rows(left, right):
    return lax.dot_general(left, right, (((0,), (0,)), ((), ())), preferred_element_type=f32)


def times_transpose(left, right):
    return lax.dot_general(left, right, (((1,), (1,)), ((), ())), preferred_element_type=f32)


def layer_norm(values, gain):
    centered = values - jnp.mean(values, axis=-1, keepdims=True)
    variance = jnp.mean(centered * centered, axis=-1, keepdims=True)
    return centered * lax.rsqrt(variance + epsilon) * gain


def exact_gelu(values):
    return jax.nn.gelu(values, approximate=False)


def table_entry(table, index):
    places = jnp.arange(table.shape[0], dtype=jnp.int32)
    return jnp.sum(jnp.where(places == index, table, 0))


def swapped(value, axis, by=1):
    size = lax.axis_size(axis)
    return lax.ppermute(value, axis, [(i, i ^ by) for i in range(size)])


def position():
    return jnp.stack([lax.axis_index(a).astype(jnp.int32) for a in ALL])


def packed(shards, group):
    blocks, first = [], 0
    for i, shard in enumerate(shards):
        size = shard.shape[0] // group
        for column in range(0, shard.shape[1], D):
            blocks.append((i, column, first, size))
            first += size
    n_in = len(shards)

    def kernel(*refs):
        out, sems = refs[-2:]
        copies = [
            pltpu.make_async_copy(
                refs[i].at[:, :, pl.ds(column, D)], out.at[pl.ds(at, size)], sems.at[n]
            )
            for n, (i, column, at, size) in enumerate(blocks)
        ]
        for copy in copies:
            copy.start()
        for copy in copies:
            copy.wait()

    return pl.pallas_call(
        kernel,
        out_shape=jax.ShapeDtypeStruct((first, group, D), shards[0].dtype),
        in_specs=[pl.BlockSpec(memory_space=pltpu.HBM)] * n_in,
        out_specs=VMEM,
        scratch_shapes=[pltpu.SemaphoreType.DMA((len(blocks),))],
        compiler_params=pltpu.CompilerParams(vmem_limit_bytes=60 * 2**20),
        cost_estimate=NOTHING,
        name="packed",
    )(*(s.reshape(s.shape[0] // group, group, s.shape[1]) for s in shards))


def in_order(pieces, places, where, cut=None):
    n_in = len(pieces)
    count, groups = len(places), pieces[0].shape[1]
    spans = [(0, groups)] if cut is None else [(0, cut), (cut, groups - cut)]

    def kernel(at, *refs):
        first = 0
        for i in range(n_in):
            for j in range(pieces[i].shape[0]):
                z = jnp.bitwise_xor(at[0], places[first])
                for o, (start, size) in enumerate(spans):
                    refs[n_in + o][z] = refs[i][j, start : start + size]
                first += 1

    outs = pl.pallas_call(
        kernel,
        out_shape=[
            jax.ShapeDtypeStruct((count, size) + pieces[0].shape[2:], pieces[0].dtype)
            for _, size in spans
        ],
        in_specs=[SMEM] + [VMEM] * n_in,
        out_specs=[VMEM] * len(spans),
        compiler_params=pltpu.CompilerParams(vmem_limit_bytes=room_for(*pieces)),
        cost_estimate=NOTHING,
        name="in_order",
    )(where, *pieces)
    return outs[0] if cut is None else outs


def half_of(own, over_x, over_y, corners, where):
    count, groups, *tail = own.shape
    tail = tuple(tail)
    half = count // 2

    def kernel(at, own_ref, x_ref, y_ref, first_ref, second_ref, out_ref):
        y, x = at[1], at[3]
        out_ref[:, y, x] = own_ref[...]
        out_ref[:, y, 1 - x] = x_ref[...]
        out_ref[:, 1 - y, x] = y_ref[...]
        out_ref[:half, 1 - y, 1 - x] = first_ref[...]
        out_ref[half:, 1 - y, 1 - x] = second_ref[...]

    return pl.pallas_call(
        kernel,
        out_shape=jax.ShapeDtypeStruct((count, 2, 2, groups) + tail, own.dtype),
        in_specs=[SMEM] + [VMEM] * 5,
        out_specs=VMEM,
        compiler_params=pltpu.CompilerParams(vmem_limit_bytes=room_for(*[own] * 4)),
        cost_estimate=NOTHING,
        name="half_of",
    )(where, own, over_x, over_y, *corners)


def assembled(own, other, cuts, where):
    count, _, _, groups, group, width = own.shape
    step = count if count <= 8 else 1

    def kernel(at, *refs):
        for dc in range(2):
            c = jnp.bitwise_xor(at[2], dc)
            for o, (first, size, blocks) in enumerate(cuts):
                for b in range(blocks):
                    here = first + b * size
                    columns = slice(b * width, (b + 1) * width)
                    for z in range(step):
                        for y in range(2):
                            block = refs[dc][z, y, :, here : here + size]
                            refs[2 + o][z, y, c, :, :, :, columns] = block

    outs = [
        jax.ShapeDtypeStruct((count, 2, 2, 2, size, group, blocks * width), own.dtype)
        for _, size, blocks in cuts
    ]
    if step == count:
        specs = dict(in_specs=[SMEM, VMEM, VMEM], out_specs=[VMEM] * len(outs))
    else:
        specs = dict(
            grid=(count,),
            in_specs=[SMEM]
            + [pl.BlockSpec((1, 2, 2, groups, group, width), lambda z: (z, 0, 0, 0, 0, 0))] * 2,
            out_specs=[
                pl.BlockSpec((1,) + out.shape[1:], lambda z: (z, 0, 0, 0, 0, 0, 0)) for out in outs
            ],
        )
    return pl.pallas_call(
        kernel,
        out_shape=outs,
        compiler_params=pltpu.CompilerParams(
            vmem_limit_bytes=room_for(*outs) if step == count else 32 * 2**20
        ),
        cost_estimate=NOTHING,
        name="assembled",
        **specs,
    )(where, own, other)


def half_by_steps(own, over_x, over_y, corner, steps, where):
    lists = (own, over_x, over_y, corner)
    arrays = [a for part in lists for a in part]
    count, tail = len(steps), own[0].shape[1:]

    def kernel(at, *refs):
        y, x = at[1], at[3]
        spots = ((y, x), (y, 1 - x), (1 - y, x), (1 - y, 1 - x))
        ref = iter(refs)
        for part, spot in zip(lists, spots):
            n = 0
            for a in part:
                source = next(ref)
                for k in range(a.shape[0]):
                    refs[-1][jnp.bitwise_xor(at[0], steps[n]), spot[0], spot[1]] = source[k]
                    n += 1

    out = jax.ShapeDtypeStruct((count, 2, 2) + tail, own[0].dtype)
    return pl.pallas_call(
        kernel,
        out_shape=out,
        in_specs=[SMEM] + [VMEM] * len(arrays),
        out_specs=VMEM,
        compiler_params=pltpu.CompilerParams(vmem_limit_bytes=room_for(out) + 2**20),
        cost_estimate=NOTHING,
        name="half_by_steps",
    )(where, *arrays)


def window_of(own, other, first_group, rows, window, where):
    count, _, _, groups, group, width = own.shape
    groups = groups - first_group
    if count > 8 or group % 8:
        whole = assembled(own, other, [(first_group, groups, 1)], where)[0]
        whole = whole.reshape(8 * count, groups * group, width)[:, :rows]
        return lax.dynamic_slice(
            whole.reshape(8 * count * rows, width), (where[4], 0), (window, width)
        )
    held = window // rows

    def kernel(at, own_ref, other_ref, out_ref):
        first = at[4] // rows
        for i in range(held):
            device = first + i
            core = jnp.bitwise_xor(device // 2 % 2, at[2])
            z, y, x = device // 8, device // 4 % 2, device % 2
            for c, ref in ((0, own_ref), (1, other_ref)):

                @pl.when(core == c)
                def _(ref=ref):
                    out_ref[i] = ref[z, y, x, first_group:]

    out = jax.ShapeDtypeStruct((held, groups, group, width), own.dtype)
    out = pl.pallas_call(
        kernel,
        out_shape=out,
        in_specs=[SMEM, VMEM, VMEM],
        out_specs=VMEM,
        compiler_params=pltpu.CompilerParams(vmem_limit_bytes=room_for(own, out)),
        cost_estimate=NOTHING,
        name="window_of",
    )(where, own, other)
    return out.reshape(window, width)


def bounds_of(doc_lengths, seg_doc, where, rows, memory_rows, window, token_rows):
    def kernel(lengths, seg, at, place, cross, own):
        document = seg[(at[0] * 2 + at[1]) * 2 + at[2]]
        start, size = jnp.int32(0), jnp.int32(0)
        for d in range(doc_lengths.shape[0]):
            start = start + jnp.where(document > d, lengths[d], 0)
            size = size + jnp.where(document == d, lengths[d], 0)
        first = jnp.minimum(start // rows * rows, memory_rows - window)
        for i in range(4):
            place[i] = at[i]
        place[4] = first
        cross[0], cross[1] = start - first, start - first + size
        own[0] = jnp.where(at[3] == 0, token_rows, 0)
        own[1] = jnp.int32(2 * token_rows)

    return pl.pallas_call(
        kernel,
        out_shape=[jax.ShapeDtypeStruct((n,), jnp.int32) for n in (5, 2, 2)],
        in_specs=[SMEM] * 3,
        out_specs=[SMEM] * 3,
        cost_estimate=NOTHING,
        name="bounds_of",
    )(doc_lengths, seg_doc, where)


def selection(where, core, slots, order):
    depth = 4 * len(order) * slots
    row = lax.broadcasted_iota(jnp.int32, (depth, 2 * depth), 0)
    column = lax.broadcasted_iota(jnp.int32, (depth, 2 * depth), 1)
    s, row = row % slots, row // slots
    z, row = jnp.zeros_like(row), row
    if len(order) > 1:
        step = row % len(order)
        bits, reversed_step = len(order).bit_length() - 1, jnp.zeros_like(row)
        for i in range(bits):
            reversed_step = reversed_step + ((step >> i) & 1) * (len(order) >> (i + 1))
        z = jnp.bitwise_xor(where[0], reversed_step)
        row = row // len(order)
    y, x = jnp.bitwise_xor(where[1], row // 2), jnp.bitwise_xor(where[3], row % 2)
    c = jnp.bitwise_xor(where[2], core)
    return (column == (((z * 2 + y) * 2 + c) * 2 + x) * slots + s).astype(bf16)


def mine_shapes(rows, width):
    return [jax.ShapeDtypeStruct((rows, width), f32)] + [
        jax.ShapeDtypeStruct((n, width), bf16) for n in (rows, rows, rows // 2, rows - rows // 2)
    ]


def taken_in(mine, received):
    _, rows, width = mine.shape
    half = rows // 2

    def kernel(mine_ref, got_ref, own, for_x, for_y, first, second):
        def total(side, at):
            return mine_ref[side, at].astype(f32) + got_ref[side, at].astype(f32)

        for i, ref in enumerate((own, for_x, for_y)):
            ref[...] = total(i, pl.ds(0, rows)).astype(ref.dtype)
        first[...] = total(3, pl.ds(0, half)).astype(bf16)
        second[...] = total(3, pl.ds(half, rows - half)).astype(bf16)

    out_shape = mine_shapes(rows, width)
    return pl.pallas_call(
        kernel,
        out_shape=out_shape,
        in_specs=[VMEM] * 2,
        out_specs=[VMEM] * 5,
        compiler_params=pltpu.CompilerParams(vmem_limit_bytes=room_for(*out_shape)),
        cost_estimate=NOTHING,
        name="taken_in",
    )(mine, received)


def sums_in_parts(where, arrays, products, memory_rows):
    order = z_places()
    slots = D // (8 * len(order))
    width = D * sum(arrays[right].shape[1] // D for _, right, _ in products if right is not None)
    width += sum(arrays[left].shape[0] for left, right, _ in products if right is None)
    given, memory = [], []
    for core in range(2):
        pick = selection(where, core, slots, order)
        columns = []
        for left, right, first in products:
            turned = times_transpose(pick, arrays[left]).astype(bf16)
            if right is not None:
                turned = matmul(turned[:, first:], arrays[right]).astype(bf16)
            columns.append(turned)
        given.append(jnp.concatenate(columns, axis=1).reshape(4, -1, width))
    if not memory_rows:
        return given
    key_grad, value_grad, key_weight, value_weight = arrays[-4:]
    grad = times_transpose(key_grad, key_weight) + times_transpose(value_grad, value_weight)
    whole = lax.dynamic_update_slice(
        jnp.zeros((8 * len(order) * memory_rows, D), bf16), grad.astype(bf16), (where[4], 0)
    ).reshape(8 * len(order), memory_rows, D)
    for core in range(2):
        c = jnp.bitwise_xor(where[2], core)
        devices = []
        for r in order:
            for side in range(4):
                y, x = jnp.bitwise_xor(where[1], side // 2), jnp.bitwise_xor(where[3], side % 2)
                devices.append(((jnp.bitwise_xor(where[0], r) * 2 + y) * 2 + c) * 2 + x)
        slabs = whole[jnp.stack(devices)].reshape(len(devices), 2, memory_rows // 2, D)
        memory.append(jnp.transpose(slabs, (1, 0, 2, 3)).reshape(-1, D))
    return given + memory


def sums_out(where, arrays, products, memory_rows=0):
    order = z_places()
    slots = D // (8 * len(order))
    if slots % 8:
        return sums_in_parts(where, arrays, products, memory_rows)
    n_in = len(arrays)
    depth = slots * len(order)
    blocks, column = [], 0
    for left, right, first in products:
        wide = arrays[left].shape[0] if right is None else arrays[right].shape[1]
        for at in range(0, wide, D):
            size = min(D, wide - at)
            blocks.append((left, right, first, at, size, column))
            column += size
    width = column
    window = arrays[-4].shape[0] if memory_rows else 8
    half = memory_rows // 2

    def kernel(at, *refs):
        ins, outs, block_ref, grad_ref = refs[:n_in], refs[n_in:-2], refs[-2], refs[-1]

        def places(core):
            c = jnp.bitwise_xor(at[2], core)
            for side in range(4):
                y, x = jnp.bitwise_xor(at[1], side // 2), jnp.bitwise_xor(at[3], side % 2)
                for i, r in enumerate(order):
                    yield side, i, ((jnp.bitwise_xor(at[0], r) * 2 + y) * 2 + c) * 2 + x

        if memory_rows:
            key_grad, value_grad, key_weight, value_weight = ins[-4:]
            grad_ref[...] = times_transpose(key_grad[...], key_weight[...]) + times_transpose(
                value_grad[...], value_weight[...]
            )
            for core in (1, 0):
                for side, i, device in places(core):
                    start = device * memory_rows - at[4]
                    inside = (start >= 0) & (start + memory_rows <= window)
                    start = pl.multiple_of(jnp.where(inside, start, 0), memory_rows)
                    slab = grad_ref[pl.ds(start, memory_rows), :]
                    slab = jnp.where(inside, slab, jnp.zeros_like(slab)).astype(bf16)
                    for n in range(2):
                        first = ((n * len(order) + i) * 4 + side) * half
                        outs[2 + core][first : first + half, :] = slab[n * half : (n + 1) * half]
        for n, (left, right, first, from_, size, to) in enumerate(blocks):
            if right is None:
                block = ins[left][...].astype(f32).T
            else:
                block = contract_rows(ins[left][first:, :], ins[right][:, from_ : from_ + size])
            slot = n % 2
            block_ref[slot, :, :, :size] = block.reshape(8 * len(order), slots, size)
            for core in (1, 0):
                for side, i, device in places(core):
                    slab = block_ref[slot, device, :, :size].astype(bf16)
                    outs[core][side, i * slots : (i + 1) * slots, to : to + size] = slab

    out_shape = [jax.ShapeDtypeStruct((4, depth, width), bf16)] * 2
    if memory_rows:
        out_shape += [jax.ShapeDtypeStruct((len(order) * 4 * memory_rows, D), bf16)] * 2
    return pl.pallas_call(
        kernel,
        out_shape=out_shape,
        in_specs=[SMEM] + [VMEM] * n_in,
        out_specs=[VMEM] * len(out_shape),
        scratch_shapes=[
            pltpu.VMEM((2, 8 * len(order), slots, D), f32),
            pltpu.VMEM((window, D), f32),
        ],
        compiler_params=pltpu.CompilerParams(
            vmem_limit_bytes=room_for(*out_shape) + 2 * D * D * 4 + window * D * 4 + 3 * 2**20
        ),
        cost_estimate=NOTHING,
        name="sums_out",
    )(where, *arrays)


def hidden_sums_out(where, activated, grad):
    hidden = activated.shape[1]
    order = z_places()
    span = hidden // len(order)
    slots, fold = span // 8, hidden // D
    part = slots // fold
    if span % 128 or part % 8:
        given = []
        for core in range(2):
            pick = selection(where, core, slots, order)
            turned = times_transpose(pick, activated).astype(bf16)
            rows = matmul(turned, grad).astype(bf16).reshape(4, len(order), fold, part, D)
            given.append(jnp.transpose(rows, (0, 1, 3, 2, 4)).reshape(4, -1, hidden))
        return given

    def kernel(at, act_ref, grad_ref, mine, other, block_ref):
        for i, r in enumerate(order):
            first = pl.multiple_of(jnp.bitwise_xor(at[0], r) * span, 128)
            block = contract_rows(act_ref[:, pl.ds(first, span)], grad_ref[...])
            block_ref[i % 2] = block.reshape(8, slots, D)
            for core, ref in ((1, other), (0, mine)):
                c = jnp.bitwise_xor(at[2], core)
                for side in range(4):
                    y, x = jnp.bitwise_xor(at[1], side // 2), jnp.bitwise_xor(at[3], side % 2)
                    slab = block_ref[i % 2, (y * 2 + c) * 2 + x].astype(bf16)
                    for j in range(fold):
                        ref[side, i * part : (i + 1) * part, j * D : (j + 1) * D] = slab[
                            j * part : (j + 1) * part
                        ]

    shape = jax.ShapeDtypeStruct((4, len(order) * part, hidden), bf16)
    return pl.pallas_call(
        kernel,
        out_shape=[shape, shape],
        in_specs=[SMEM] + [VMEM] * 2,
        out_specs=[VMEM] * 2,
        scratch_shapes=[pltpu.VMEM((2, 8, slots, D), f32)],
        compiler_params=pltpu.CompilerParams(
            vmem_limit_bytes=room_for(shape, shape) + 8 * 2**20
        ),
        cost_estimate=NOTHING,
        name="hidden_sums_out",
    )(where, activated, grad)


def hold(*values):
    return lax.optimization_barrier(values)


def z_first(shard):
    return swapped(shard[None], "z", lax.axis_size("z") // 2)


def z_rest(shard, received):
    by = lax.axis_size("z") // 2
    pieces, places = [shard[None], received], [0, by]
    while by > 1:
        by //= 2
        received = swapped(jnp.concatenate(pieces), "z", by)
        pieces, places = pieces + [received], places + [p ^ by for p in places]
    return pieces


def z_places():
    by, places = lax.axis_size("z") // 2, [0]
    while by:
        places = places + [p ^ by for p in places]
        by //= 2
    return places


def corners_in(over_x, over_y):
    half = over_x.shape[0] // 2
    return swapped(over_x[:half], "y"), swapped(over_y[half:], "x")


def corners_out(mine):
    return swapped(mine[3], "y"), swapped(mine[4], "x")


def sides_out(mine, corners, following=None):
    _, for_x, for_y = mine[:3]
    rows, width = for_x.shape
    half = rows // 2
    (over_y, y_first), (over_x, x_first) = corners
    more = [] if following is None else [following[3], following[4]]
    tail = half if more else 0

    def kernel(x_ref, y_ref, over_y_ref, over_x_ref, *refs):
        x_out, y_out = refs[-2:]
        came = over_y_ref[y_first : y_first + half].astype(f32)
        x_out[:half] = (x_ref[:half].astype(f32) + came).astype(bf16)
        x_out[half:rows] = x_ref[half:]
        came = over_x_ref[x_first : x_first + half].astype(f32)
        y_out[:half] = y_ref[:half]
        y_out[half:rows] = (y_ref[half:].astype(f32) + came).astype(bf16)
        if tail:
            y_out[rows:] = refs[0][...]
            x_out[rows:] = refs[1][...]

    shape = jax.ShapeDtypeStruct((rows + tail, width), bf16)
    x_out, y_out = pl.pallas_call(
        kernel,
        out_shape=[shape, shape],
        in_specs=[VMEM] * (4 + len(more)),
        out_specs=[VMEM] * 2,
        compiler_params=pltpu.CompilerParams(vmem_limit_bytes=room_for(shape, shape)),
        cost_estimate=NOTHING,
        name="sides_out",
    )(for_x, for_y, over_y, over_x, *more)
    return swapped(x_out, "x"), swapped(y_out, "y")


def apart(corners):
    return [(c, 0) for c in corners]


def halved(terms, parts, begin=0):
    rows, width = sum(parts), terms[0].shape[1]
    n_in = len(terms)

    def kernel(*refs):
        start, out = begin, 0
        for part in parts:
            half = part // 2
            for first, ref in ((start, refs[n_in]), (start + half, refs[n_in + 1])):
                total = sum(r[pl.ds(first, half), :].astype(f32) for r in refs[:n_in])
                ref[pl.ds(out, half), :] = total.astype(ref.dtype)
            start, out = start + part, out + half

    return pl.pallas_call(
        kernel,
        out_shape=[
            jax.ShapeDtypeStruct((rows // 2, width), f32),
            jax.ShapeDtypeStruct((rows // 2, width), bf16),
        ],
        in_specs=[VMEM] * n_in,
        out_specs=[VMEM] * 2,
        compiler_params=pltpu.CompilerParams(vmem_limit_bytes=room_for(terms[0])),
        cost_estimate=NOTHING,
        name="halved",
    )(*terms)


def halved_pair(first, second):
    rows, width = first[0].shape
    half = rows // 2
    counts = (len(first), len(second))

    def kernel(*refs):
        keep, give = refs[-2:]
        start = 0
        for n, count in enumerate(counts):
            terms = refs[start : start + count]
            start += count
            for at, ref in ((0, keep), (half, give)):
                total = sum(r[pl.ds(at, half), :].astype(f32) for r in terms)
                ref[pl.ds(n * half, half), :] = total.astype(ref.dtype)

    shapes = [jax.ShapeDtypeStruct((rows, width), kind) for kind in (f32, bf16)]
    return pl.pallas_call(
        kernel,
        out_shape=shapes,
        in_specs=[VMEM] * sum(counts),
        out_specs=[VMEM] * 2,
        compiler_params=pltpu.CompilerParams(vmem_limit_bytes=room_for(*shapes)),
        cost_estimate=NOTHING,
        name="halved_pair",
    )(*first, *second)


def z_most(terms, parts, begin=0, pair=None):
    by = 1
    keep, give = halved(terms, parts, begin) if pair is None else halved_pair(terms, pair)
    received, parts = swapped(give, "z", by), [p // 2 for p in parts]
    while 2 * by < lax.axis_size("z") // 2:
        by *= 2
        keep, give = halved([keep, received], parts)
        received, parts = swapped(give, "z", by), [p // 2 for p in parts]
    return keep, received


def z_last(keep, received, parts):
    by = lax.axis_size("z") // 2
    keep, give = halved([keep, received], [p // by for p in parts])
    return keep, swapped(give, "z", by)


def memory_taken(keep, received, rows):
    def kernel(keep_ref, got_ref, *outs):
        half = rows // 2
        for n in range(2):
            for z in range(2):
                for side in range(4):
                    here = pl.ds(((n * 2 + z) * 4 + side) * half, half)
                    total = keep_ref[here, :] + got_ref[here, :].astype(f32)
                    outs[side][pl.ds(z * rows + n * half, half), :] = total.astype(outs[side].dtype)

    out_shape = [like(2 * rows, D, f32)] + [like(2 * rows, D, bf16)] * 3
    return pl.pallas_call(
        kernel,
        out_shape=out_shape,
        in_specs=[VMEM] * 2,
        out_specs=[VMEM] * 4,
        compiler_params=pltpu.CompilerParams(vmem_limit_bytes=room_for(*out_shape, keep)),
        cost_estimate=NOTHING,
        name="memory_taken",
    )(keep, received)


def plus(keep, received):
    return keep + received.astype(f32)


def lane_halves(block):
    lanes = lax.broadcasted_iota(jnp.int32, block.shape, 1)
    zero = jnp.zeros_like(block)
    return jnp.where(lanes < HEAD, block, zero), jnp.where(lanes < HEAD, zero, block)


def fill_bias(bias_ref, first, bounds, causal):
    shape = bias_ref.shape
    rows = shape[1] // 2
    keys = first + lax.broadcasted_iota(jnp.int32, shape, 0)
    allowed = (keys >= bounds[0]) & (keys < bounds[1])
    if causal:
        queries = lax.broadcasted_iota(jnp.int32, shape, 1)
        queries = jnp.where(queries < rows, queries, queries - rows)
        allowed = allowed & (keys - rows <= queries)
    bias_ref[...] = jnp.where(allowed, 0.0, big_negative)


def both_halves(block):
    return jnp.concatenate(lane_halves(block), axis=0)


def key_block(width):
    return next(width // n for n in range(1, width) if width % (16 * n) == 0 and width // n <= 1536)


def attend_kernel(causal, block, bounds, q_ref, k_ref, v_ref, out_ref, low_ref, lse_ref, bias_ref):
    rows, width = q_ref.shape[0], k_ref.shape[0]
    if width == block:
        fill_bias(bias_ref, 0, bounds, causal)

    def pair(h, carried):
        lanes = pl.ds(pl.multiple_of(h * PAIR, PAIR), PAIR)
        both = both_halves(q_ref[:, lanes] * SCALE)

        def step(i, state):
            first = pl.multiple_of(i * block, block)
            if width > block:
                fill_bias(bias_ref, first, bounds, causal)
            keys, values = k_ref[pl.ds(first, block), lanes], v_ref[pl.ds(first, block), lanes]
            scores = times_transpose(keys, both) + bias_ref[...]
            top = jnp.max(scores, axis=0, keepdims=True)
            if state is not None:
                top = jnp.maximum(state[0], top)
            weights = jnp.exp(scores - top)
            total = jnp.sum(weights, axis=0, keepdims=True)
            summed = contract_rows(values, weights.astype(bf16))
            if state is not None:
                factor = jnp.exp(state[0] - top)
                total, summed = total + state[1] * factor, summed + state[2] * factor
            return top, total, summed

        state = step(0, None)
        if width > block:
            state = lax.fori_loop(1, width // block, step, state)
        top, total, summed = state
        out = summed / total
        out = jnp.concatenate([out[:HEAD, :rows], out[HEAD:, rows:]], axis=0).T
        out_ref[:, lanes] = out
        low_ref[:, lanes] = out.astype(bf16)
        lse_ref[h] = top + jnp.log(total)
        return carried

    lax.fori_loop(0, PAIRS, pair, 0, unroll=2)


def attend(queries, keys, values, bounds, causal):
    rows, width = queries.shape[0], keys.shape[0]
    block = key_block(width)
    out_shape = [
        jax.ShapeDtypeStruct((rows, D), f32),
        jax.ShapeDtypeStruct((rows, D), bf16),
        jax.ShapeDtypeStruct((PAIRS, 1, 2 * rows), f32),
    ]
    return pl.pallas_call(
        lambda *refs: attend_kernel(causal, block, *refs),
        scratch_shapes=[pltpu.VMEM((block, 2 * rows), f32)],
        in_specs=[SMEM] + [VMEM] * 3,
        out_specs=[VMEM] * 3,
        out_shape=out_shape,
        compiler_params=pltpu.CompilerParams(
            vmem_limit_bytes=16 * 2**20 if width <= 2048 else 48 * 2**20
        ),
        cost_estimate=NOTHING,
        name="attend_self" if causal else "attend_cross",
    )(bounds, queries, keys, values)


def attend_back_kernel(
    causal,
    block,
    bounds,
    q_ref,
    k_ref,
    v_ref,
    o_ref,
    g_ref,
    lse_ref,
    dq_ref,
    dk_ref,
    dv_ref,
    bias_ref,
):
    rows, width = q_ref.shape[0], k_ref.shape[0]
    if width == block:
        fill_bias(bias_ref, 0, bounds, causal)

    def pair(h, carried):
        lanes = pl.ds(pl.multiple_of(h * PAIR, PAIR), PAIR)
        queries = both_halves(q_ref[:, lanes] * SCALE)
        grads = both_halves(g_ref[:, lanes])
        products = (g_ref[:, lanes].astype(f32) * o_ref[:, lanes]).T
        delta = jnp.concatenate(
            [
                jnp.sum(products[:HEAD], axis=0, keepdims=True),
                jnp.sum(products[HEAD:], axis=0, keepdims=True),
            ],
            axis=1,
        )

        def step(i, query_grad):
            first = pl.multiple_of(i * block, block)
            if width > block:
                fill_bias(bias_ref, first, bounds, causal)
            here = pl.ds(first, block)
            keys, values = k_ref[here, lanes], v_ref[here, lanes]
            scores = times_transpose(keys, queries) + bias_ref[...]
            probs = jnp.exp(scores - lse_ref[h])
            dv_ref[here, lanes] = matmul(probs.astype(bf16), grads).astype(bf16)
            slopes = times_transpose(values, grads)
            score_grad = (probs * (slopes - delta)).astype(bf16)
            dk_ref[here, lanes] = matmul(score_grad, queries).astype(bf16)
            part = contract_rows(keys, score_grad)
            return part if query_grad is None else query_grad + part

        grad = step(0, None)
        if width > block:
            grad = lax.fori_loop(1, width // block, step, grad)
        grad = jnp.concatenate([grad[:HEAD, :rows], grad[HEAD:, rows:]], axis=0)
        dq_ref[:, lanes] = (grad * SCALE).T.astype(bf16)
        return carried

    lax.fori_loop(0, PAIRS, pair, 0, unroll=2)


def attend_back(queries, keys, values, out, grad, lse, bounds, causal):
    rows, width = queries.shape[0], keys.shape[0]
    block = key_block(width)
    out_shape = [
        jax.ShapeDtypeStruct((rows, D), bf16),
        jax.ShapeDtypeStruct((width, D), bf16),
        jax.ShapeDtypeStruct((width, D), bf16),
    ]
    return pl.pallas_call(
        lambda *refs: attend_back_kernel(causal, block, *refs),
        scratch_shapes=[pltpu.VMEM((block, 2 * rows), f32)],
        in_specs=[SMEM] + [VMEM] * 6,
        out_specs=[VMEM] * 3,
        out_shape=out_shape,
        compiler_params=pltpu.CompilerParams(
            vmem_limit_bytes=26 * 2**20 if width <= 2048 else 62 * 2**20
        ),
        cost_estimate=NOTHING,
        name="attend_back_self" if causal else "attend_back_cross",
    )(bounds, queries, keys, values, out, grad, lse)


def activate(values, weight):
    rows, hidden = values.shape[0], weight.shape[1]
    step = min(hidden, D)

    def kernel(values_ref, weight_ref, out_ref, slope_ref):
        for at in range(0, hidden, step):
            inner = matmul(values_ref[...], weight_ref[:, at : at + step])
            below = 0.5 * (1.0 + lax.erf(inner * (0.5**0.5)))
            out_ref[:, at : at + step] = (inner * below).astype(bf16)
            bell = jnp.exp(-0.5 * inner * inner) * (1.0 / math.sqrt(2.0 * math.pi))
            slope_ref[:, at : at + step] = below + inner * bell

    return pl.pallas_call(
        kernel,
        out_shape=[
            jax.ShapeDtypeStruct((rows, hidden), bf16),
            jax.ShapeDtypeStruct((rows, hidden), f32),
        ],
        in_specs=[VMEM] * 2,
        out_specs=[VMEM] * 2,
        compiler_params=pltpu.CompilerParams(vmem_limit_bytes=8 * 2**20),
        cost_estimate=NOTHING,
        name="activate",
    )(values, weight)


def whole_kernel(kernel, name, out_shape, *arrays, spare=2):
    return pl.pallas_call(
        kernel,
        out_shape=out_shape,
        in_specs=[VMEM] * len(arrays),
        out_specs=[VMEM] * len(out_shape),
        compiler_params=pltpu.CompilerParams(
            vmem_limit_bytes=min(room_for(*out_shape) + spare * 2**20, 62 * 2**20)
        ),
        cost_estimate=NOTHING,
        name=name,
    )(*arrays)


def like(rows, columns, dtype):
    return jax.ShapeDtypeStruct((rows, columns), dtype)


def row_mean(values):
    return jnp.sum(values, axis=-1, keepdims=True) * (1.0 / values.shape[-1])


def normed(values):
    centered = values - row_mean(values)
    inverse = lax.rsqrt(row_mean(centered * centered) + epsilon)
    return centered * inverse, inverse


def norm_back(grad, unit, inverse, gain):
    scaled = grad * gain
    inner = scaled - row_mean(scaled) - unit * row_mean(scaled * unit)
    return inner * inverse, jnp.sum(grad * unit, axis=0, keepdims=True)


def add_and_norm(base, out, weight, gain):
    rows = base.shape[0]

    def kernel(b_ref, o_ref, w_ref, g_ref, hidden_ref, low_ref, unit_ref, inverse_ref):
        mid = b_ref[...].astype(f32) + matmul(o_ref[...], w_ref[...])
        unit, inverse = normed(mid)
        hidden = unit * g_ref[...]
        hidden_ref[...], low_ref[...] = hidden, hidden.astype(bf16)
        unit_ref[...], inverse_ref[...] = unit, inverse

    out_shape = [like(rows, D, f32), like(rows, D, bf16), like(rows, D, f32), like(rows, 1, f32)]
    return whole_kernel(kernel, "add_and_norm", out_shape, base, out, weight, gain)


def feed_turn(activated, weight, hidden, gain, cotangent):
    rows = hidden.shape[0]

    def kernel(a_ref, w_ref, h_ref, g_ref, c_ref, out_ref, grad_ref, low_ref, gain_ref):
        unit, inverse = normed(h_ref[...] + matmul(a_ref[...], w_ref[...]))
        gain = g_ref[...]
        out_ref[...] = (unit * gain).astype(bf16)
        grad, gain_grad = norm_back(c_ref[...].astype(f32), unit, inverse, gain)
        grad_ref[...], low_ref[...], gain_ref[...] = grad, grad.astype(bf16), gain_grad

    out_shape = [like(rows, D, bf16), like(rows, D, f32), like(rows, D, bf16), like(1, D, f32)]
    return whole_kernel(
        kernel, "feed_turn", out_shape, activated, weight, hidden, gain, cotangent
    )


def self_turn(above, grad, weight, unit, inverse, gain, out_weight, gain_cross, gain_feed):
    rows = above.shape[0]

    def kernel(a_ref, d_ref, w_ref, u_ref, i_ref, g_ref, o_ref, c_ref, f_ref, *outs):
        grad_ref, low_ref, gains_ref, out_ref = outs
        total = a_ref[...] + times_transpose(d_ref[...], w_ref[...])
        grad, gain_grad = norm_back(total, u_ref[...], i_ref[...], g_ref[...])
        low = grad.astype(bf16)
        grad_ref[...], low_ref[...] = grad, low
        rest = jnp.zeros((125, D), f32)
        gains = jnp.concatenate([gain_grad, c_ref[...], f_ref[...], rest], axis=0)
        gains_ref[...] = gains.astype(bf16)
        out_ref[...] = times_transpose(low, o_ref[...]).astype(bf16)

    out_shape = [like(rows, D, f32), like(rows, D, bf16), like(128, D, bf16), like(rows, D, bf16)]
    return whole_kernel(
        kernel,
        "self_turn",
        out_shape,
        above,
        grad,
        weight,
        unit,
        inverse,
        gain,
        out_weight,
        gain_cross,
        gain_feed,
    )


def padded(shard, rows):
    return jnp.pad(shard, ((0, rows - shard.shape[0]), (0, 0)))


def grouped(shard, group):
    return shard.reshape(shard.shape[0] // group, group, shard.shape[1])


def per_device(
    tokens,
    memory,
    self_query,
    self_key,
    self_value,
    self_output,
    cross_query,
    cross_key,
    cross_value,
    cross_output,
    feed_in,
    feed_out,
    gain_self,
    gain_cross,
    gain_feed,
    doc_lengths,
    seg_doc,
    cotangent,
):
    where = position()
    token_rows = tokens.shape[0]
    count = lax.axis_size("z") * 8
    slots = self_query.shape[0]
    memory_rows = memory.shape[0]
    group = math.gcd(8, slots) if slots % 4 == 0 else slots
    memory_groups = pl.cdiv(memory_rows, group)
    gain_groups = pl.cdiv(3, group)
    gain_rows = gain_groups * group
    slot_groups = slots // group

    gains = jnp.pad(jnp.stack([gain_self, gain_cross, gain_feed]), ((0, gain_rows - 3), (0, D - slots)))
    hidden = feed_in.shape[1]
    places = z_places()
    cuts1 = [(i * slot_groups, slot_groups, 1) for i in range(4)]
    cuts1.append((4 * slot_groups, gain_groups, 1))
    cuts2 = [(i * slot_groups, slot_groups, 1) for i in range(3)]
    cuts3 = [(0, slot_groups, 1), (slot_groups, slot_groups, hidden // D)]
    cuts4 = [(0, feed_out.shape[0] // group, 1)]
    s1 = packed([self_query, self_key, self_value, self_output, gains], group)
    s2 = packed(
        [cross_query, cross_key, cross_value, padded(memory, memory_groups * group)], group
    )
    s3 = packed([cross_output, feed_in], group)
    s4 = grouped(feed_out, group)

    window = count * memory_rows // 2 + memory_rows
    where_window, cross_bounds, self_bounds = bounds_of(
        doc_lengths, seg_doc, where, memory_rows, count * memory_rows, window, token_rows
    )
    a1 = z_first(s1)
    earlier = lax.ppermute(tokens, "x", [(0, 1)])
    a1, s2, s3, s4 = hold(a1, s2, s3, s4)
    near = jnp.concatenate([s1[None], a1])
    early = near.shape[0] == lax.axis_size("z") // 2
    b1 = z_rest(s1, a1)
    a2 = z_first(s2)
    if early:
        x1, y1 = [swapped(near, "x")], [swapped(near, "y")]
        own1, far = [near], b1[2]
        far, a2, earlier, s3, s4, x1, y1 = hold(far, a2, earlier, s3, s4, x1, y1)
        own1.append(far)
        x1.append(swapped(far, "x"))
        y1.append(swapped(far, "y"))
    else:
        own1 = in_order(b1, places, where)
        own1, a2, earlier, s3, s4 = hold(own1, a2, earlier, s3, s4)
        x1, y1 = swapped(own1, "x"), swapped(own1, "y")
    b2 = z_rest(s2, a2)
    a3 = z_first(s3)
    both_tokens = jnp.concatenate([earlier, tokens], axis=0)
    own2 = in_order(b2, places, where)
    own2, x1, y1, own1, both_tokens, s4 = hold(own2, x1, y1, own1, both_tokens, s4)

    if early:
        d1 = swapped(x1[0], "y"), swapped(y1[1], "x")
    else:
        d1 = corners_in(x1, y1)
    x2, y2 = swapped(own2, "x"), swapped(own2, "y")
    b3 = z_rest(s3, a3)
    own3 = in_order(b3, places, where)
    a4 = z_first(s4)
    d1, x2, y2, own2, own3, a4, where_window, cross_bounds, self_bounds = hold(
        d1, x2, y2, own2, own3, a4, where_window, cross_bounds, self_bounds
    )

    d2 = corners_in(x2, y2)
    x3, y3 = swapped(own3, "x"), swapped(own3, "y")
    if early:
        half1 = half_by_steps(own1, x1, y1, d1, places, where)
    else:
        half1 = half_of(own1, x1, y1, d1, where)
    c1 = swapped(half1, "c")
    wholes = assembled(half1, c1, cuts1, where)
    self_query, self_key, self_value, self_output = (w.reshape(D, D) for w in wholes[:4])
    b4 = z_rest(s4, a4)
    gains = wholes[4].reshape(count, gain_rows, D)[:, :3, :slots]
    gain_self, gain_cross, gain_feed = (
        gains[:, i].reshape(D).astype(f32) for i in range(3)
    )
    queries = matmul(tokens, self_query).astype(bf16)
    keys = matmul(both_tokens, self_key).astype(bf16)
    values = matmul(both_tokens, self_value).astype(bf16)
    self_full, self_out, self_lse = attend(queries, keys, values, self_bounds, True)
    b4, self_out = hold(b4, self_out)
    own4 = in_order(b4, places, where)
    hidden_self, hidden_self_low, unit_self, inverse_self = add_and_norm(
        tokens, self_out, self_output, gain_self.reshape(1, D)
    )
    d2, x3, y3, own3, own4, hidden_self, hidden_self_low = hold(
        d2, x3, y3, own3, own4, hidden_self, hidden_self_low
    )

    d3 = corners_in(x3, y3)
    x4, y4 = swapped(own4, "x"), swapped(own4, "y")
    half2 = half_of(own2, x2, y2, d2, where)
    c2 = swapped(half2, "c")
    wholes = assembled(half2, c2, cuts2, where)
    cross_query, cross_key, cross_value = (w.reshape(D, D) for w in wholes)
    memory_here = window_of(half2, c2, 3 * slot_groups, memory_rows, window, where_window)
    cross_queries = matmul(hidden_self_low, cross_query).astype(bf16)
    memory_keys = matmul(memory_here, cross_key).astype(bf16)
    memory_values = matmul(memory_here, cross_value).astype(bf16)
    cross_full, cross_out, cross_lse = attend(
        cross_queries, memory_keys, memory_values, cross_bounds, False
    )
    d3, x4, y4, own4, cross_out = hold(d3, x4, y4, own4, cross_out)

    d4 = corners_in(x4, y4)
    half3 = half_of(own3, x3, y3, d3, where)
    c3 = swapped(half3, "c")
    wholes = assembled(half3, c3, cuts3, where)
    cross_output, feed_in = (w.reshape(D, w.shape[-1]) for w in wholes)
    mid_cross = hidden_self + matmul(cross_out, cross_output)
    hidden_cross, back_cross = jax.vjp(layer_norm, mid_cross, gain_cross)
    hidden_cross_low = hidden_cross.astype(bf16)
    activated, slope = activate(hidden_cross_low, feed_in)
    d4, activated, own4 = hold(d4, activated, own4)
    half4 = half_of(own4, x4, y4, d4, where)
    c4 = swapped(half4, "c")
    wholes = assembled(half4, c4, cuts4, where)
    feed_out = wholes[0].reshape(hidden, D)
    layer_out, gradient_feed_mid, feed_rounded, gain_feed_sum = feed_turn(
        activated, feed_out, hidden_cross, gain_feed.reshape(1, D), cotangent
    )
    m4, o4 = hidden_sums_out(where, activated, feed_rounded)
    m4, o4, feed_rounded = hold(m4, o4, feed_rounded)
    r4 = swapped(o4, "c")
    gradient_inner = (times_transpose(feed_rounded, feed_out) * slope).astype(bf16)
    m3, o3 = sums_out(where, [hidden_cross_low, gradient_inner], [(0, 1, 0)])
    r4, m3, o3, gradient_inner = hold(r4, m3, o3, gradient_inner)
    m4 = taken_in(m4, r4)
    d4 = corners_out(m4)
    r3 = swapped(o3, "c")
    gradient_hidden_cross = gradient_feed_mid + times_transpose(gradient_inner, feed_in)
    gradient_cross_mid, gain_cross_sum = back_cross(gradient_hidden_cross)
    cross_rounded = gradient_cross_mid.astype(bf16)

    outgoing = times_transpose(cross_rounded, cross_output).astype(bf16)
    r3, d4, outgoing, cross_rounded = hold(r3, d4, outgoing, cross_rounded)
    m3 = taken_in(m3, r3)
    x4, y4 = sides_out(m4, apart(d4), m3)
    cross_query_grad, memory_key_grad, memory_value_grad = attend_back(
        cross_queries,
        memory_keys,
        memory_values,
        cross_full,
        outgoing,
        cross_lse,
        cross_bounds,
        False,
    )
    gradient_self_mid, self_rounded, gain_sums, self_outgoing = self_turn(
        gradient_cross_mid,
        cross_query_grad,
        cross_query,
        unit_self,
        inverse_self,
        gain_self.reshape(1, D),
        self_output,
        gain_cross_sum.reshape(1, D),
        gain_feed_sum,
    )

    query_grad, key_grad, value_grad = attend_back(
        queries, keys, values, self_full, self_outgoing, self_lse, self_bounds, True
    )
    m1, o1 = sums_out(
        where,
        [
            both_tokens,
            query_grad,
            key_grad,
            value_grad,
            self_out,
            self_rounded,
            gain_sums,
        ],
        [(0, 1, token_rows), (0, 2, 0), (0, 3, 0), (4, 5, 0), (6, None, 0)],
    )
    x4, y4, m1, o1, cross_query_grad, query_grad, key_grad, value_grad = hold(
        x4, y4, m1, o1, cross_query_grad, query_grad, key_grad, value_grad
    )
    x3, y3 = sides_out(m3, [(y4, D // 8), (x4, D // 8)])
    parts1, parts5 = [D // 8], [count * memory_rows // 4] * 2
    k4 = z_most([m4[0], x4, y4], parts1)
    r1 = swapped(o1, "c")
    m2, o2, m5, o5 = sums_out(
        where_window,
        [
            hidden_self_low,
            cross_query_grad,
            memory_here,
            cross_out,
            cross_rounded,
            gain_sums,
            memory_key_grad,
            memory_value_grad,
            cross_key,
            cross_value,
        ],
        [(0, 1, 0), (2, 6, 0), (2, 7, 0), (3, 4, 0), (5, None, 0)],
        memory_rows,
    )
    x3, y3, k4, m1, r1, m2, o2, m5, o5, query_grad, key_grad, value_grad = hold(
        x3, y3, k4, m1, r1, m2, o2, m5, o5, query_grad, key_grad, value_grad
    )
    m1 = taken_in(m1, r1)
    d1 = corners_out(m1)
    r2, r5 = swapped(o2, "c"), swapped(o5, "c")
    k3 = z_most([m3[0], x3, y3], parts1)
    both_grad = times_transpose(key_grad, self_key) + times_transpose(value_grad, self_value)
    to_earlier = both_grad[:token_rows].astype(bf16)
    partial_tokens = (
        gradient_self_mid + times_transpose(query_grad, self_query) + both_grad[token_rows:]
    )
    d1, m1, r2, r5, k3, k4, m2, m5, partial_tokens, to_earlier = hold(
        d1, m1, r2, r5, k3, k4, m2, m5, partial_tokens, to_earlier
    )
    m2 = taken_in(m2, r2)
    x1, y1 = sides_out(m1, apart(d1), m2)
    k5 = z_most([m5, r5], parts5)
    x1, y1, k3, k4, k5 = hold(x1, y1, k3, k4, k5)
    x2, y2 = sides_out(m2, [(y1, D // 8), (x1, D // 8)])
    k1 = z_most([m1[0], x1, y1], parts1)
    keep, give = halved_pair(list(k4), list(k3))
    k3 = keep, swapped(give, "z", lax.axis_size("z") // 2)
    x2, y2, k1, k3, k5, to_earlier = hold(x2, y2, k1, k3, k5, to_earlier)
    total_feed = plus(*k3)
    k2 = z_most([m2[0], x2, y2], parts1)
    k1 = z_last(*k1, parts1)
    m5 = memory_taken(*k5, memory_rows)
    x5, y5 = swapped(m5[1], "x"), swapped(m5[2], "y")
    d5 = lax.ppermute(m5[3], ("y", "x"), [(i, 3 - i) for i in range(4)])
    k2, x5, y5, d5, k1, to_earlier = hold(k2, x5, y5, d5, k1, to_earlier)
    sent_back = lax.ppermute(to_earlier, "x", [(1, 0)])
    k2 = z_last(*k2, parts1)
    keep, give = halved([m5[0], x5, y5, d5], [2 * memory_rows])
    k5 = keep, swapped(give, "z", lax.axis_size("z") // 2)
    total_self = plus(*k1)
    gradient_memory = plus(*k5)
    gradient_tokens = plus(partial_tokens, sent_back)
    total_cross = plus(*k2)

    self_parts = [total_self[:, i * D : (i + 1) * D] for i in range(4)]
    cross_parts = [total_cross[:, i * D : (i + 1) * D] for i in range(4)]
    return (
        layer_out,
        gradient_tokens,
        gradient_memory,
        *self_parts,
        *cross_parts,
        total_feed[slots:],
        jnp.concatenate([total_feed[:slots, i * D : (i + 1) * D] for i in range(hidden // D)]),
        total_self[:, 4 * D],
        total_self[:, 4 * D + 1],
        total_self[:, 4 * D + 2],
    )


def solution(mesh):
    fine = Mesh(mesh.devices.reshape(-1, 2, 2, 2), ALL)
    rows = P(ALL, None)
    return jax.shard_map(
        per_device,
        mesh=fine,
        in_specs=(rows,) * 12 + (P(ALL),) * 3 + (P(), P(), rows),
        out_specs=(rows,) * 13 + (P(ALL),) * 3,
        check_vma=False,
    )
```

```python
import math

import jax
import jax.numpy as jnp
from jax import lax
from jax.experimental import pallas as pl
from jax.experimental.pallas import tpu as pltpu
from jax.sharding import Mesh
from jax.sharding import PartitionSpec as P

D = 768
HEADS = 12
HEAD = 64
PAIR = 2 * HEAD
PAIRS = HEADS // 2
SCALE = HEAD ** (-0.5)

big_negative = -1e30
epsilon = 1e-05
bf16 = jnp.bfloat16
f32 = jnp.float32
ALL = ("z", "y", "c", "x")
NOTHING = pl.CostEstimate(flops=1, bytes_accessed=1, transcendentals=0)
VMEM = pl.BlockSpec(memory_space=pltpu.VMEM)
ANY = pl.BlockSpec(memory_space=pl.ANY)


def room_for(*arrays):
    held = 0
    for a in arrays:
        rows, width = a.shape[-2], a.shape[-1]
        held += math.prod(a.shape[:-2]) * pl.cdiv(rows, 16 if rows % 8 else 8) * (
            16 if rows % 8 else 8
        ) * pl.cdiv(width, 128) * 128 * a.dtype.itemsize
    return held + 2 * 2**20
SMEM = pl.BlockSpec(memory_space=pltpu.SMEM)


def matmul(left, right):
    return jnp.dot(left, right, preferred_element_type=f32)


def contract_rows(left, right):
    return lax.dot_general(left, right, (((0,), (0,)), ((), ())), preferred_element_type=f32)


def times_transpose(left, right):
    return lax.dot_general(left, right, (((1,), (1,)), ((), ())), preferred_element_type=f32)


def layer_norm(values, gain):
    centered = values - jnp.mean(values, axis=-1, keepdims=True)
    variance = jnp.mean(centered * centered, axis=-1, keepdims=True)
    return centered * lax.rsqrt(variance + epsilon) * gain


def exact_gelu(values):
    return jax.nn.gelu(values, approximate=False)


def table_entry(table, index):
    places = jnp.arange(table.shape[0], dtype=jnp.int32)
    return jnp.sum(jnp.where(places == index, table, 0))


def swapped(value, axis, by=1):
    size = lax.axis_size(axis)
    return lax.ppermute(value, axis, [(i, i ^ by) for i in range(size)])


def position():
    return jnp.stack([lax.axis_index(a).astype(jnp.int32) for a in ALL])


def packed(shards, group):
    blocks, first = [], 0
    for i, shard in enumerate(shards):
        size = shard.shape[0] // group
        for column in range(0, shard.shape[1], D):
            blocks.append((i, column, first, size))
            first += size
    n_in = len(shards)

    def kernel(*refs):
        out, sems = refs[-2:]
        copies = [
            pltpu.make_async_copy(
                refs[i].at[:, :, pl.ds(column, D)], out.at[pl.ds(at, size)], sems.at[n]
            )
            for n, (i, column, at, size) in enumerate(blocks)
        ]
        for copy in copies:
            copy.start()
        for copy in copies:
            copy.wait()

    return pl.pallas_call(
        kernel,
        out_shape=jax.ShapeDtypeStruct((first, group, D), shards[0].dtype),
        in_specs=[pl.BlockSpec(memory_space=pltpu.HBM)] * n_in,
        out_specs=VMEM,
        scratch_shapes=[pltpu.SemaphoreType.DMA((len(blocks),))],
        compiler_params=pltpu.CompilerParams(vmem_limit_bytes=60 * 2**20),
        cost_estimate=NOTHING,
        name="packed",
    )(*(s.reshape(s.shape[0] // group, group, s.shape[1]) for s in shards))


def in_order(pieces, places, where, cut=None):
    n_in = len(pieces)
    count, groups = len(places), pieces[0].shape[1]
    spans = [(0, groups)] if cut is None else [(0, cut), (cut, groups - cut)]

    def kernel(at, *refs):
        first = 0
        for i in range(n_in):
            for j in range(pieces[i].shape[0]):
                z = jnp.bitwise_xor(at[0], places[first])
                for o, (start, size) in enumerate(spans):
                    refs[n_in + o][z] = refs[i][j, start : start + size]
                first += 1

    outs = pl.pallas_call(
        kernel,
        out_shape=[
            jax.ShapeDtypeStruct((count, size) + pieces[0].shape[2:], pieces[0].dtype)
            for _, size in spans
        ],
        in_specs=[SMEM] + [VMEM] * n_in,
        out_specs=[VMEM] * len(spans),
        compiler_params=pltpu.CompilerParams(vmem_limit_bytes=room_for(*pieces)),
        cost_estimate=NOTHING,
        name="in_order",
    )(where, *pieces)
    return outs[0] if cut is None else outs


def half_of(own, over_x, over_y, corners, where):
    count, groups, *tail = own.shape
    tail = tuple(tail)
    half = count // 2

    def kernel(at, own_ref, x_ref, y_ref, first_ref, second_ref, out_ref):
        y, x = at[1], at[3]
        out_ref[:, y, x] = own_ref[...]
        out_ref[:, y, 1 - x] = x_ref[...]
        out_ref[:, 1 - y, x] = y_ref[...]
        out_ref[:half, 1 - y, 1 - x] = first_ref[...]
        out_ref[half:, 1 - y, 1 - x] = second_ref[...]

    return pl.pallas_call(
        kernel,
        out_shape=jax.ShapeDtypeStruct((count, 2, 2, groups) + tail, own.dtype),
        in_specs=[SMEM] + [VMEM] * 5,
        out_specs=VMEM,
        compiler_params=pltpu.CompilerParams(vmem_limit_bytes=room_for(*[own] * 4)),
        cost_estimate=NOTHING,
        name="half_of",
    )(where, own, over_x, over_y, *corners)


def assembled(own, other, cuts, where):
    count, _, _, groups, group, width = own.shape
    step = count if count <= 8 else 1

    def kernel(at, *refs):
        for dc in range(2):
            c = jnp.bitwise_xor(at[2], dc)
            for o, (first, size, blocks) in enumerate(cuts):
                for b in range(blocks):
                    here = first + b * size
                    columns = slice(b * width, (b + 1) * width)
                    for z in range(step):
                        for y in range(2):
                            block = refs[dc][z, y, :, here : here + size]
                            refs[2 + o][z, y, c, :, :, :, columns] = block

    outs = [
        jax.ShapeDtypeStruct((count, 2, 2, 2, size, group, blocks * width), own.dtype)
        for _, size, blocks in cuts
    ]
    if step == count:
        specs = dict(in_specs=[SMEM, VMEM, VMEM], out_specs=[VMEM] * len(outs))
    else:
        specs = dict(
            grid=(count,),
            in_specs=[SMEM]
            + [pl.BlockSpec((1, 2, 2, groups, group, width), lambda z: (z, 0, 0, 0, 0, 0))] * 2,
            out_specs=[
                pl.BlockSpec((1,) + out.shape[1:], lambda z: (z, 0, 0, 0, 0, 0, 0)) for out in outs
            ],
        )
    return pl.pallas_call(
        kernel,
        out_shape=outs,
        compiler_params=pltpu.CompilerParams(
            vmem_limit_bytes=room_for(*outs) if step == count else 32 * 2**20
        ),
        cost_estimate=NOTHING,
        name="assembled",
        **specs,
    )(where, own, other)


def half_by_steps(own, over_x, over_y, corner, steps, where):
    lists = (own, over_x, over_y, corner)
    arrays = [a for part in lists for a in part]
    count, tail = len(steps), own[0].shape[1:]

    def kernel(at, *refs):
        y, x = at[1], at[3]
        spots = ((y, x), (y, 1 - x), (1 - y, x), (1 - y, 1 - x))
        ref = iter(refs)
        for part, spot in zip(lists, spots):
            n = 0
            for a in part:
                source = next(ref)
                for k in range(a.shape[0]):
                    refs[-1][jnp.bitwise_xor(at[0], steps[n]), spot[0], spot[1]] = source[k]
                    n += 1

    out = jax.ShapeDtypeStruct((count, 2, 2) + tail, own[0].dtype)
    return pl.pallas_call(
        kernel,
        out_shape=out,
        in_specs=[SMEM] + [VMEM] * len(arrays),
        out_specs=VMEM,
        compiler_params=pltpu.CompilerParams(vmem_limit_bytes=room_for(out) + 2**20),
        cost_estimate=NOTHING,
        name="half_by_steps",
    )(where, *arrays)


def window_of(own, other, first_group, rows, window, where):
    count, _, _, groups, group, width = own.shape
    groups = groups - first_group
    if count > 8 or group % 8:
        whole = assembled(own, other, [(first_group, groups, 1)], where)[0]
        whole = whole.reshape(8 * count, groups * group, width)[:, :rows]
        return lax.dynamic_slice(
            whole.reshape(8 * count * rows, width), (where[4], 0), (window, width)
        )
    held = window // rows

    def kernel(at, own_ref, other_ref, out_ref):
        first = at[4] // rows
        for i in range(held):
            device = first + i
            core = jnp.bitwise_xor(device // 2 % 2, at[2])
            z, y, x = device // 8, device // 4 % 2, device % 2
            for c, ref in ((0, own_ref), (1, other_ref)):

                @pl.when(core == c)
                def _(ref=ref):
                    out_ref[i] = ref[z, y, x, first_group:]

    out = jax.ShapeDtypeStruct((held, groups, group, width), own.dtype)
    out = pl.pallas_call(
        kernel,
        out_shape=out,
        in_specs=[SMEM, VMEM, VMEM],
        out_specs=VMEM,
        compiler_params=pltpu.CompilerParams(vmem_limit_bytes=room_for(own, out)),
        cost_estimate=NOTHING,
        name="window_of",
    )(where, own, other)
    return out.reshape(window, width)


def bounds_of(doc_lengths, seg_doc, where, rows, memory_rows, window, token_rows):
    def kernel(lengths, seg, at, place, cross, own):
        document = seg[(at[0] * 2 + at[1]) * 2 + at[2]]
        start, size = jnp.int32(0), jnp.int32(0)
        for d in range(doc_lengths.shape[0]):
            start = start + jnp.where(document > d, lengths[d], 0)
            size = size + jnp.where(document == d, lengths[d], 0)
        first = jnp.minimum(start // rows * rows, memory_rows - window)
        for i in range(4):
            place[i] = at[i]
        place[4] = first
        cross[0], cross[1] = start - first, start - first + size
        own[0] = jnp.where(at[3] == 0, token_rows, 0)
        own[1] = jnp.int32(2 * token_rows)

    return pl.pallas_call(
        kernel,
        out_shape=[jax.ShapeDtypeStruct((n,), jnp.int32) for n in (5, 2, 2)],
        in_specs=[SMEM] * 3,
        out_specs=[SMEM] * 3,
        cost_estimate=NOTHING,
        name="bounds_of",
    )(doc_lengths, seg_doc, where)


def selection(where, core, slots, order):
    depth = 4 * len(order) * slots
    row = lax.broadcasted_iota(jnp.int32, (depth, 2 * depth), 0)
    column = lax.broadcasted_iota(jnp.int32, (depth, 2 * depth), 1)
    s, row = row % slots, row // slots
    z, row = jnp.zeros_like(row), row
    if len(order) > 1:
        step = row % len(order)
        bits, reversed_step = len(order).bit_length() - 1, jnp.zeros_like(row)
        for i in range(bits):
            reversed_step = reversed_step + ((step >> i) & 1) * (len(order) >> (i + 1))
        z = jnp.bitwise_xor(where[0], reversed_step)
        row = row // len(order)
    y, x = jnp.bitwise_xor(where[1], row // 2), jnp.bitwise_xor(where[3], row % 2)
    c = jnp.bitwise_xor(where[2], core)
    return (column == (((z * 2 + y) * 2 + c) * 2 + x) * slots + s).astype(bf16)


def mine_shapes(rows, width):
    return [jax.ShapeDtypeStruct((rows, width), f32)] + [
        jax.ShapeDtypeStruct((n, width), bf16) for n in (rows, rows, rows // 2, rows - rows // 2)
    ]


def taken_in(mine, received):
    _, rows, width = mine.shape
    half = rows // 2

    def kernel(mine_ref, got_ref, own, for_x, for_y, first, second):
        def total(side, at):
            return mine_ref[side, at].astype(f32) + got_ref[side, at].astype(f32)

        for i, ref in enumerate((own, for_x, for_y)):
            ref[...] = total(i, pl.ds(0, rows)).astype(ref.dtype)
        first[...] = total(3, pl.ds(0, half)).astype(bf16)
        second[...] = total(3, pl.ds(half, rows - half)).astype(bf16)

    out_shape = mine_shapes(rows, width)
    return pl.pallas_call(
        kernel,
        out_shape=out_shape,
        in_specs=[VMEM] * 2,
        out_specs=[VMEM] * 5,
        compiler_params=pltpu.CompilerParams(vmem_limit_bytes=room_for(*out_shape)),
        cost_estimate=NOTHING,
        name="taken_in",
    )(mine, received)


def sums_in_parts(where, arrays, products, memory_rows):
    order = z_places()
    slots = D // (8 * len(order))
    width = D * sum(arrays[right].shape[1] // D for _, right, _ in products if right is not None)
    width += sum(arrays[left].shape[0] for left, right, _ in products if right is None)
    given, memory = [], []
    for core in range(2):
        pick = selection(where, core, slots, order)
        columns = []
        for left, right, first in products:
            turned = times_transpose(pick, arrays[left]).astype(bf16)
            if right is not None:
                turned = matmul(turned[:, first:], arrays[right]).astype(bf16)
            columns.append(turned)
        given.append(jnp.concatenate(columns, axis=1).reshape(4, -1, width))
    if not memory_rows:
        return given
    key_grad, value_grad, key_weight, value_weight = arrays[-4:]
    grad = times_transpose(key_grad, key_weight) + times_transpose(value_grad, value_weight)
    whole = lax.dynamic_update_slice(
        jnp.zeros((8 * len(order) * memory_rows, D), bf16), grad.astype(bf16), (where[4], 0)
    ).reshape(8 * len(order), memory_rows, D)
    for core in range(2):
        c = jnp.bitwise_xor(where[2], core)
        devices = []
        for r in order:
            for side in range(4):
                y, x = jnp.bitwise_xor(where[1], side // 2), jnp.bitwise_xor(where[3], side % 2)
                devices.append(((jnp.bitwise_xor(where[0], r) * 2 + y) * 2 + c) * 2 + x)
        slabs = whole[jnp.stack(devices)].reshape(len(devices), 2, memory_rows // 2, D)
        memory.append(jnp.transpose(slabs, (1, 0, 2, 3)).reshape(-1, D))
    return given + memory


def sums_out(where, arrays, products, memory_rows=0):
    order = z_places()
    slots = D // (8 * len(order))
    if slots % 8:
        return sums_in_parts(where, arrays, products, memory_rows)
    n_in = len(arrays)
    depth = slots * len(order)
    blocks, column = [], 0
    for left, right, first in products:
        wide = arrays[left].shape[0] if right is None else arrays[right].shape[1]
        for at in range(0, wide, D):
            size = min(D, wide - at)
            blocks.append((left, right, first, at, size, column))
            column += size
    width = column
    window = arrays[-4].shape[0] if memory_rows else 8
    half = memory_rows // 2

    def kernel(at, *refs):
        ins, outs, block_ref, grad_ref = refs[:n_in], refs[n_in:-2], refs[-2], refs[-1]

        def places(core):
            c = jnp.bitwise_xor(at[2], core)
            for side in range(4):
                y, x = jnp.bitwise_xor(at[1], side // 2), jnp.bitwise_xor(at[3], side % 2)
                for i, r in enumerate(order):
                    yield side, i, ((jnp.bitwise_xor(at[0], r) * 2 + y) * 2 + c) * 2 + x

        if memory_rows:
            key_grad, value_grad, key_weight, value_weight = ins[-4:]
            grad_ref[...] = times_transpose(key_grad[...], key_weight[...]) + times_transpose(
                value_grad[...], value_weight[...]
            )
            for core in (1, 0):
                for side, i, device in places(core):
                    start = device * memory_rows - at[4]
                    inside = (start >= 0) & (start + memory_rows <= window)
                    start = pl.multiple_of(jnp.where(inside, start, 0), memory_rows)
                    slab = grad_ref[pl.ds(start, memory_rows), :]
                    slab = jnp.where(inside, slab, jnp.zeros_like(slab)).astype(bf16)
                    for n in range(2):
                        first = ((n * len(order) + i) * 4 + side) * half
                        outs[2 + core][first : first + half, :] = slab[n * half : (n + 1) * half]
        for n, (left, right, first, from_, size, to) in enumerate(blocks):
            if right is None:
                block = ins[left][...].astype(f32).T
            else:
                block = contract_rows(ins[left][first:, :], ins[right][:, from_ : from_ + size])
            slot = n % 2
            block_ref[slot, :, :, :size] = block.reshape(8 * len(order), slots, size)
            for core in (1, 0):
                for side, i, device in places(core):
                    slab = block_ref[slot, device, :, :size].astype(bf16)
                    outs[core][side, i * slots : (i + 1) * slots, to : to + size] = slab

    out_shape = [jax.ShapeDtypeStruct((4, depth, width), bf16)] * 2
    if memory_rows:
        out_shape += [jax.ShapeDtypeStruct((len(order) * 4 * memory_rows, D), bf16)] * 2
    return pl.pallas_call(
        kernel,
        out_shape=out_shape,
        in_specs=[SMEM] + [VMEM] * n_in,
        out_specs=[VMEM] * len(out_shape),
        scratch_shapes=[
            pltpu.VMEM((2, 8 * len(order), slots, D), f32),
            pltpu.VMEM((window, D), f32),
        ],
        compiler_params=pltpu.CompilerParams(
            vmem_limit_bytes=room_for(*out_shape) + 2 * D * D * 4 + window * D * 4 + 3 * 2**20
        ),
        cost_estimate=NOTHING,
        name="sums_out",
    )(where, *arrays)


def hidden_sums_out(where, activated, grad):
    hidden = activated.shape[1]
    order = z_places()
    span = hidden // len(order)
    slots, fold = span // 8, hidden // D
    part = slots // fold
    if span % 128 or part % 8:
        given = []
        for core in range(2):
            pick = selection(where, core, slots, order)
            turned = times_transpose(pick, activated).astype(bf16)
            rows = matmul(turned, grad).astype(bf16).reshape(4, len(order), fold, part, D)
            given.append(jnp.transpose(rows, (0, 1, 3, 2, 4)).reshape(4, -1, hidden))
        return given

    def kernel(at, act_ref, grad_ref, mine, other, block_ref):
        for i, r in enumerate(order):
            first = pl.multiple_of(jnp.bitwise_xor(at[0], r) * span, 128)
            block = contract_rows(act_ref[:, pl.ds(first, span)], grad_ref[...])
            block_ref[i % 2] = block.reshape(8, slots, D)
            for core, ref in ((1, other), (0, mine)):
                c = jnp.bitwise_xor(at[2], core)
                for side in range(4):
                    y, x = jnp.bitwise_xor(at[1], side // 2), jnp.bitwise_xor(at[3], side % 2)
                    slab = block_ref[i % 2, (y * 2 + c) * 2 + x].astype(bf16)
                    for j in range(fold):
                        ref[side, i * part : (i + 1) * part, j * D : (j + 1) * D] = slab[
                            j * part : (j + 1) * part
                        ]

    shape = jax.ShapeDtypeStruct((4, len(order) * part, hidden), bf16)
    return pl.pallas_call(
        kernel,
        out_shape=[shape, shape],
        in_specs=[SMEM] + [VMEM] * 2,
        out_specs=[VMEM] * 2,
        scratch_shapes=[pltpu.VMEM((2, 8, slots, D), f32)],
        compiler_params=pltpu.CompilerParams(
            vmem_limit_bytes=room_for(shape, shape) + 8 * 2**20
        ),
        cost_estimate=NOTHING,
        name="hidden_sums_out",
    )(where, activated, grad)


def hold(*values):
    return lax.optimization_barrier(values)


def z_first(shard):
    return swapped(shard[None], "z", lax.axis_size("z") // 2)


def z_rest(shard, received):
    by = lax.axis_size("z") // 2
    pieces, places = [shard[None], received], [0, by]
    while by > 1:
        by //= 2
        received = swapped(jnp.concatenate(pieces), "z", by)
        pieces, places = pieces + [received], places + [p ^ by for p in places]
    return pieces


def z_places():
    by, places = lax.axis_size("z") // 2, [0]
    while by:
        places = places + [p ^ by for p in places]
        by //= 2
    return places


def corners_in(over_x, over_y):
    half = over_x.shape[0] // 2
    return swapped(over_x[:half], "y"), swapped(over_y[half:], "x")


def corners_out(mine):
    return swapped(mine[3], "y"), swapped(mine[4], "x")


def sides_out(mine, corners, following=None):
    _, for_x, for_y = mine[:3]
    rows, width = for_x.shape
    half = rows // 2
    (over_y, y_first), (over_x, x_first) = corners
    more = [] if following is None else [following[3], following[4]]
    tail = half if more else 0

    def kernel(x_ref, y_ref, over_y_ref, over_x_ref, *refs):
        x_out, y_out = refs[-2:]
        came = over_y_ref[y_first : y_first + half].astype(f32)
        x_out[:half] = (x_ref[:half].astype(f32) + came).astype(bf16)
        x_out[half:rows] = x_ref[half:]
        came = over_x_ref[x_first : x_first + half].astype(f32)
        y_out[:half] = y_ref[:half]
        y_out[half:rows] = (y_ref[half:].astype(f32) + came).astype(bf16)
        if tail:
            y_out[rows:] = refs[0][...]
            x_out[rows:] = refs[1][...]

    shape = jax.ShapeDtypeStruct((rows + tail, width), bf16)
    x_out, y_out = pl.pallas_call(
        kernel,
        out_shape=[shape, shape],
        in_specs=[VMEM] * (4 + len(more)),
        out_specs=[VMEM] * 2,
        compiler_params=pltpu.CompilerParams(vmem_limit_bytes=room_for(shape, shape)),
        cost_estimate=NOTHING,
        name="sides_out",
    )(for_x, for_y, over_y, over_x, *more)
    return swapped(x_out, "x"), swapped(y_out, "y")


def apart(corners):
    return [(c, 0) for c in corners]


def halved(terms, parts, begin=0):
    rows, width = sum(parts), terms[0].shape[1]
    n_in = len(terms)

    def kernel(*refs):
        start, out = begin, 0
        for part in parts:
            half = part // 2
            for first, ref in ((start, refs[n_in]), (start + half, refs[n_in + 1])):
                total = sum(r[pl.ds(first, half), :].astype(f32) for r in refs[:n_in])
                ref[pl.ds(out, half), :] = total.astype(ref.dtype)
            start, out = start + part, out + half

    return pl.pallas_call(
        kernel,
        out_shape=[
            jax.ShapeDtypeStruct((rows // 2, width), f32),
            jax.ShapeDtypeStruct((rows // 2, width), bf16),
        ],
        in_specs=[VMEM] * n_in,
        out_specs=[VMEM] * 2,
        compiler_params=pltpu.CompilerParams(vmem_limit_bytes=room_for(terms[0])),
        cost_estimate=NOTHING,
        name="halved",
    )(*terms)


def halved_pair(first, second):
    rows, width = first[0].shape
    half = rows // 2
    counts = (len(first), len(second))

    def kernel(*refs):
        keep, give = refs[-2:]
        start = 0
        for n, count in enumerate(counts):
            terms = refs[start : start + count]
            start += count
            for at, ref in ((0, keep), (half, give)):
                total = sum(r[pl.ds(at, half), :].astype(f32) for r in terms)
                ref[pl.ds(n * half, half), :] = total.astype(ref.dtype)

    shapes = [jax.ShapeDtypeStruct((rows, width), kind) for kind in (f32, bf16)]
    return pl.pallas_call(
        kernel,
        out_shape=shapes,
        in_specs=[VMEM] * sum(counts),
        out_specs=[VMEM] * 2,
        compiler_params=pltpu.CompilerParams(vmem_limit_bytes=room_for(*shapes)),
        cost_estimate=NOTHING,
        name="halved_pair",
    )(*first, *second)


def z_most(terms, parts, begin=0, pair=None):
    by = 1
    keep, give = halved(terms, parts, begin) if pair is None else halved_pair(terms, pair)
    received, parts = swapped(give, "z", by), [p // 2 for p in parts]
    while 2 * by < lax.axis_size("z") // 2:
        by *= 2
        keep, give = halved([keep, received], parts)
        received, parts = swapped(give, "z", by), [p // 2 for p in parts]
    return keep, received


def z_last(keep, received, parts):
    by = lax.axis_size("z") // 2
    keep, give = halved([keep, received], [p // by for p in parts])
    return keep, swapped(give, "z", by)


def memory_taken(keep, received, rows):
    def kernel(keep_ref, got_ref, *outs):
        half = rows // 2
        for n in range(2):
            for z in range(2):
                for side in range(4):
                    here = pl.ds(((n * 2 + z) * 4 + side) * half, half)
                    total = keep_ref[here, :] + got_ref[here, :].astype(f32)
                    outs[side][pl.ds(z * rows + n * half, half), :] = total.astype(outs[side].dtype)

    out_shape = [like(2 * rows, D, f32)] + [like(2 * rows, D, bf16)] * 3
    return pl.pallas_call(
        kernel,
        out_shape=out_shape,
        in_specs=[VMEM] * 2,
        out_specs=[VMEM] * 4,
        compiler_params=pltpu.CompilerParams(vmem_limit_bytes=room_for(*out_shape, keep)),
        cost_estimate=NOTHING,
        name="memory_taken",
    )(keep, received)


def plus(keep, received):
    return keep + received.astype(f32)


def lane_halves(block):
    lanes = lax.broadcasted_iota(jnp.int32, block.shape, 1)
    zero = jnp.zeros_like(block)
    return jnp.where(lanes < HEAD, block, zero), jnp.where(lanes < HEAD, zero, block)


def fill_bias(bias_ref, first, bounds, causal):
    shape = bias_ref.shape
    rows = shape[1] // 2
    keys = first + lax.broadcasted_iota(jnp.int32, shape, 0)
    allowed = (keys >= bounds[0]) & (keys < bounds[1])
    if causal:
        queries = lax.broadcasted_iota(jnp.int32, shape, 1)
        queries = jnp.where(queries < rows, queries, queries - rows)
        allowed = allowed & (keys - rows <= queries)
    bias_ref[...] = jnp.where(allowed, 0.0, big_negative)


def both_halves(block):
    return jnp.concatenate(lane_halves(block), axis=0)


def key_block(width):
    return next(width // n for n in range(1, width) if width % (16 * n) == 0 and width // n <= 1536)


def attend_kernel(causal, block, bounds, q_ref, k_ref, v_ref, out_ref, low_ref, lse_ref, bias_ref):
    rows, width = q_ref.shape[0], k_ref.shape[0]
    if width == block:
        fill_bias(bias_ref, 0, bounds, causal)

    def pair(h, carried):
        lanes = pl.ds(pl.multiple_of(h * PAIR, PAIR), PAIR)
        both = both_halves(q_ref[:, lanes] * SCALE)

        def step(i, state):
            first = pl.multiple_of(i * block, block)
            if width > block:
                fill_bias(bias_ref, first, bounds, causal)
            keys, values = k_ref[pl.ds(first, block), lanes], v_ref[pl.ds(first, block), lanes]
            scores = times_transpose(keys, both) + bias_ref[...]
            top = jnp.max(scores, axis=0, keepdims=True)
            if state is not None:
                top = jnp.maximum(state[0], top)
            weights = jnp.exp(scores - top)
            total = jnp.sum(weights, axis=0, keepdims=True)
            summed = contract_rows(values, weights.astype(bf16))
            if state is not None:
                factor = jnp.exp(state[0] - top)
                total, summed = total + state[1] * factor, summed + state[2] * factor
            return top, total, summed

        state = step(0, None)
        if width > block:
            state = lax.fori_loop(1, width // block, step, state)
        top, total, summed = state
        out = summed / total
        out = jnp.concatenate([out[:HEAD, :rows], out[HEAD:, rows:]], axis=0).T
        out_ref[:, lanes] = out
        low_ref[:, lanes] = out.astype(bf16)
        lse_ref[h] = top + jnp.log(total)
        return carried

    lax.fori_loop(0, PAIRS, pair, 0, unroll=2)


def attend(queries, keys, values, bounds, causal):
    rows, width = queries.shape[0], keys.shape[0]
    block = key_block(width)
    out_shape = [
        jax.ShapeDtypeStruct((rows, D), f32),
        jax.ShapeDtypeStruct((rows, D), bf16),
        jax.ShapeDtypeStruct((PAIRS, 1, 2 * rows), f32),
    ]
    return pl.pallas_call(
        lambda *refs: attend_kernel(causal, block, *refs),
        scratch_shapes=[pltpu.VMEM((block, 2 * rows), f32)],
        in_specs=[SMEM] + [VMEM] * 3,
        out_specs=[VMEM] * 3,
        out_shape=out_shape,
        compiler_params=pltpu.CompilerParams(
            vmem_limit_bytes=16 * 2**20 if width <= 2048 else 48 * 2**20
        ),
        cost_estimate=NOTHING,
        name="attend_self" if causal else "attend_cross",
    )(bounds, queries, keys, values)


def attend_back_kernel(
    causal,
    block,
    bounds,
    q_ref,
    k_ref,
    v_ref,
    o_ref,
    g_ref,
    lse_ref,
    dq_ref,
    dk_ref,
    dv_ref,
    bias_ref,
):
    rows, width = q_ref.shape[0], k_ref.shape[0]
    if width == block:
        fill_bias(bias_ref, 0, bounds, causal)

    def pair(h, carried):
        lanes = pl.ds(pl.multiple_of(h * PAIR, PAIR), PAIR)
        queries = both_halves(q_ref[:, lanes] * SCALE)
        grads = both_halves(g_ref[:, lanes])
        products = (g_ref[:, lanes].astype(f32) * o_ref[:, lanes]).T
        delta = jnp.concatenate(
            [
                jnp.sum(products[:HEAD], axis=0, keepdims=True),
                jnp.sum(products[HEAD:], axis=0, keepdims=True),
            ],
            axis=1,
        )

        def step(i, query_grad):
            first = pl.multiple_of(i * block, block)
            if width > block:
                fill_bias(bias_ref, first, bounds, causal)
            here = pl.ds(first, block)
            keys, values = k_ref[here, lanes], v_ref[here, lanes]
            scores = times_transpose(keys, queries) + bias_ref[...]
            probs = jnp.exp(scores - lse_ref[h])
            dv_ref[here, lanes] = matmul(probs.astype(bf16), grads).astype(bf16)
            slopes = times_transpose(values, grads)
            score_grad = (probs * (slopes - delta)).astype(bf16)
            dk_ref[here, lanes] = matmul(score_grad, queries).astype(bf16)
            part = contract_rows(keys, score_grad)
            return part if query_grad is None else query_grad + part

        grad = step(0, None)
        if width > block:
            grad = lax.fori_loop(1, width // block, step, grad)
        grad = jnp.concatenate([grad[:HEAD, :rows], grad[HEAD:, rows:]], axis=0)
        dq_ref[:, lanes] = (grad * SCALE).T.astype(bf16)
        return carried

    lax.fori_loop(0, PAIRS, pair, 0, unroll=2)


def attend_back(queries, keys, values, out, grad, lse, bounds, causal):
    rows, width = queries.shape[0], keys.shape[0]
    block = key_block(width)
    out_shape = [
        jax.ShapeDtypeStruct((rows, D), bf16),
        jax.ShapeDtypeStruct((width, D), bf16),
        jax.ShapeDtypeStruct((width, D), bf16),
    ]
    return pl.pallas_call(
        lambda *refs: attend_back_kernel(causal, block, *refs),
        scratch_shapes=[pltpu.VMEM((block, 2 * rows), f32)],
        in_specs=[SMEM] + [VMEM] * 6,
        out_specs=[VMEM] * 3,
        out_shape=out_shape,
        compiler_params=pltpu.CompilerParams(
            vmem_limit_bytes=26 * 2**20 if width <= 2048 else 62 * 2**20
        ),
        cost_estimate=NOTHING,
        name="attend_back_self" if causal else "attend_back_cross",
    )(bounds, queries, keys, values, out, grad, lse)


def activate(values, weight):
    rows, hidden = values.shape[0], weight.shape[1]
    step = min(hidden, D)

    def kernel(values_ref, weight_ref, out_ref, slope_ref):
        for at in range(0, hidden, step):
            inner = matmul(values_ref[...], weight_ref[:, at : at + step])
            below = 0.5 * (1.0 + lax.erf(inner * (0.5**0.5)))
            out_ref[:, at : at + step] = (inner * below).astype(bf16)
            bell = jnp.exp(-0.5 * inner * inner) * (1.0 / math.sqrt(2.0 * math.pi))
            slope_ref[:, at : at + step] = below + inner * bell

    return pl.pallas_call(
        kernel,
        out_shape=[
            jax.ShapeDtypeStruct((rows, hidden), bf16),
            jax.ShapeDtypeStruct((rows, hidden), f32),
        ],
        in_specs=[VMEM] * 2,
        out_specs=[VMEM] * 2,
        compiler_params=pltpu.CompilerParams(vmem_limit_bytes=8 * 2**20),
        cost_estimate=NOTHING,
        name="activate",
    )(values, weight)


def whole_kernel(kernel, name, out_shape, *arrays, spare=2):
    return pl.pallas_call(
        kernel,
        out_shape=out_shape,
        in_specs=[VMEM] * len(arrays),
        out_specs=[VMEM] * len(out_shape),
        compiler_params=pltpu.CompilerParams(
            vmem_limit_bytes=min(room_for(*out_shape) + spare * 2**20, 62 * 2**20)
        ),
        cost_estimate=NOTHING,
        name=name,
    )(*arrays)


def like(rows, columns, dtype):
    return jax.ShapeDtypeStruct((rows, columns), dtype)


def row_mean(values):
    return jnp.sum(values, axis=-1, keepdims=True) * (1.0 / values.shape[-1])


def normed(values):
    centered = values - row_mean(values)
    inverse = lax.rsqrt(row_mean(centered * centered) + epsilon)
    return centered * inverse, inverse


def norm_back(grad, unit, inverse, gain):
    scaled = grad * gain
    inner = scaled - row_mean(scaled) - unit * row_mean(scaled * unit)
    return inner * inverse, jnp.sum(grad * unit, axis=0, keepdims=True)


def add_and_norm(base, out, weight, gain):
    rows = base.shape[0]

    def kernel(b_ref, o_ref, w_ref, g_ref, hidden_ref, low_ref, unit_ref, inverse_ref):
        mid = b_ref[...].astype(f32) + matmul(o_ref[...], w_ref[...])
        unit, inverse = normed(mid)
        hidden = unit * g_ref[...]
        hidden_ref[...], low_ref[...] = hidden, hidden.astype(bf16)
        unit_ref[...], inverse_ref[...] = unit, inverse

    out_shape = [like(rows, D, f32), like(rows, D, bf16), like(rows, D, f32), like(rows, 1, f32)]
    return whole_kernel(kernel, "add_and_norm", out_shape, base, out, weight, gain)


def feed_turn(activated, weight, hidden, gain, cotangent):
    rows = hidden.shape[0]

    def kernel(a_ref, w_ref, h_ref, g_ref, c_ref, out_ref, grad_ref, low_ref, gain_ref):
        unit, inverse = normed(h_ref[...] + matmul(a_ref[...], w_ref[...]))
        gain = g_ref[...]
        out_ref[...] = (unit * gain).astype(bf16)
        grad, gain_grad = norm_back(c_ref[...].astype(f32), unit, inverse, gain)
        grad_ref[...], low_ref[...], gain_ref[...] = grad, grad.astype(bf16), gain_grad

    out_shape = [like(rows, D, bf16), like(rows, D, f32), like(rows, D, bf16), like(1, D, f32)]
    return whole_kernel(
        kernel, "feed_turn", out_shape, activated, weight, hidden, gain, cotangent
    )


def self_turn(above, grad, weight, unit, inverse, gain, out_weight, gain_cross, gain_feed):
    rows = above.shape[0]

    def kernel(a_ref, d_ref, w_ref, u_ref, i_ref, g_ref, o_ref, c_ref, f_ref, *outs):
        grad_ref, low_ref, gains_ref, out_ref = outs
        total = a_ref[...] + times_transpose(d_ref[...], w_ref[...])
        grad, gain_grad = norm_back(total, u_ref[...], i_ref[...], g_ref[...])
        low = grad.astype(bf16)
        grad_ref[...], low_ref[...] = grad, low
        rest = jnp.zeros((125, D), f32)
        gains = jnp.concatenate([gain_grad, c_ref[...], f_ref[...], rest], axis=0)
        gains_ref[...] = gains.astype(bf16)
        out_ref[...] = times_transpose(low, o_ref[...]).astype(bf16)

    out_shape = [like(rows, D, f32), like(rows, D, bf16), like(128, D, bf16), like(rows, D, bf16)]
    return whole_kernel(
        kernel,
        "self_turn",
        out_shape,
        above,
        grad,
        weight,
        unit,
        inverse,
        gain,
        out_weight,
        gain_cross,
        gain_feed,
    )


def padded(shard, rows):
    return jnp.pad(shard, ((0, rows - shard.shape[0]), (0, 0)))


def grouped(shard, group):
    return shard.reshape(shard.shape[0] // group, group, shard.shape[1])


def per_device(
    tokens,
    memory,
    self_query,
    self_key,
    self_value,
    self_output,
    cross_query,
    cross_key,
    cross_value,
    cross_output,
    feed_in,
    feed_out,
    gain_self,
    gain_cross,
    gain_feed,
    doc_lengths,
    seg_doc,
    cotangent,
):
    where = position()
    token_rows = tokens.shape[0]
    count = lax.axis_size("z") * 8
    slots = self_query.shape[0]
    memory_rows = memory.shape[0]
    group = math.gcd(8, slots) if slots % 4 == 0 else slots
    memory_groups = pl.cdiv(memory_rows, group)
    gain_groups = pl.cdiv(3, group)
    gain_rows = gain_groups * group
    slot_groups = slots // group

    gains = jnp.pad(jnp.stack([gain_self, gain_cross, gain_feed]), ((0, gain_rows - 3), (0, D - slots)))
    hidden = feed_in.shape[1]
    places = z_places()
    cuts1 = [(i * slot_groups, slot_groups, 1) for i in range(4)]
    cuts1.append((4 * slot_groups, gain_groups, 1))
    cuts2 = [(i * slot_groups, slot_groups, 1) for i in range(3)]
    cuts3 = [(0, slot_groups, 1), (slot_groups, slot_groups, hidden // D)]
    cuts4 = [(0, feed_out.shape[0] // group, 1)]
    s1 = packed([self_query, self_key, self_value, self_output, gains], group)
    s2 = packed(
        [cross_query, cross_key, cross_value, padded(memory, memory_groups * group)], group
    )
    s3 = packed([cross_output, feed_in], group)
    s4 = grouped(feed_out, group)

    window = count * memory_rows // 2 + memory_rows
    where_window, cross_bounds, self_bounds = bounds_of(
        doc_lengths, seg_doc, where, memory_rows, count * memory_rows, window, token_rows
    )
    a1 = z_first(s1)
    earlier = lax.ppermute(tokens, "x", [(0, 1)])
    a1, s2, s3, s4 = hold(a1, s2, s3, s4)
    near = jnp.concatenate([s1[None], a1])
    early = near.shape[0] == lax.axis_size("z") // 2
    b1 = z_rest(s1, a1)
    a2 = z_first(s2)
    if early:
        x1, y1 = [swapped(near, "x")], [swapped(near, "y")]
        own1, far = [near], b1[2]
        far, a2, earlier, s3, s4, x1, y1 = hold(far, a2, earlier, s3, s4, x1, y1)
        own1.append(far)
        x1.append(swapped(far, "x"))
        y1.append(swapped(far, "y"))
    else:
        own1 = in_order(b1, places, where)
        own1, a2, earlier, s3, s4 = hold(own1, a2, earlier, s3, s4)
        x1, y1 = swapped(own1, "x"), swapped(own1, "y")
    b2 = z_rest(s2, a2)
    a3 = z_first(s3)
    both_tokens = jnp.concatenate([earlier, tokens], axis=0)
    own2 = in_order(b2, places, where)
    own2, x1, y1, own1, both_tokens, s4 = hold(own2, x1, y1, own1, both_tokens, s4)

    if early:
        d1 = swapped(x1[0], "y"), swapped(y1[1], "x")
    else:
        d1 = corners_in(x1, y1)
    x2, y2 = swapped(own2, "x"), swapped(own2, "y")
    b3 = z_rest(s3, a3)
    own3 = in_order(b3, places, where)
    a4 = z_first(s4)
    d1, x2, y2, own2, own3, a4, where_window, cross_bounds, self_bounds = hold(
        d1, x2, y2, own2, own3, a4, where_window, cross_bounds, self_bounds
    )

    d2 = corners_in(x2, y2)
    x3, y3 = swapped(own3, "x"), swapped(own3, "y")
    if early:
        half1 = half_by_steps(own1, x1, y1, d1, places, where)
    else:
        half1 = half_of(own1, x1, y1, d1, where)
    c1 = swapped(half1, "c")
    wholes = assembled(half1, c1, cuts1, where)
    self_query, self_key, self_value, self_output = (w.reshape(D, D) for w in wholes[:4])
    b4 = z_rest(s4, a4)
    gains = wholes[4].reshape(count, gain_rows, D)[:, :3, :slots]
    gain_self, gain_cross, gain_feed = (
        gains[:, i].reshape(D).astype(f32) for i in range(3)
    )
    queries = matmul(tokens, self_query).astype(bf16)
    keys = matmul(both_tokens, self_key).astype(bf16)
    values = matmul(both_tokens, self_value).astype(bf16)
    self_full, self_out, self_lse = attend(queries, keys, values, self_bounds, True)
    b4, self_out = hold(b4, self_out)
    own4 = in_order(b4, places, where)
    hidden_self, hidden_self_low, unit_self, inverse_self = add_and_norm(
        tokens, self_out, self_output, gain_self.reshape(1, D)
    )
    d2, x3, y3, own3, own4, hidden_self, hidden_self_low = hold(
        d2, x3, y3, own3, own4, hidden_self, hidden_self_low
    )

    d3 = corners_in(x3, y3)
    x4, y4 = swapped(own4, "x"), swapped(own4, "y")
    half2 = half_of(own2, x2, y2, d2, where)
    c2 = swapped(half2, "c")
    wholes = assembled(half2, c2, cuts2, where)
    cross_query, cross_key, cross_value = (w.reshape(D, D) for w in wholes)
    memory_here = window_of(half2, c2, 3 * slot_groups, memory_rows, window, where_window)
    cross_queries = matmul(hidden_self_low, cross_query).astype(bf16)
    memory_keys = matmul(memory_here, cross_key).astype(bf16)
    memory_values = matmul(memory_here, cross_value).astype(bf16)
    cross_full, cross_out, cross_lse = attend(
        cross_queries, memory_keys, memory_values, cross_bounds, False
    )
    d3, x4, y4, own4, cross_out = hold(d3, x4, y4, own4, cross_out)

    d4 = corners_in(x4, y4)
    half3 = half_of(own3, x3, y3, d3, where)
    c3 = swapped(half3, "c")
    wholes = assembled(half3, c3, cuts3, where)
    cross_output, feed_in = (w.reshape(D, w.shape[-1]) for w in wholes)
    mid_cross = hidden_self + matmul(cross_out, cross_output)
    hidden_cross, back_cross = jax.vjp(layer_norm, mid_cross, gain_cross)
    hidden_cross_low = hidden_cross.astype(bf16)
    activated, slope = activate(hidden_cross_low, feed_in)
    d4, activated, own4 = hold(d4, activated, own4)
    half4 = half_of(own4, x4, y4, d4, where)
    c4 = swapped(half4, "c")
    wholes = assembled(half4, c4, cuts4, where)
    feed_out = wholes[0].reshape(hidden, D)
    layer_out, gradient_feed_mid, feed_rounded, gain_feed_sum = feed_turn(
        activated, feed_out, hidden_cross, gain_feed.reshape(1, D), cotangent
    )
    m4, o4 = hidden_sums_out(where, activated, feed_rounded)
    m4, o4, feed_rounded = hold(m4, o4, feed_rounded)
    r4 = swapped(o4, "c")
    gradient_inner = (times_transpose(feed_rounded, feed_out) * slope).astype(bf16)
    m3, o3 = sums_out(where, [hidden_cross_low, gradient_inner], [(0, 1, 0)])
    r4, m3, o3, gradient_inner = hold(r4, m3, o3, gradient_inner)
    m4 = taken_in(m4, r4)
    d4 = corners_out(m4)
    r3 = swapped(o3, "c")
    gradient_hidden_cross = gradient_feed_mid + times_transpose(gradient_inner, feed_in)
    gradient_cross_mid, gain_cross_sum = back_cross(gradient_hidden_cross)
    cross_rounded = gradient_cross_mid.astype(bf16)

    outgoing = times_transpose(cross_rounded, cross_output).astype(bf16)
    r3, d4, outgoing, cross_rounded = hold(r3, d4, outgoing, cross_rounded)
    m3 = taken_in(m3, r3)
    x4, y4 = sides_out(m4, apart(d4), m3)
    cross_query_grad, memory_key_grad, memory_value_grad = attend_back(
        cross_queries,
        memory_keys,
        memory_values,
        cross_full,
        outgoing,
        cross_lse,
        cross_bounds,
        False,
    )
    gradient_self_mid, self_rounded, gain_sums, self_outgoing = self_turn(
        gradient_cross_mid,
        cross_query_grad,
        cross_query,
        unit_self,
        inverse_self,
        gain_self.reshape(1, D),
        self_output,
        gain_cross_sum.reshape(1, D),
        gain_feed_sum,
    )

    query_grad, key_grad, value_grad = attend_back(
        queries, keys, values, self_full, self_outgoing, self_lse, self_bounds, True
    )
    m1, o1 = sums_out(
        where,
        [
            both_tokens,
            query_grad,
            key_grad,
            value_grad,
            self_out,
            self_rounded,
            gain_sums,
        ],
        [(0, 1, token_rows), (0, 2, 0), (0, 3, 0), (4, 5, 0), (6, None, 0)],
    )
    x4, y4, m1, o1, cross_query_grad, query_grad, key_grad, value_grad = hold(
        x4, y4, m1, o1, cross_query_grad, query_grad, key_grad, value_grad
    )
    x3, y3 = sides_out(m3, [(y4, D // 8), (x4, D // 8)])
    parts1, parts5 = [D // 8], [count * memory_rows // 4] * 2
    k4 = z_most([m4[0], x4, y4], parts1)
    r1 = swapped(o1, "c")
    m2, o2, m5, o5 = sums_out(
        where_window,
        [
            hidden_self_low,
            cross_query_grad,
            memory_here,
            cross_out,
            cross_rounded,
            gain_sums,
            memory_key_grad,
            memory_value_grad,
            cross_key,
            cross_value,
        ],
        [(0, 1, 0), (2, 6, 0), (2, 7, 0), (3, 4, 0), (5, None, 0)],
        memory_rows,
    )
    x3, y3, k4, m1, r1, m2, o2, m5, o5, query_grad, key_grad, value_grad = hold(
        x3, y3, k4, m1, r1, m2, o2, m5, o5, query_grad, key_grad, value_grad
    )
    m1 = taken_in(m1, r1)
    d1 = corners_out(m1)
    r2, r5 = swapped(o2, "c"), swapped(o5, "c")
    m1, x3, y3 = hold(m1, x3, y3)
    k3 = z_most([m3[0], x3, y3], parts1)
    both_grad = times_transpose(key_grad, self_key) + times_transpose(value_grad, self_value)
    to_earlier = both_grad[:token_rows].astype(bf16)
    partial_tokens = (
        gradient_self_mid + times_transpose(query_grad, self_query) + both_grad[token_rows:]
    )
    d1, m1, r2, r5, k3, k4, m2, m5, partial_tokens, to_earlier = hold(
        d1, m1, r2, r5, k3, k4, m2, m5, partial_tokens, to_earlier
    )
    m2 = taken_in(m2, r2)
    x1, y1 = sides_out(m1, apart(d1), m2)
    k5 = z_most([m5, r5], parts5)
    x1, y1, k3, k4, k5 = hold(x1, y1, k3, k4, k5)
    x2, y2 = sides_out(m2, [(y1, D // 8), (x1, D // 8)])
    k1 = z_most([m1[0], x1, y1], parts1)
    keep, give = halved_pair(list(k4), list(k3))
    k3 = keep, swapped(give, "z", lax.axis_size("z") // 2)
    x2, y2, k1, k3, k5, to_earlier = hold(x2, y2, k1, k3, k5, to_earlier)
    total_feed = plus(*k3)
    k2 = z_most([m2[0], x2, y2], parts1)
    k1 = z_last(*k1, parts1)
    m5 = memory_taken(*k5, memory_rows)
    x5, y5 = swapped(m5[1], "x"), swapped(m5[2], "y")
    d5 = lax.ppermute(m5[3], ("y", "x"), [(i, 3 - i) for i in range(4)])
    k2, x5, y5, d5, k1, to_earlier = hold(k2, x5, y5, d5, k1, to_earlier)
    sent_back = lax.ppermute(to_earlier, "x", [(1, 0)])
    k2 = z_last(*k2, parts1)
    keep, give = halved([m5[0], x5, y5, d5], [2 * memory_rows])
    k5 = keep, swapped(give, "z", lax.axis_size("z") // 2)
    total_self = plus(*k1)
    gradient_memory = plus(*k5)
    gradient_tokens = plus(partial_tokens, sent_back)
    total_cross = plus(*k2)

    self_parts = [total_self[:, i * D : (i + 1) * D] for i in range(4)]
    cross_parts = [total_cross[:, i * D : (i + 1) * D] for i in range(4)]
    return (
        layer_out,
        gradient_tokens,
        gradient_memory,
        *self_parts,
        *cross_parts,
        total_feed[slots:],
        jnp.concatenate([total_feed[:slots, i * D : (i + 1) * D] for i in range(hidden // D)]),
        total_self[:, 4 * D],
        total_self[:, 4 * D + 1],
        total_self[:, 4 * D + 2],
    )


def solution(mesh):
    fine = Mesh(mesh.devices.reshape(-1, 2, 2, 2), ALL)
    rows = P(ALL, None)
    return jax.shard_map(
        per_device,
        mesh=fine,
        in_specs=(rows,) * 12 + (P(ALL),) * 3 + (P(), P(), rows),
        out_specs=(rows,) * 13 + (P(ALL),) * 3,
        check_vma=False,
    )
```
